512 devices in a mesh: tm: 8 (over z), rows: 64 (over y, x, core).
Axes of the slice: x: 4, y: 8, z: 8, core: 2. Of those that a mesh axis runs over, the one named last changes fastest.
Arguments:
- w_inv: bfloat16 [8, 1536, 1536], P('tm', 'rows'), may hold values from -1 to 1, as said below
- lower_block: bfloat16 [8, 1536, 1536], P('tm', 'rows'), may hold values from -0.15625 to 0.15625
- sigma_end: float32 [1536, 1536], P('rows'), may hold values from -3 to 3, as said below
- chain_break: int32 [8], replicated, may hold values 0 or 1
Outputs:
- sigma_diag: float32 [8, 1536, 1536], P('tm', 'rows')
- sigma_cross: float32 [8, 1536, 1536], P('tm', 'rows')
The draws below stay inside these ranges and needn't reach their ends.
Inputs may be any that keep to these rules, and one draw needn't show every extreme that they name: w_inv is lower triangular with a positive diagonal. sigma_end is symmetric with a positive diagonal.
All inputs are finite; a program needn't handle non-finite values.
Results may differ from the reference program's by a relative error of at most 0.0045.
Values may be sent and summed in bfloat16 or wider, within the bound.
A program may use at most 64 MiB of HBM per device.

```python
import math
import jax
import jax.numpy as jnp

B = 1536
N_TM = 8


def draw_w_inv(key, part):
    key_off, key_diag = jax.random.split(key)
    row_ids = jnp.arange(B)[:, None]
    col_ids = jnp.arange(B)[None, :]
    off = jnp.clip(0.4 * jax.random.normal(key_off, (N_TM, B, B), jnp.float32), -0.7, 0.7)
    diag = jnp.exp(jax.random.uniform(key_diag, (N_TM, B, 1), jnp.float32, math.log(0.25), math.log(0.95)))
    off = off / math.sqrt(B)
    lower = jnp.where(col_ids < row_ids, off, 0.0)
    return (lower + jnp.where(col_ids == row_ids, diag, 0.0)).astype(jnp.bfloat16)


def draw_sigma_end(key, part):
    key_off, key_diag = jax.random.split(key)
    row_ids = jnp.arange(B)[:, None]
    col_ids = jnp.arange(B)[None, :]
    noise = jnp.clip(jax.random.normal(key_off, (B, B), jnp.float32), -3.0, 3.0)
    diag = jnp.exp(jax.random.uniform(key_diag, (B, 1), jnp.float32, math.log(0.5), math.log(2.0)))
    sym = 0.5 * (noise + noise.T) / math.sqrt(B)
    return jnp.where(col_ids == row_ids, diag, sym)


def place_ends(values, rng, smallest, largest):
    extent = values.shape
    index_at = [jax.random.randint(jax.random.fold_in(rng, axis), (), 0, extent[axis]) for axis in range(len(extent))]
    values = values.at[tuple(index_at)].set(smallest)
    longest = extent.index(max(extent))
    index_at[longest] = (index_at[longest] + 1) % extent[longest]
    return values.at[tuple(index_at)].set(largest)


def level_of(stream_key, dims, pieces, least, high):
    gain = 1.0
    for position, blocks in pieces:
        heights = jax.random.uniform(jax.random.fold_in(jax.random.fold_in(stream_key, 6), position), (blocks,), jnp.float32, least / len(pieces), high / len(pieces))
        gain = gain * jnp.repeat(jnp.exp(heights), dims[position] // blocks).reshape((-1,) + (1,) * (len(dims) - 1 - position))
    return gain


def gaussian(rng, shape, scale, reach, pieces=(), held_as=jnp.bfloat16):
    entries = jax.random.normal(rng, shape, jnp.float32) * scale
    if len(pieces) > 0:
        entries = level_of(rng, shape, pieces, -0.22, 0.18) * entries
    return jnp.clip(entries, min=-reach, max=reach).astype(held_as)


def setup_inputs(seed: int = 0) -> dict:
    keys = jax.random.split(jax.random.key(seed), 5)
    return {
        "w_inv": draw_w_inv(jax.random.fold_in(keys[4], 71), 0),
        "lower_block": gaussian(keys[1], (N_TM, B, B), B ** -0.5, 0.15625, ((0, 8), (1, 64))),
        "sigma_end": draw_sigma_end(jax.random.fold_in(keys[4], 71), 0),
        "chain_break": place_ends((jax.random.randint(keys[3], (N_TM,), 0, 4) < 1).astype(jnp.int32), jax.random.fold_in(keys[3], 1), 0, 1),
    }


def reference(w_inv, lower_block, sigma_end, chain_break):
    end_b = sigma_end.astype(jnp.bfloat16)
    carried = end_b
    diag_list = []
    cross_list = []
    for part in range(N_TM - 1, -1, -1):
        weight = w_inv[part]
        coupled = jnp.dot(lower_block[part], weight, preferred_element_type=jnp.float32).astype(jnp.bfloat16)
        gram = jnp.dot(weight.T, weight, preferred_element_type=jnp.float32)
        use_end = jnp.logical_or(chain_break[part] == 1, part == N_TM - 1)
        source = jnp.where(use_end, end_b, carried)
        product = jnp.dot(source, coupled, preferred_element_type=jnp.float32)
        product_b = product.astype(jnp.bfloat16)
        sigma = gram + jnp.dot(product_b.T, coupled, preferred_element_type=jnp.float32)
        carried = sigma.astype(jnp.bfloat16)
        diag_list.insert(0, sigma)
        cross_list.insert(0, -product)
    return jnp.stack(diag_list), jnp.stack(cross_list)
```

```python
import jax
import jax.numpy as jnp
from jax import lax
from jax.experimental import pallas as pl
from jax.experimental.pallas import tpu as pltpu
from jax.sharding import PartitionSpec as P

MESH = pl.DeviceIdType.MESH
BF16 = jnp.bfloat16
F32 = jnp.float32
B = 1536
CHIPS = 32
HALF_CHIPS = 16
PANEL = 48
OWN = 24
HALF = 768


def dot(a, b):
    return jnp.dot(a, b, preferred_element_type=F32)


def message(product, j):
    start = PANEL * j
    tile, off = start // 128, start % 128
    lanes = lax.broadcasted_iota(jnp.int32, (PANEL, 128), 1)
    block = product[:, tile * 128:(tile + 1) * 128]
    if off:
        block = pltpu.roll(block, 128 - off, 1)
        if off + PANEL > 128:
            after = pltpu.roll(product[:, (tile + 1) * 128:(tile + 2) * 128], 128 - off, 1)
            block = jnp.where(lanes < 128 - off, block, after)
    top = jnp.where(lanes[:16] < 64, block[:16], pltpu.roll(block[16:32], 64, 1))
    return jnp.concatenate([top, block[32:48]], axis=0).astype(BF16)


def chain(
    flag_ref, coupled_ref, gram_ref, end_ref, sigma_ref, cross_ref,
    end_buf, next_buf, next_out, part_out, part_in, part2_out, part2_in, pack, recv, rows_out,
    end_sem, next_sem, part_sem, part2_sem, rows_sem, pack_send, pack_recv,
):
    parts = 8
    p = lax.axis_index("tm")
    r = lax.axis_index("rows")
    chip, core = r // 2, r % 2
    half = chip // HALF_CHIPS
    place = chip % HALF_CHIPS
    sibling = (p, chip * 2 + 1 - core)

    def peer(j):
        return (p, (core * HALF_CHIPS + j) * 2 + half)

    barrier = pltpu.get_barrier_semaphore()
    pl.semaphore_signal(barrier, 1, device_id=sibling, device_id_type=MESH)

    @pl.when(p > 0)
    def _():
        pl.semaphore_signal(barrier, 1, device_id=(p - 1, r), device_id_type=MESH)

    @pl.when(p < parts - 1)
    def _():
        pl.semaphore_signal(barrier, 1, device_id=(p + 1, r), device_id_type=MESH)

    def is_self(j):
        return jnp.logical_and(core == half, place == j)

    for j in range(HALF_CHIPS):
        @pl.when(jnp.logical_not(is_self(j)))
        def _():
            pl.semaphore_signal(barrier, 1, device_id=peer(j), device_id_type=MESH)

    expected = (
        1 + jnp.where(p > 0, 1, 0) + jnp.where(p < parts - 1, 1, 0)
        + HALF_CHIPS - jnp.where(core == half, 1, 0)
    )
    pl.semaphore_wait(barrier, expected)

    mine = pl.ds(pl.multiple_of(core * HALF, 128), HALF)
    theirs = pl.ds(pl.multiple_of((1 - core) * HALF, 128), HALF)
    my_rows = pl.ds(pl.multiple_of(core * OWN, 8), OWN)
    their_rows = pl.ds(pl.multiple_of((1 - core) * OWN, 8), OWN)

    def to_sibling(src, dst, sems):
        return pltpu.make_async_remote_copy(
            src_ref=src, dst_ref=dst, send_sem=sems.at[0], recv_sem=sems.at[1],
            device_id=sibling, device_id_type=MESH)

    end_copy = to_sibling(end_ref.at[:, theirs], end_buf.at[my_rows], end_sem)
    end_copy.start()
    end_buf[my_rows] = end_ref[:, mine]
    end_copy.wait()

    next_copy = pltpu.make_async_remote_copy(
        src_ref=next_out, dst_ref=next_buf, send_sem=next_sem.at[0], recv_sem=next_sem.at[1],
        device_id=(jnp.maximum(p - 1, 0), r), device_id_type=MESH)

    @pl.when(p < parts - 1)
    def _():
        next_copy.wait_recv()

    @pl.when(p == parts - 1)
    def _():
        next_buf[...] = jnp.zeros_like(next_buf)

    use_end = jnp.logical_or(flag_ref[0] == 1, p == parts - 1)
    source = jnp.where(use_end, end_buf[...].astype(BF16), next_buf[...])

    part_copy = to_sibling(part_out, part_in, part_sem)
    part_out[...] = dot(source, coupled_ref[:, :, theirs].reshape(HALF, HALF))
    part_copy.start()
    product = dot(source, coupled_ref[:, :, mine].reshape(HALF, HALF))
    part_copy.wait_recv()
    product = product + part_in[...]

    def pack_copy(j):
        return pltpu.make_async_remote_copy(
            src_ref=pack.at[j], dst_ref=recv.at[place], send_sem=pack_send.at[j],
            recv_sem=pack_recv.at[place], device_id=peer(j), device_id_type=MESH)

    def arrival(j):
        return pltpu.make_async_remote_copy(
            src_ref=pack.at[j], dst_ref=recv.at[j], send_sem=pack_send.at[j],
            recv_sem=pack_recv.at[j], device_id=peer(j), device_id_type=MESH)

    for j in range(HALF_CHIPS):
        pack[j] = message(product, j)

        @pl.when(jnp.logical_not(is_self(j)))
        def _():
            pack_copy(j).start()

        @pl.when(is_self(j))
        def _():
            recv[j] = pack[j]

    rows_out[0] = -product
    cross_copy = to_sibling(rows_out.at[0, their_rows], cross_ref.at[:, mine], rows_sem.at[0])
    cross_copy.start()
    cross_ref[:, mine] = rows_out[0, my_rows]

    for j in range(HALF_CHIPS):
        @pl.when(jnp.logical_not(is_self(j)))
        def _():
            arrival(j).wait_recv()

    first = recv[:, :16].reshape(HALF_CHIPS * 16, 128).T
    second = recv[:, 16:].reshape(HALF_CHIPS * 16, 128).T

    def update(columns):
        def rows(k):
            return coupled_ref[:, 16 * k:16 * k + 16, columns].reshape(HALF_CHIPS * 16, HALF)
        return dot(first[:48], rows(0)) + dot(first[64:112], rows(1)) + dot(second[:48], rows(2))

    part2_copy = to_sibling(part2_out, part2_in, part2_sem)
    part2_out[...] = update(theirs)
    part2_copy.start()
    sigma = update(mine) + gram_ref[...]
    part2_copy.wait_recv()
    sigma = sigma + part2_in[...]

    @pl.when(p > 0)
    def _():
        next_out[...] = sigma.astype(BF16)
        next_copy.start()

    rows_out[1] = sigma
    sigma_copy = to_sibling(rows_out.at[1, their_rows], sigma_ref.at[:, mine], rows_sem.at[1])
    sigma_copy.start()
    sigma_ref[:, mine] = rows_out[1, my_rows]

    @pl.when(p > 0)
    def _():
        next_copy.wait_send()

    part_copy.wait_send()
    part2_copy.wait_send()
    for j in range(HALF_CHIPS):
        @pl.when(jnp.logical_not(is_self(j)))
        def _():
            pack_copy(j).wait_send()
    cross_copy.wait()
    sigma_copy.wait()


def run_chain(flag, coupled, gram, end):
    vmem = pl.BlockSpec(memory_space=pltpu.VMEM)
    dma = pltpu.SemaphoreType.DMA
    return pl.pallas_call(
        chain,
        out_shape=[jax.ShapeDtypeStruct((OWN, B), F32)] * 2,
        in_specs=[pl.BlockSpec(memory_space=pltpu.SMEM), vmem, vmem, vmem],
        out_specs=[vmem, vmem],
        scratch_shapes=[
            pltpu.VMEM((PANEL, HALF), F32),
            pltpu.VMEM((PANEL, HALF), BF16),
            pltpu.VMEM((PANEL, HALF), BF16),
            pltpu.VMEM((PANEL, HALF), F32),
            pltpu.VMEM((PANEL, HALF), F32),
            pltpu.VMEM((PANEL, HALF), F32),
            pltpu.VMEM((PANEL, HALF), F32),
            pltpu.VMEM((HALF_CHIPS, 32, 128), BF16),
            pltpu.VMEM((HALF_CHIPS, 32, 128), BF16),
            pltpu.VMEM((2, PANEL, HALF), F32),
            dma((2,)), dma((2,)), dma((2,)), dma((2,)), dma((2, 2)),
            dma((HALF_CHIPS,)), dma((HALF_CHIPS,)),
        ],
        compiler_params=pltpu.CompilerParams(
            collective_id=0, has_side_effects=True, vmem_limit_bytes=40 * 1024 * 1024),
    )(flag, coupled, gram, end)


def shards(w_inv, lower_block, sigma_end, chain_break):
    weight_rows = w_inv[0]
    lower_rows = lower_block[0]
    r = lax.axis_index("rows")
    chip, core = r // 2, r % 2
    weight_full = lax.all_gather(weight_rows, "rows", axis=0, tiled=True)
    coupled_rows = jnp.dot(lower_rows, weight_full, preferred_element_type=F32)
    coupled_full = lax.all_gather(coupled_rows.astype(BF16), "rows", axis=0, tiled=True)
    coupled = lax.dynamic_slice_in_dim(coupled_full, core * HALF, HALF, 0)
    own = lax.dynamic_slice_in_dim(weight_full, chip * PANEL, PANEL, 1)
    cols = lax.dynamic_slice_in_dim(weight_full, core * HALF, HALF, 1)
    gram = lax.dot_general(own, cols, (((0,), (0,)), ((), ())), preferred_element_type=F32)
    part = lax.axis_index("tm")
    flag = lax.dynamic_slice_in_dim(chain_break, part, 1, 0)
    sigma, cross = run_chain(flag, coupled.reshape(HALF_CHIPS, PANEL, B), gram, sigma_end)
    return (sigma[None], cross[None])


def solution(mesh):
    in_specs = (P("tm", "rows", None), P("tm", "rows", None), P("rows", None), P())
    out_specs = (P("tm", "rows", None), P("tm", "rows", None))
    return jax.shard_map(shards, mesh=mesh, in_specs=in_specs, out_specs=out_specs, check_vma=False)
```

```python
import jax
import jax.numpy as jnp
from jax import lax
from jax.experimental import pallas as pl
from jax.experimental.pallas import tpu as pltpu
from jax.sharding import PartitionSpec as P

MESH = pl.DeviceIdType.MESH
BF16 = jnp.bfloat16
F32 = jnp.float32
B = 1536
CHIPS = 32
HALF_CHIPS = 16
PANEL = 48
OWN = 24
HALF = 768
WINDOW = 256


def dot(a, b):
    return jnp.dot(a, b, preferred_element_type=F32)


def message(product, j):
    start = PANEL * j
    tile, off = start // 128, start % 128
    lanes = lax.broadcasted_iota(jnp.int32, (PANEL, 128), 1)
    block = product[:, tile * 128:(tile + 1) * 128]
    if off:
        block = pltpu.roll(block, 128 - off, 1)
        if off + PANEL > 128:
            after = pltpu.roll(product[:, (tile + 1) * 128:(tile + 2) * 128], 128 - off, 1)
            block = jnp.where(lanes < 128 - off, block, after)
    top = jnp.where(lanes[:16] < 64, block[:16], pltpu.roll(block[16:32], 64, 1))
    return jnp.concatenate([top, block[32:48]], axis=0).astype(BF16)


class Ring:
    def __init__(self, buf, sems, p, y, x, core, place, source):
        self.buf, self.sems = buf, sems
        self.p, self.y, self.x, self.core = p, y, x, core
        self.place, self.source = place, source
        self.sign = 1 - 2 * core

    def copy(self, slot, second, send, receive, y, x):
        block = self.buf.at[slot, :, HALF * second:HALF * (second + 1)]
        return pltpu.make_async_remote_copy(
            src_ref=block, dst_ref=block, send_sem=send, recv_sem=receive,
            device_id=(self.p, (y * 4 + x) * 2 + self.core), device_id_type=MESH)

    def along_x(self, slot, second, way):
        sends = self.sems[0].at[slot, second, 1 + way]
        return self.copy(
            slot, second, sends, self.sems[1].at[slot, second], self.y, (self.x + way) % 4)

    def along_y(self, slot, second, back):
        step = -self.sign if back else self.sign
        sends = self.sems[0].at[slot, second, back]
        return self.copy(
            slot, second, sends, self.sems[1].at[slot, second], (self.y + step + 8) % 8, self.x)

    def arrived(self, slot, second):
        self.along_x(slot, second, 1).wait_recv()

    def columns(self):
        return [(self.x + i) % 4 for i in (0, 1, 3, 2)]

    def own_sends(self, act):
        act(self.along_y(self.place, 1, 0))
        act(self.along_y(self.place, 1, 1))
        for way in (1, 3, 2):
            act(self.along_x(self.place, 0, way))
        act(self.along_y(self.place, 0, 0))
        act(self.along_y(self.place, 0, 1))
        for way in (1, 3, 2):
            act(self.along_x(self.place, 1, way))

    def row_sends(self, act, wait):
        for column in self.columns()[1:]:
            slot = (self.y % 4) * 4 + column
            if wait:
                self.arrived(slot, 0)
            act(self.along_y(slot, 0, 0))
            act(self.along_y(slot, 0, 1))

    def hop(self, act, wait, distance, back):
        step = self.sign * distance * (1 if back else -1)
        origin = (self.y + step + 8) % 8
        last = distance == (3 if back else 4)

        @pl.when(origin // 4 == self.core)
        def _():
            row = (origin % 4) * 4
            slot = row + self.x
            if wait:
                self.arrived(slot, 1)
            if not last:
                act(self.along_y(slot, 1, back))
            for way in (1, 3, 2):
                act(self.along_x(slot, 1, way))
            for column in self.columns():
                if wait:
                    self.arrived(row + column, 0)
                if not last:
                    act(self.along_y(row + column, 0, back))

    def walk(self, act, wait):
        @pl.when(self.source)
        def _():
            self.own_sends(act)
            self.row_sends(act, wait)

        for distance in range(1, 5):
            self.hop(act, wait, distance, 0)
            if distance < 4:
                self.hop(act, wait, distance, 1)

    def run(self):
        self.walk(lambda copy: copy.start(), True)
        for s in range(4):
            for way in (1, 3, 2):
                self.arrived(s * 4 + (self.x + way) % 4, 1)

    def finish(self):
        self.walk(lambda copy: copy.wait_send(), False)


def chain(
    flag_ref, weight_rows, lower_rows, end_ref, sigma_ref, cross_ref,
    weight_ref, coupled_ref, weight_out, weight_in, lower_out, lower_buf,
    coupled_out, coupled_in, gram_buf, end_buf, next_buf, next_out, part_out, part_in, part2_out, part2_in, pack, recv, rows_out,
    weight_sem, lower_sem, coupled_sem, weight_send, weight_recv, coupled_send, coupled_recv,
    end_sem, next_sem, part_sem, part2_sem, rows_sem, pack_send, pack_recv,
):
    parts = 8
    p = lax.axis_index("tm")
    r = lax.axis_index("rows")
    chip, core = r // 2, r % 2
    half = chip // HALF_CHIPS
    place = chip % HALF_CHIPS
    y, x = chip // 4, chip % 4
    source_core = core == half
    sibling = (p, chip * 2 + 1 - core)

    def peer(j):
        return (p, (core * HALF_CHIPS + j) * 2 + half)

    barrier = pltpu.get_barrier_semaphore()
    pl.semaphore_signal(barrier, 1, device_id=sibling, device_id_type=MESH)

    @pl.when(p > 0)
    def _():
        pl.semaphore_signal(barrier, 1, device_id=(p - 1, r), device_id_type=MESH)

    @pl.when(p < parts - 1)
    def _():
        pl.semaphore_signal(barrier, 1, device_id=(p + 1, r), device_id_type=MESH)

    def is_self(j):
        return jnp.logical_and(core == half, place == j)

    for j in range(HALF_CHIPS):
        @pl.when(jnp.logical_not(is_self(j)))
        def _():
            pl.semaphore_signal(barrier, 1, device_id=peer(j), device_id_type=MESH)

    for around in (1, 7):
        there = ((y + around) % 8) * 4 + x
        pl.semaphore_signal(
            barrier, 1, device_id=(p, there * 2 + core), device_id_type=MESH)
    for around in (1, 2, 3):
        there = y * 4 + (x + around) % 4
        pl.semaphore_signal(
            barrier, 1, device_id=(p, there * 2 + core), device_id_type=MESH)

    expected = (
        6 + jnp.where(p > 0, 1, 0) + jnp.where(p < parts - 1, 1, 0)
        + HALF_CHIPS - jnp.where(core == half, 1, 0)
    )
    pl.semaphore_wait(barrier, expected)

    mine = pl.ds(pl.multiple_of(core * HALF, 128), HALF)
    theirs = pl.ds(pl.multiple_of((1 - core) * HALF, 128), HALF)
    my_rows = pl.ds(pl.multiple_of(core * OWN, 8), OWN)
    their_rows = pl.ds(pl.multiple_of((1 - core) * OWN, 8), OWN)

    def to_sibling(src, dst, sems):
        return pltpu.make_async_remote_copy(
            src_ref=src, dst_ref=dst, send_sem=sems.at[0], recv_sem=sems.at[1],
            device_id=sibling, device_id_type=MESH)

    end_copy = to_sibling(end_ref.at[:, theirs], end_buf.at[my_rows], end_sem)
    end_copy.start()
    end_buf[my_rows] = end_ref[:, mine]

    weight_out[...] = weight_rows[...].astype(F32)
    weight_copy = to_sibling(weight_out, weight_in.at[my_rows], weight_sem)

    @pl.when(jnp.logical_not(source_core))
    def _():
        weight_copy.start()

    lower_out[...] = lower_rows[...].astype(F32)
    lower_copy = to_sibling(lower_out.at[:, theirs], lower_buf.at[my_rows], lower_sem)
    lower_copy.start()
    lower_buf[my_rows] = lower_out[:, mine]

    weight_ring = Ring(weight_ref, (weight_send, weight_recv), p, y, x, core, place, source_core)
    coupled_ring = Ring(
        coupled_ref, (coupled_send, coupled_recv), p, y, x, core, place, source_core)

    @pl.when(source_core)
    def _():
        weight_in[my_rows] = weight_out[...]
        weight_copy.wait_recv()
        weight_ref[place] = weight_in[...].astype(BF16)

    weight_ring.run()
    lower_copy.wait_recv()
    lower = lower_buf[...].astype(BF16)

    def coupled_copy(k):
        columns = pl.ds(HALF * k, HALF)
        return to_sibling(
            coupled_out.at[:, columns], coupled_in.at[:, columns], coupled_sem.at[k])

    for k in range(2):
        coupled_out[:, HALF * k:HALF * (k + 1)] = dot(
            lower, weight_ref[:, :, HALF * k:HALF * (k + 1)].reshape(HALF, HALF))

        @pl.when(jnp.logical_not(source_core))
        def _():
            coupled_copy(k).start()

    @pl.when(source_core)
    def _():
        for k in range(2):
            coupled_copy(k).wait_recv()
        coupled_ref[place] = (coupled_out[...] + coupled_in[...]).astype(BF16)

    coupled_ring.run()
    end_copy.wait_recv()

    next_copy = pltpu.make_async_remote_copy(
        src_ref=next_out, dst_ref=next_buf, send_sem=next_sem.at[0], recv_sem=next_sem.at[1],
        device_id=(jnp.maximum(p - 1, 0), r), device_id_type=MESH)

    @pl.when(p < parts - 1)
    def _():
        next_copy.wait_recv()

    @pl.when(p == parts - 1)
    def _():
        next_buf[...] = jnp.zeros_like(next_buf)

    use_end = jnp.logical_or(flag_ref[p] == 1, p == parts - 1)
    source = jnp.where(use_end, end_buf[...].astype(BF16), next_buf[...])

    part_copy = to_sibling(part_out, part_in, part_sem)
    part_out[...] = dot(source, coupled_ref[:, :, theirs].reshape(HALF, HALF))
    part_copy.start()
    product = dot(source, coupled_ref[:, :, mine].reshape(HALF, HALF))
    part_copy.wait_recv()
    product = product + part_in[...]

    def pack_copy(j):
        return pltpu.make_async_remote_copy(
            src_ref=pack.at[j], dst_ref=recv.at[place], send_sem=pack_send.at[j],
            recv_sem=pack_recv.at[place], device_id=peer(j), device_id_type=MESH)

    def arrival(j):
        return pltpu.make_async_remote_copy(
            src_ref=pack.at[j], dst_ref=recv.at[j], send_sem=pack_send.at[j],
            recv_sem=pack_recv.at[j], device_id=peer(j), device_id_type=MESH)

    for j in range(HALF_CHIPS):
        pack[j] = message(product, j)

        @pl.when(jnp.logical_not(is_self(j)))
        def _():
            pack_copy(j).start()

        @pl.when(is_self(j))
        def _():
            recv[j] = pack[j]

    rows_out[0] = -product
    cross_copy = to_sibling(rows_out.at[0, their_rows], cross_ref.at[:, mine], rows_sem.at[0])
    cross_copy.start()
    cross_ref[:, mine] = rows_out[0, my_rows]

    window = jnp.minimum(chip * PANEL // 128, (B - WINDOW) // 128) * 128
    own = weight_ref[:, :, pl.ds(pl.multiple_of(window, 128), WINDOW)].reshape(HALF, WINDOW).T
    for k in range(B // WINDOW):
        gram_buf[:, WINDOW * k:WINDOW * (k + 1)] = dot(
            own, weight_ref[:, :, WINDOW * k:WINDOW * (k + 1)].reshape(HALF, WINDOW))
    gram_rows = pl.ds(pl.multiple_of(chip * PANEL - window, 16), PANEL)

    for j in range(HALF_CHIPS):
        @pl.when(jnp.logical_not(is_self(j)))
        def _():
            arrival(j).wait_recv()

    first = recv[:, :16].reshape(HALF_CHIPS * 16, 128).T
    second = recv[:, 16:].reshape(HALF_CHIPS * 16, 128).T

    def update(columns):
        def rows(k):
            return coupled_ref[:, 16 * k:16 * k + 16, columns].reshape(HALF_CHIPS * 16, HALF)
        return (
            gram_buf[gram_rows, columns]
            + dot(first[:48], rows(0)) + dot(first[64:112], rows(1)) + dot(second[:48], rows(2)))

    part2_copy = to_sibling(part2_out, part2_in, part2_sem)
    part2_out[...] = update(theirs)
    part2_copy.start()
    sigma = update(mine)
    part2_copy.wait_recv()
    sigma = sigma + part2_in[...]

    @pl.when(p > 0)
    def _():
        next_out[...] = sigma.astype(BF16)
        next_copy.start()

    rows_out[1] = sigma
    sigma_copy = to_sibling(rows_out.at[1, their_rows], sigma_ref.at[:, mine], rows_sem.at[1])
    sigma_copy.start()
    sigma_ref[:, mine] = rows_out[1, my_rows]

    @pl.when(p > 0)
    def _():
        next_copy.wait_send()

    end_copy.wait_send()
    lower_copy.wait_send()

    @pl.when(jnp.logical_not(source_core))
    def _():
        weight_copy.wait_send()
        for k in range(2):
            coupled_copy(k).wait_send()

    weight_ring.finish()
    coupled_ring.finish()
    part_copy.wait_send()
    part2_copy.wait_send()
    for j in range(HALF_CHIPS):
        @pl.when(jnp.logical_not(is_self(j)))
        def _():
            pack_copy(j).wait_send()
    cross_copy.wait()
    sigma_copy.wait()


def run_chain(flag, weight, lower, end):
    vmem = pl.BlockSpec(memory_space=pltpu.VMEM)
    dma = pltpu.SemaphoreType.DMA
    return pl.pallas_call(
        chain,
        out_shape=[jax.ShapeDtypeStruct((OWN, B), F32)] * 2,
        in_specs=[pl.BlockSpec(memory_space=pltpu.SMEM), vmem, vmem, vmem],
        out_specs=[vmem, vmem],
        scratch_shapes=[
            pltpu.VMEM((HALF_CHIPS, PANEL, B), BF16),
            pltpu.VMEM((HALF_CHIPS, PANEL, B), BF16),
            pltpu.VMEM((OWN, B), F32),
            pltpu.VMEM((PANEL, B), F32),
            pltpu.VMEM((OWN, B), F32),
            pltpu.VMEM((PANEL, HALF), F32),
            pltpu.VMEM((PANEL, B), F32),
            pltpu.VMEM((PANEL, B), F32),
            pltpu.VMEM((WINDOW, B), F32),
            pltpu.VMEM((PANEL, HALF), F32),
            pltpu.VMEM((PANEL, HALF), BF16),
            pltpu.VMEM((PANEL, HALF), BF16),
            pltpu.VMEM((PANEL, HALF), F32),
            pltpu.VMEM((PANEL, HALF), F32),
            pltpu.VMEM((PANEL, HALF), F32),
            pltpu.VMEM((PANEL, HALF), F32),
            pltpu.VMEM((HALF_CHIPS, 32, 128), BF16),
            pltpu.VMEM((HALF_CHIPS, 32, 128), BF16),
            pltpu.VMEM((2, PANEL, HALF), F32),
            dma((2,)), dma((2,)), dma((2, 2)),
            dma((HALF_CHIPS, 2, 5)), dma((HALF_CHIPS, 2)),
            dma((HALF_CHIPS, 2, 5)), dma((HALF_CHIPS, 2)),
            dma((2,)), dma((2,)), dma((2,)), dma((2,)), dma((2, 2)),
            dma((HALF_CHIPS,)), dma((HALF_CHIPS,)),
        ],
        compiler_params=pltpu.CompilerParams(
            collective_id=0, has_side_effects=True, vmem_limit_bytes=40 * 1024 * 1024),
    )(flag, weight, lower, end)


def shards(w_inv, lower_block, sigma_end, chain_break):
    sigma, cross = run_chain(chain_break, w_inv[0], lower_block[0], sigma_end)
    return (sigma[None], cross[None])


def solution(mesh):
    in_specs = (P("tm", "rows", None), P("tm", "rows", None), P("rows", None), P())
    out_specs = (P("tm", "rows", None), P("tm", "rows", None))
    return jax.shard_map(shards, mesh=mesh, in_specs=in_specs, out_specs=out_specs, check_vma=False)
```

```python
import jax
import jax.numpy as jnp
from jax import lax
from jax.experimental import pallas as pl
from jax.experimental.pallas import tpu as pltpu
from jax.sharding import PartitionSpec as P

MESH = pl.DeviceIdType.MESH
BF16 = jnp.bfloat16
F32 = jnp.float32
B = 1536
CHIPS = 32
HALF_CHIPS = 16
PANEL = 48
OWN = 24
HALF = 768
WINDOW = 256


def dot(a, b):
    return jnp.dot(a, b, preferred_element_type=F32)


def message(product, j):
    start = PANEL * j
    tile, off = start // 128, start % 128
    lanes = lax.broadcasted_iota(jnp.int32, (PANEL, 128), 1)
    block = product[:, tile * 128:(tile + 1) * 128]
    if off:
        block = pltpu.roll(block, 128 - off, 1)
        if off + PANEL > 128:
            after = pltpu.roll(product[:, (tile + 1) * 128:(tile + 2) * 128], 128 - off, 1)
            block = jnp.where(lanes < 128 - off, block, after)
    top = jnp.where(lanes[:16] < 64, block[:16], pltpu.roll(block[16:32], 64, 1))
    return jnp.concatenate([top, block[32:48]], axis=0).astype(BF16)


class Ring:
    def __init__(self, lower, weight, sems, p, y, x, core, place, source):
        self.lower, self.weight = lower, weight
        self.sends, self.receives, self.over, self.came = sems
        self.p, self.y, self.x, self.core = p, y, x, core
        self.place, self.source = place, source
        self.sign = 1 - 2 * core

    def block(self, slot, kind, core):
        if kind == 0:
            return self.lower.at[slot]
        return self.weight.at[HALF_CHIPS * core + slot, :, HALF * (kind - 1):HALF * kind]

    def copy(self, slot, kind, way, y, x):
        block = self.block(slot, kind, self.core)
        return pltpu.make_async_remote_copy(
            src_ref=block, dst_ref=block, send_sem=self.sends.at[slot, kind, way],
            recv_sem=self.receives.at[slot, kind],
            device_id=(self.p, (y * 4 + x) * 2 + self.core), device_id_type=MESH)

    def along_x(self, slot, kind, way):
        return self.copy(slot, kind, 1 + way, self.y, (self.x + way) % 4)

    def along_y(self, slot, kind, back):
        step = self.turn(slot, kind) * (-1 if back else 1)
        return self.copy(slot, kind, back, (self.y + step + 8) % 8, self.x)

    def turn(self, slot, kind):
        return self.sign * (1 - 2 * (slot % 2)) if kind == 0 else self.sign

    def across(self, slot, kind, core):
        block = self.block(slot, kind, core)
        chip = self.y * 4 + self.x
        return pltpu.make_async_remote_copy(
            src_ref=block, dst_ref=block, send_sem=self.over.at[slot, kind - 1],
            recv_sem=self.came.at[slot, kind - 1],
            device_id=(self.p, chip * 2 + 1 - self.core), device_id_type=MESH)

    def arrived(self, slot, kind):
        self.along_x(slot, kind, 1).wait_recv()

    def weights(self, act):
        act(1)

        @pl.when(self.core == 1)
        def _():
            act(2)

    def columns(self):
        return [(self.x + i) % 4 for i in (0, 1, 3, 2)]

    def spread(self, act, slot, kind):
        for way in (1, 3, 2):
            act(self.along_x(slot, kind, way))
        if kind:
            act(self.across(slot, kind, self.core))

    def own_sends(self, act):
        def round_y(kind):
            act(self.along_y(self.place, kind, 0))
            act(self.along_y(self.place, kind, 1))

        self.spread(act, self.place, 0)
        self.weights(round_y)
        round_y(0)
        self.weights(lambda kind: self.spread(act, self.place, kind))

    def row_sends(self, act, wait):
        for column in self.columns()[1:]:
            slot = (self.y % 4) * 4 + column
            if wait:
                self.arrived(slot, 0)
            act(self.along_y(slot, 0, 0))
            act(self.along_y(slot, 0, 1))

    def lower_hop(self, act, wait, distance, pair):
        columns = [(self.x + pair) % 4, (self.x + pair + 2) % 4]
        for back in range(2 if distance < 4 else 1):
            step = self.turn(columns[0], 0) * distance * (1 if back else -1)
            origin = (self.y + step + 8) % 8

            @pl.when(origin // 4 == self.core)
            def _():
                for column in columns:
                    slot = (origin % 4) * 4 + column
                    if wait:
                        self.arrived(slot, 0)
                    if distance < (3 if back else 4):
                        act(self.along_y(slot, 0, back))

    def weight_hop(self, act, wait, distance):
        for back in range(2 if distance < 4 else 1):
            origin = (self.y + self.sign * distance * (1 if back else -1) + 8) % 8

            @pl.when(origin // 4 == self.core)
            def _():
                slot = (origin % 4) * 4 + self.x

                def pass_on(kind):
                    if wait:
                        self.arrived(slot, kind)
                    if distance < (3 if back else 4):
                        act(self.along_y(slot, kind, back))
                    self.spread(act, slot, kind)

                self.weights(pass_on)

    def weight_across(self, act, wait):
        for s in range(4):
            for way in (1, 3, 2):
                slot = s * 4 + (self.x + way) % 4

                def to_sibling(kind):
                    if wait:
                        self.arrived(slot, kind)
                    act(self.across(slot, kind, self.core))

                self.weights(to_sibling)

    def walk(self, act, wait):
        @pl.when(self.source)
        def _():
            self.own_sends(act)
            self.row_sends(act, wait)

        self.weight_hop(act, wait, 1)
        self.lower_hop(act, wait, 1, 0)
        self.weight_hop(act, wait, 2)
        self.lower_hop(act, wait, 1, 1)
        self.weight_hop(act, wait, 3)
        self.lower_hop(act, wait, 2, 0)
        self.weight_hop(act, wait, 4)
        self.lower_hop(act, wait, 2, 1)
        self.lower_hop(act, wait, 3, 0)
        self.lower_hop(act, wait, 3, 1)
        self.weight_across(act, wait)
        self.lower_hop(act, wait, 4, 0)
        self.lower_hop(act, wait, 4, 1)

    def run(self):
        self.walk(lambda copy: copy.start(), True)
        for slot in range(HALF_CHIPS):
            self.across(slot, 1, 1 - self.core).wait_recv()

            @pl.when(self.core == 0)
            def _():
                self.across(slot, 2, 1 - self.core).wait_recv()

    def finish(self):
        self.walk(lambda copy: copy.wait_send(), False)


def chain(
    flag_ref, weight_hbm, lower_hbm, end_hbm, sigma_ref, cross_ref,
    weight_rows, lower_rows, end_ref, weight_ref, lower_ref, coupled_ref,
    rows_there, rows_here, gram_buf, end_buf, next_buf, next_out,
    part_out, part_in, part2_out, part2_in, pack, recv, rows_out,
    load_sem, here_sem, ring_send, ring_recv, across_send, across_recv,
    end_sem, next_sem, part_sem, part2_sem, rows_sem, pack_send, pack_recv,
):
    parts = 8
    p = lax.axis_index("tm")
    r = lax.axis_index("rows")
    chip, core = r // 2, r % 2
    half = chip // HALF_CHIPS
    place = chip % HALF_CHIPS
    y, x = chip // 4, chip % 4
    source_core = core == half
    sibling = (p, chip * 2 + 1 - core)

    def peer(j):
        return (p, (core * HALF_CHIPS + j) * 2 + half)

    loads = [
        pltpu.make_async_copy(src, dst, load_sem.at[k])
        for k, (src, dst) in enumerate(
            ((lower_hbm, lower_rows), (weight_hbm, weight_rows), (end_hbm, end_ref)))
    ]
    for load in loads:
        load.start()
    barrier = pltpu.get_barrier_semaphore()
    pl.semaphore_signal(barrier, 1, device_id=sibling, device_id_type=MESH)

    @pl.when(p > 0)
    def _():
        pl.semaphore_signal(barrier, 1, device_id=(p - 1, r), device_id_type=MESH)

    @pl.when(p < parts - 1)
    def _():
        pl.semaphore_signal(barrier, 1, device_id=(p + 1, r), device_id_type=MESH)

    def is_self(j):
        return jnp.logical_and(core == half, place == j)

    for around in (1, 7):
        there = ((y + around) % 8) * 4 + x
        pl.semaphore_signal(
            barrier, 1, device_id=(p, there * 2 + core), device_id_type=MESH)
    for around in (1, 2, 3):
        there = y * 4 + (x + around) % 4
        pl.semaphore_signal(
            barrier, 1, device_id=(p, there * 2 + core), device_id_type=MESH)

    expected = 6 + jnp.where(p > 0, 1, 0) + jnp.where(p < parts - 1, 1, 0)
    weight_ref[:HALF_CHIPS, :, HALF:] = jnp.zeros((HALF_CHIPS, PANEL, HALF), BF16)
    for load in loads:
        load.wait()
    rows_here[0] = lower_rows[...].astype(F32)
    rows_here[1] = weight_rows[...].astype(F32)
    pl.semaphore_wait(barrier, expected)

    mine = pl.ds(pl.multiple_of(core * HALF, 128), HALF)
    theirs = pl.ds(pl.multiple_of((1 - core) * HALF, 128), HALF)
    my_rows = pl.ds(pl.multiple_of(core * OWN, 8), OWN)
    their_rows = pl.ds(pl.multiple_of((1 - core) * OWN, 8), OWN)

    def to_sibling(src, dst, sems):
        return pltpu.make_async_remote_copy(
            src_ref=src, dst_ref=dst, send_sem=sems.at[0], recv_sem=sems.at[1],
            device_id=sibling, device_id_type=MESH)

    here_copy = to_sibling(rows_here, rows_there, here_sem)

    @pl.when(jnp.logical_not(source_core))
    def _():
        here_copy.start()

    end_copy = to_sibling(end_ref.at[:, theirs], end_buf.at[my_rows], end_sem)
    end_copy.start()
    end_buf[my_rows] = end_ref[:, mine]
    ring = Ring(
        lower_ref, weight_ref, (ring_send, ring_recv, across_send, across_recv),
        p, y, x, core, place, source_core)

    @pl.when(source_core)
    def _():
        here_copy.wait_recv()
        for which, there in ((0, rows_there[0]), (1, rows_there[1])):
            ours = rows_here[which]
            low = jnp.where(core == 0, ours, there)
            high = jnp.where(core == 0, there, ours)
            both = jnp.concatenate([low, high], axis=0).astype(BF16)
            if which == 0:
                lower_ref[place] = both
            else:
                weight_ref[chip] = both

    ring.run()

    @pl.loop(0, B // WINDOW)
    def _(k):
        columns = pl.ds(pl.multiple_of(k * WINDOW, WINDOW), WINDOW)
        right = weight_ref[HALF_CHIPS:, :, columns].reshape(HALF, WINDOW)
        total = dot(lower_ref[:, :, HALF:].reshape(HALF, HALF), right)
        coupled_ref[:, :, columns] = total.astype(BF16).reshape(HALF_CHIPS, PANEL, WINDOW)

        @pl.when(k < HALF // WINDOW)
        def _():
            left = weight_ref[:HALF_CHIPS, :, columns].reshape(HALF, WINDOW)
            more = dot(lower_ref[:, :, :HALF].reshape(HALF, HALF), left) + total
            coupled_ref[:, :, columns] = more.astype(BF16).reshape(HALF_CHIPS, PANEL, WINDOW)

    end_copy.wait_recv()

    next_copy = pltpu.make_async_remote_copy(
        src_ref=next_out, dst_ref=next_buf, send_sem=next_sem.at[0], recv_sem=next_sem.at[1],
        device_id=(jnp.maximum(p - 1, 0), r), device_id_type=MESH)

    @pl.when(p < parts - 1)
    def _():
        next_copy.wait_recv()

    @pl.when(p == parts - 1)
    def _():
        next_buf[...] = jnp.zeros_like(next_buf)

    use_end = jnp.logical_or(flag_ref[p] == 1, p == parts - 1)
    source = jnp.where(use_end, end_buf[...].astype(BF16), next_buf[...])

    part_copy = to_sibling(part_out, part_in, part_sem)
    part_out[...] = dot(source, coupled_ref[:, :, theirs].reshape(HALF, HALF))
    part_copy.start()
    product = dot(source, coupled_ref[:, :, mine].reshape(HALF, HALF))
    part_copy.wait_recv()
    product = product + part_in[...]

    def pack_copy(j):
        return pltpu.make_async_remote_copy(
            src_ref=pack.at[j], dst_ref=recv.at[place], send_sem=pack_send.at[j],
            recv_sem=pack_recv.at[place], device_id=peer(j), device_id_type=MESH)

    def arrival(j):
        return pltpu.make_async_remote_copy(
            src_ref=pack.at[j], dst_ref=recv.at[j], send_sem=pack_send.at[j],
            recv_sem=pack_recv.at[j], device_id=peer(j), device_id_type=MESH)

    for j in range(HALF_CHIPS):
        pack[j] = message(product, j)

        @pl.when(jnp.logical_not(is_self(j)))
        def _():
            pack_copy(j).start()

        @pl.when(is_self(j))
        def _():
            recv[j] = pack[j]

    rows_out[0] = -product
    cross_copy = to_sibling(rows_out.at[0, their_rows], cross_ref.at[:, mine], rows_sem.at[0])
    cross_copy.start()
    cross_ref[:, mine] = rows_out[0, my_rows]

    window = jnp.minimum(chip * PANEL // 128, (B - WINDOW) // 128) * 128
    chips = pl.ds(core * HALF_CHIPS, HALF_CHIPS)
    own = weight_ref[chips, :, pl.ds(pl.multiple_of(window, 128), WINDOW)].reshape(HALF, WINDOW).T
    for k in range(B // WINDOW):
        gram_buf[:, WINDOW * k:WINDOW * (k + 1)] = dot(
            own, weight_ref[chips, :, WINDOW * k:WINDOW * (k + 1)].reshape(HALF, WINDOW))
    gram_rows = pl.ds(pl.multiple_of(chip * PANEL - window, 16), PANEL)

    for j in range(HALF_CHIPS):
        @pl.when(jnp.logical_not(is_self(j)))
        def _():
            arrival(j).wait_recv()

    first = recv[:, :16].reshape(HALF_CHIPS * 16, 128).T
    second = recv[:, 16:].reshape(HALF_CHIPS * 16, 128).T

    def update(columns):
        def rows(k):
            return coupled_ref[:, 16 * k:16 * k + 16, columns].reshape(HALF_CHIPS * 16, HALF)
        return (
            gram_buf[gram_rows, columns]
            + dot(first[:48], rows(0)) + dot(first[64:112], rows(1)) + dot(second[:48], rows(2)))

    part2_copy = to_sibling(part2_out, part2_in, part2_sem)
    part2_out[...] = update(theirs)
    part2_copy.start()
    sigma = update(mine)
    part2_copy.wait_recv()
    sigma = sigma + part2_in[...]

    @pl.when(p > 0)
    def _():
        next_out[...] = sigma.astype(BF16)
        next_copy.start()

    rows_out[1] = sigma
    sigma_copy = to_sibling(rows_out.at[1, their_rows], sigma_ref.at[:, mine], rows_sem.at[1])
    sigma_copy.start()
    sigma_ref[:, mine] = rows_out[1, my_rows]

    @pl.when(p > 0)
    def _():
        next_copy.wait_send()

    end_copy.wait_send()

    @pl.when(jnp.logical_not(source_core))
    def _():
        here_copy.wait_send()

    ring.finish()
    part_copy.wait_send()
    part2_copy.wait_send()
    for j in range(HALF_CHIPS):
        @pl.when(jnp.logical_not(is_self(j)))
        def _():
            pack_copy(j).wait_send()
    cross_copy.wait()
    sigma_copy.wait()


def run_chain(flag, weight, lower, end):
    vmem = pl.BlockSpec(memory_space=pltpu.VMEM)
    dma = pltpu.SemaphoreType.DMA
    return pl.pallas_call(
        chain,
        out_shape=[jax.ShapeDtypeStruct((OWN, B), F32)] * 2,
        in_specs=[pl.BlockSpec(memory_space=pltpu.SMEM)] + [pl.BlockSpec(memory_space=pl.ANY)] * 3,
        out_specs=[vmem, vmem],
        scratch_shapes=[
            pltpu.VMEM((OWN, B), BF16),
            pltpu.VMEM((OWN, B), BF16),
            pltpu.VMEM((OWN, B), F32),
            pltpu.VMEM((CHIPS, PANEL, B), BF16),
            pltpu.VMEM((HALF_CHIPS, PANEL, B), BF16),
            pltpu.VMEM((HALF_CHIPS, PANEL, B), BF16),
            pltpu.VMEM((2, OWN, B), F32),
            pltpu.VMEM((2, OWN, B), F32),
            pltpu.VMEM((WINDOW, B), F32),
            pltpu.VMEM((PANEL, HALF), F32),
            pltpu.VMEM((PANEL, HALF), BF16),
            pltpu.VMEM((PANEL, HALF), BF16),
            pltpu.VMEM((PANEL, HALF), F32),
            pltpu.VMEM((PANEL, HALF), F32),
            pltpu.VMEM((PANEL, HALF), F32),
            pltpu.VMEM((PANEL, HALF), F32),
            pltpu.VMEM((HALF_CHIPS, 32, 128), BF16),
            pltpu.VMEM((HALF_CHIPS, 32, 128), BF16),
            pltpu.VMEM((2, PANEL, HALF), F32),
            dma((3,)), dma((2,)),
            dma((HALF_CHIPS, 3, 5)), dma((HALF_CHIPS, 3)),
            dma((HALF_CHIPS, 2)), dma((HALF_CHIPS, 2)),
            dma((2,)), dma((2,)), dma((2,)), dma((2,)), dma((2, 2)),
            dma((HALF_CHIPS,)), dma((HALF_CHIPS,)),
        ],
        compiler_params=pltpu.CompilerParams(
            collective_id=0, has_side_effects=True, vmem_limit_bytes=40 * 1024 * 1024),
    )(flag, weight, lower, end)


def shards(w_inv, lower_block, sigma_end, chain_break):
    sigma, cross = run_chain(chain_break, w_inv[0], lower_block[0], sigma_end)
    return (sigma[None], cross[None])


def solution(mesh):
    in_specs = (P("tm", "rows", None), P("tm", "rows", None), P("rows", None), P())
    out_specs = (P("tm", "rows", None), P("tm", "rows", None))
    return jax.shard_map(shards, mesh=mesh, in_specs=in_specs, out_specs=out_specs, check_vma=False)
```

```python
import jax
import jax.numpy as jnp
from jax import lax
from jax.experimental import pallas as pl
from jax.experimental.pallas import tpu as pltpu
from jax.sharding import PartitionSpec as P

MESH = pl.DeviceIdType.MESH
BF16 = jnp.bfloat16
F32 = jnp.float32
B = 1536
CHIPS = 32
HALF_CHIPS = 16
PANEL = 48
OWN = 24
HALF = 768
WINDOW = 256
SPLIT = 4


def dot(a, b):
    return jnp.dot(a, b, preferred_element_type=F32)


def message(product, j):
    start = PANEL * j
    tile, off = start // 128, start % 128
    lanes = lax.broadcasted_iota(jnp.int32, (PANEL, 128), 1)
    block = product[:, tile * 128:(tile + 1) * 128]
    if off:
        block = pltpu.roll(block, 128 - off, 1)
        if off + PANEL > 128:
            after = pltpu.roll(product[:, (tile + 1) * 128:(tile + 2) * 128], 128 - off, 1)
            block = jnp.where(lanes < 128 - off, block, after)
    top = jnp.where(lanes[:16] < 64, block[:16], pltpu.roll(block[16:32], 64, 1))
    return jnp.concatenate([top, block[32:48]], axis=0).astype(BF16)


class Ring:
    def __init__(self, lower, weight, sems, p, y, x, core, place, source):
        self.lower, self.weight = lower, weight
        self.sends, self.receives, self.over, self.came = sems
        self.p, self.y, self.x, self.core = p, y, x, core
        self.place, self.source = place, source
        self.sign = 1 - 2 * core

    def block(self, slot, kind, core):
        if kind == 0:
            return self.lower.at[slot]
        return self.weight.at[HALF_CHIPS * core + slot, :, HALF * (kind - 1):HALF * kind]

    def copy(self, slot, kind, way, y, x):
        block = self.block(slot, kind, self.core)
        return pltpu.make_async_remote_copy(
            src_ref=block, dst_ref=block, send_sem=self.sends.at[slot, kind, way],
            recv_sem=self.receives.at[slot, kind],
            device_id=(self.p, (y * 4 + x) * 2 + self.core), device_id_type=MESH)

    def along_x(self, slot, kind, way):
        return self.copy(slot, kind, 1 + way, self.y, (self.x + way) % 4)

    def along_y(self, slot, kind, back):
        step = self.turn(slot, kind) * (-1 if back else 1)
        return self.copy(slot, kind, back, (self.y + step + 8) % 8, self.x)

    def turn(self, slot, kind):
        return self.sign * (1 - 2 * (slot % 2)) if kind == 0 else self.sign

    def across(self, slot, kind, core):
        block = self.block(slot, kind, core)
        chip = self.y * 4 + self.x
        return pltpu.make_async_remote_copy(
            src_ref=block, dst_ref=block, send_sem=self.over.at[slot, kind - 1],
            recv_sem=self.came.at[slot, kind - 1],
            device_id=(self.p, chip * 2 + 1 - self.core), device_id_type=MESH)

    def arrived(self, slot, kind):
        self.along_x(slot, kind, 1).wait_recv()

    def weights(self, act):
        act(1)

        @pl.when(self.core == 1)
        def _():
            act(2)

    def columns(self):
        return [(self.x + i) % 4 for i in (0, 1, 3, 2)]

    def spread(self, act, slot, kind):
        for way in (1, 3, 2):
            act(self.along_x(slot, kind, way))
        if kind:
            act(self.across(slot, kind, self.core))

    def own_sends(self, act):
        def round_y(kind):
            act(self.along_y(self.place, kind, 0))
            act(self.along_y(self.place, kind, 1))

        self.spread(act, self.place, 0)
        self.weights(round_y)
        round_y(0)
        self.weights(lambda kind: self.spread(act, self.place, kind))

    def row_sends(self, act, wait):
        for column in self.columns()[1:]:
            slot = (self.y % 4) * 4 + column
            if wait:
                self.arrived(slot, 0)
            act(self.along_y(slot, 0, 0))
            act(self.along_y(slot, 0, 1))

    def lower_hop(self, act, wait, distance, pair):
        columns = [(self.x + pair) % 4, (self.x + pair + 2) % 4]
        for back in range(2 if distance < 4 else 1):
            step = self.turn(columns[0], 0) * distance * (1 if back else -1)
            origin = (self.y + step + 8) % 8

            @pl.when(origin // 4 == self.core)
            def _():
                for column in columns:
                    slot = (origin % 4) * 4 + column
                    if wait:
                        self.arrived(slot, 0)
                    if distance < (3 if back else 4):
                        act(self.along_y(slot, 0, back))

    def weight_hop(self, act, wait, distance):
        for back in range(2 if distance < 4 else 1):
            origin = (self.y + self.sign * distance * (1 if back else -1) + 8) % 8

            @pl.when(origin // 4 == self.core)
            def _():
                slot = (origin % 4) * 4 + self.x

                def pass_on(kind):
                    if wait:
                        self.arrived(slot, kind)
                    if distance < (3 if back else 4):
                        act(self.along_y(slot, kind, back))
                    self.spread(act, slot, kind)

                self.weights(pass_on)

    def weight_across(self, act, wait):
        for s in range(4):
            for way in (1, 3, 2):
                slot = s * 4 + (self.x + way) % 4

                def to_sibling(kind):
                    if wait:
                        self.arrived(slot, kind)
                    act(self.across(slot, kind, self.core))

                self.weights(to_sibling)

    def walk(self, act, wait):
        @pl.when(self.source)
        def _():
            self.own_sends(act)
            self.row_sends(act, wait)

        self.weight_hop(act, wait, 1)
        self.lower_hop(act, wait, 1, 0)
        self.weight_hop(act, wait, 2)
        self.lower_hop(act, wait, 1, 1)
        self.weight_hop(act, wait, 3)
        self.lower_hop(act, wait, 2, 0)
        self.weight_hop(act, wait, 4)
        self.lower_hop(act, wait, 2, 1)
        self.lower_hop(act, wait, 3, 0)
        self.lower_hop(act, wait, 3, 1)
        self.weight_across(act, wait)
        self.lower_hop(act, wait, 4, 0)
        self.lower_hop(act, wait, 4, 1)

    def run(self):
        self.walk(lambda copy: copy.start(), True)
        for slot in range(HALF_CHIPS):
            self.across(slot, 1, 1 - self.core).wait_recv()

            @pl.when(self.core == 0)
            def _():
                self.across(slot, 2, 1 - self.core).wait_recv()

    def finish(self):
        self.walk(lambda copy: copy.wait_send(), False)


class PlainRing(Ring):
    def __init__(self, held, sems, p, y, x, core, place, source):
        super().__init__(held, held, sems + (None, None), p, y, x, core, place, source)

    def block(self, slot, kind, core):
        return self.lower.at[slot, :, HALF * kind:HALF * (kind + 1)]

    def weights(self, act):
        act(1)

    def spread(self, act, slot, kind):
        for way in (1, 3, 2):
            act(self.along_x(slot, kind, way))

    def weight_across(self, act, wait):
        if wait:
            for s in range(4):
                for way in (1, 3, 2):
                    self.arrived(s * 4 + (self.x + way) % 4, 1)

    def run(self):
        self.walk(lambda copy: copy.start(), True)


def chain(
    flag_ref, weight_hbm, lower_hbm, end_hbm, sigma_ref, cross_ref,
    weight_rows, lower_rows, end_ref, weight_ref, lower_ref, coupled_ref,
    through_ref, through_in, through_out, first_sigma,
    rows_there, rows_here, gram_buf, end_buf, next_buf, next_out,
    part_out, part_in, part2_out, part2_in, pack, recv, rows_out,
    load_sem, here_sem, ring_send, ring_recv, across_send, across_recv,
    through_send, through_recv, through_sem, through_hop, ahead_sem,
    end_sem, next_sem, part_sem, part2_sem, rows_sem, pack_send, pack_recv,
):
    parts = 8
    p = lax.axis_index("tm")
    r = lax.axis_index("rows")
    chip, core = r // 2, r % 2
    half = chip // HALF_CHIPS
    place = chip % HALF_CHIPS
    y, x = chip // 4, chip % 4
    source_core = core == half
    sibling = (p, chip * 2 + 1 - core)

    def peer(j):
        return (p, (core * HALF_CHIPS + j) * 2 + half)

    loads = [
        pltpu.make_async_copy(src, dst, load_sem.at[k])
        for k, (src, dst) in enumerate(
            ((lower_hbm, lower_rows), (weight_hbm, weight_rows), (end_hbm, end_ref)))
    ]
    for load in loads:
        load.start()
    barrier = pltpu.get_barrier_semaphore()
    pl.semaphore_signal(barrier, 1, device_id=sibling, device_id_type=MESH)

    @pl.when(p > 0)
    def _():
        pl.semaphore_signal(barrier, 1, device_id=(p - 1, r), device_id_type=MESH)

    @pl.when(p < parts - 1)
    def _():
        pl.semaphore_signal(barrier, 1, device_id=(p + 1, r), device_id_type=MESH)

    def is_self(j):
        return jnp.logical_and(core == half, place == j)

    for around in (1, 7):
        there = ((y + around) % 8) * 4 + x
        pl.semaphore_signal(
            barrier, 1, device_id=(p, there * 2 + core), device_id_type=MESH)
    for around in (1, 2, 3):
        there = y * 4 + (x + around) % 4
        pl.semaphore_signal(
            barrier, 1, device_id=(p, there * 2 + core), device_id_type=MESH)

    @pl.when(p < SPLIT - 1)
    def _():
        pl.semaphore_signal(barrier, 1, device_id=(SPLIT, r), device_id_type=MESH)

    expected = (
        6 + jnp.where(p > 0, 1, 0) + jnp.where(p < parts - 1, 1, 0)
        + jnp.where(p == SPLIT, SPLIT - 1, 0))
    weight_ref[:HALF_CHIPS, :, HALF:] = jnp.zeros((HALF_CHIPS, PANEL, HALF), BF16)
    for load in loads:
        load.wait()
    rows_here[0] = lower_rows[...].astype(F32)
    rows_here[1] = weight_rows[...].astype(F32)
    pl.semaphore_wait(barrier, expected)

    mine = pl.ds(pl.multiple_of(core * HALF, 128), HALF)
    theirs = pl.ds(pl.multiple_of((1 - core) * HALF, 128), HALF)
    my_rows = pl.ds(pl.multiple_of(core * OWN, 8), OWN)
    their_rows = pl.ds(pl.multiple_of((1 - core) * OWN, 8), OWN)

    def to_sibling(src, dst, sems):
        return pltpu.make_async_remote_copy(
            src_ref=src, dst_ref=dst, send_sem=sems.at[0], recv_sem=sems.at[1],
            device_id=sibling, device_id_type=MESH)

    here_copy = to_sibling(rows_here, rows_there, here_sem)

    @pl.when(jnp.logical_not(source_core))
    def _():
        here_copy.start()

    end_copy = to_sibling(end_ref.at[:, theirs], end_buf.at[my_rows], end_sem)
    end_copy.start()
    end_buf[my_rows] = end_ref[:, mine]
    ring = Ring(
        lower_ref, weight_ref, (ring_send, ring_recv, across_send, across_recv),
        p, y, x, core, place, source_core)

    @pl.when(source_core)
    def _():
        here_copy.wait_recv()
        for which, there in ((0, rows_there[0]), (1, rows_there[1])):
            ours = rows_here[which]
            low = jnp.where(core == 0, ours, there)
            high = jnp.where(core == 0, there, ours)
            both = jnp.concatenate([low, high], axis=0).astype(BF16)
            if which == 0:
                lower_ref[place] = both
            else:
                weight_ref[chip] = both

    ring.run()

    @pl.loop(0, B // WINDOW)
    def _(k):
        columns = pl.ds(pl.multiple_of(k * WINDOW, WINDOW), WINDOW)
        right = weight_ref[HALF_CHIPS:, :, columns].reshape(HALF, WINDOW)
        total = dot(lower_ref[:, :, HALF:].reshape(HALF, HALF), right)
        coupled_ref[:, :, columns] = total.astype(BF16).reshape(HALF_CHIPS, PANEL, WINDOW)

        @pl.when(k < HALF // WINDOW)
        def _():
            left = weight_ref[:HALF_CHIPS, :, columns].reshape(HALF, WINDOW)
            more = dot(lower_ref[:, :, :HALF].reshape(HALF, HALF), left) + total
            coupled_ref[:, :, columns] = more.astype(BF16).reshape(HALF_CHIPS, PANEL, WINDOW)

    end_copy.wait_recv()
    end_b = end_buf[...].astype(BF16)
    broken = flag_ref[p] == 1
    early = p < SPLIT

    def down(src, dst, send, receive, target):
        return pltpu.make_async_remote_copy(
            src_ref=src, dst_ref=dst, send_sem=send, recv_sem=receive,
            device_id=(target, r), device_id_type=MESH)

    below = jnp.maximum(p - 1, 0)
    hops = [
        down(next_out.at[0], next_buf.at[0], next_sem.at[0, 0], next_sem.at[0, 1], below),
        None,
        down(next_out.at[1], next_buf.at[2], next_sem.at[2, 0], next_sem.at[2, 1], below),
    ]
    jumps = [
        down(next_out.at[0], next_buf.at[1], ahead_sem.at[q], next_sem.at[1, 1], q)
        for q in range(SPLIT)
    ]
    through_copy = down(
        through_out, through_in, through_hop.at[0], through_hop.at[1], below)

    def sum_halves(k, source, right_ref):
        copy = to_sibling(part_out.at[k], part_in.at[k], part_sem.at[k])
        part_out[k] = dot(source, right_ref[:, :, theirs].reshape(HALF, HALF))
        copy.start()
        own = dot(source, right_ref[:, :, mine].reshape(HALF, HALF))
        copy.wait_recv()
        return own + part_in[k]

    def pack_copy(k, j):
        return pltpu.make_async_remote_copy(
            src_ref=pack.at[k, j], dst_ref=recv.at[k, place], send_sem=pack_send.at[k, j],
            recv_sem=pack_recv.at[k, place], device_id=peer(j), device_id_type=MESH)

    def arrival(k, j):
        return pltpu.make_async_remote_copy(
            src_ref=pack.at[k, j], dst_ref=recv.at[k, j], send_sem=pack_send.at[k, j],
            recv_sem=pack_recv.at[k, j], device_id=peer(j), device_id_type=MESH)

    def emit(which, value, out_ref, act):
        copy = to_sibling(
            rows_out.at[which, their_rows], out_ref.at[:, mine], rows_sem.at[which])
        if act == "start":
            rows_out[which] = value
            copy.start()
            out_ref[:, mine] = rows_out[which, my_rows]
        else:
            copy.wait()

    def step(k, source, right_ref, meanwhile):
        product = sum_halves(k, source, right_ref)
        for j in range(HALF_CHIPS):
            pack[k, j] = message(product, j)

            @pl.when(jnp.logical_not(is_self(j)))
            def _():
                pack_copy(k, j).start()

            @pl.when(is_self(j))
            def _():
                recv[k, j] = pack[k, j]

        base = meanwhile(product)
        for j in range(HALF_CHIPS):
            @pl.when(jnp.logical_not(is_self(j)))
            def _():
                arrival(k, j).wait_recv()

        first = recv[k, :, :16].reshape(HALF_CHIPS * 16, 128).T
        second = recv[k, :, 16:].reshape(HALF_CHIPS * 16, 128).T

        def update(columns):
            def rows(i):
                return right_ref[:, 16 * i:16 * i + 16, columns].reshape(HALF_CHIPS * 16, HALF)
            total = dot(first[:48], rows(0)) + dot(first[64:112], rows(1))
            total = total + dot(second[:48], rows(2))
            return total if base is None else total + base(columns)

        copy = to_sibling(part2_out.at[k], part2_in.at[k], part2_sem.at[k])
        part2_out[k] = update(theirs)
        copy.start()
        sigma = update(mine)
        copy.wait_recv()
        return sigma + part2_in[k]

    through_ring = PlainRing(
        through_ref, (through_send, through_recv), p, y, x, core, place, source_core)
    through_half = to_sibling(through_out, through_out, through_sem.at[0])
    through_here = to_sibling(through_out, through_ref.at[place, :, mine], through_sem.at[1])
    zero = jnp.zeros((PANEL, HALF), BF16)

    @pl.when(p == SPLIT - 1)
    def _():
        @pl.when(source_core)
        def _():
            next_out[1] = jnp.where(broken, zero, coupled_ref[place, :, theirs])
            half_copy = to_sibling(next_out.at[1], through_out, through_sem.at[0])
            half_copy.start()
            through_out[...] = jnp.where(broken, zero, coupled_ref[place, :, mine])
            half_copy.wait_send()

        @pl.when(jnp.logical_not(source_core))
        def _():
            through_half.wait_recv()

        through_copy.start()

        @pl.loop(0, HALF_CHIPS)
        def _(j):
            rows = coupled_ref[j]
            through_ref[j] = jnp.where(broken, jnp.zeros_like(rows), rows)

    @pl.when(p < SPLIT - 1)
    def _():
        through_copy.wait_recv()
        rows = sum_halves(2, through_in[...], coupled_ref).astype(BF16)
        through_out[...] = jnp.where(broken, zero, rows)

        @pl.when(p > 0)
        def _():
            through_copy.start()

        @pl.when(source_core)
        def _():
            through_ref[place, :, mine] = through_out[...]

        @pl.when(jnp.logical_not(source_core))
        def _():
            through_here.start()

    def gather_through():
        @pl.when(source_core)
        def _():
            to_sibling(through_out, through_ref.at[place, :, theirs], through_sem.at[1]).wait_recv()

        through_ring.run()

    @pl.when(p < SPLIT - 2)
    def _():
        gather_through()

    has_above = jnp.logical_and(p != parts - 1, p != SPLIT - 1)

    @pl.when(has_above)
    def _():
        hops[0].wait_recv()

    @pl.when(jnp.logical_not(has_above))
    def _():
        next_buf[0] = zero

    use_end = jnp.logical_or(broken, p == parts - 1)

    def gram(product):
        window = jnp.minimum(chip * PANEL // 128, (B - WINDOW) // 128) * 128
        chips = pl.ds(core * HALF_CHIPS, HALF_CHIPS)
        own = weight_ref[chips, :, pl.ds(pl.multiple_of(window, 128), WINDOW)]
        own = own.reshape(HALF, WINDOW).T
        for k in range(B // WINDOW):
            columns = slice(WINDOW * k, WINDOW * (k + 1))
            gram_buf[:, columns] = dot(own, weight_ref[chips, :, columns].reshape(HALF, WINDOW))
        gram_rows = pl.ds(pl.multiple_of(chip * PANEL - window, 16), PANEL)

        @pl.when(jnp.logical_not(early))
        def _():
            emit(0, -product, cross_ref, "start")

        return lambda columns: gram_buf[gram_rows, columns]

    sigma = step(0, jnp.where(use_end, end_b, next_buf[0]), coupled_ref, gram)
    next_out[0] = sigma.astype(BF16)
    sends_down = jnp.logical_and(p > 0, p != SPLIT)

    @pl.when(sends_down)
    def _():
        hops[0].start()

    @pl.when(p == SPLIT)
    def _():
        for jump in jumps:
            jump.start()

    @pl.when(jnp.logical_not(early))
    def _():
        emit(1, sigma, sigma_ref, "start")

    @pl.when(early)
    def _():
        first_sigma[...] = sigma

        @pl.when(p == SPLIT - 2)
        def _():
            gather_through()

        jumps[0].wait_recv()
        whole = first_sigma[...] + step(1, next_buf[1], through_ref, lambda product: None)
        next_out[1] = whole.astype(BF16)

        @pl.when(p > 0)
        def _():
            hops[2].start()

        emit(1, whole, sigma_ref, "start")

        @pl.when(p < SPLIT - 1)
        def _():
            hops[2].wait_recv()

        @pl.when(p == SPLIT - 1)
        def _():
            next_buf[2] = next_buf[1]

        source = jnp.where(broken, end_b, next_buf[2])
        emit(0, -sum_halves(3, source, coupled_ref), cross_ref, "start")

    end_copy.wait_send()

    @pl.when(jnp.logical_not(source_core))
    def _():
        here_copy.wait_send()

    ring.finish()

    def sent(k):
        to_sibling(part_out.at[k], part_in.at[k], part_sem.at[k]).wait_send()

    def step_sent(k):
        sent(k)
        to_sibling(part2_out.at[k], part2_in.at[k], part2_sem.at[k]).wait_send()
        for j in range(HALF_CHIPS):
            @pl.when(jnp.logical_not(is_self(j)))
            def _():
                pack_copy(k, j).wait_send()

    step_sent(0)

    @pl.when(sends_down)
    def _():
        hops[0].wait_send()

    @pl.when(p == SPLIT)
    def _():
        for jump in jumps:
            jump.wait_send()

    @pl.when(early)
    def _():
        step_sent(1)
        sent(3)

        @pl.when(p > 0)
        def _():
            through_copy.wait_send()
            hops[2].wait_send()

    @pl.when(p < SPLIT - 1)
    def _():
        sent(2)
        through_ring.finish()

        @pl.when(jnp.logical_not(source_core))
        def _():
            through_here.wait_send()

    emit(0, None, cross_ref, "wait")
    emit(1, None, sigma_ref, "wait")


def run_chain(flag, weight, lower, end):
    vmem = pl.BlockSpec(memory_space=pltpu.VMEM)
    dma = pltpu.SemaphoreType.DMA
    return pl.pallas_call(
        chain,
        out_shape=[jax.ShapeDtypeStruct((OWN, B), F32)] * 2,
        in_specs=[pl.BlockSpec(memory_space=pltpu.SMEM)] + [pl.BlockSpec(memory_space=pl.ANY)] * 3,
        out_specs=[vmem, vmem],
        scratch_shapes=[
            pltpu.VMEM((OWN, B), BF16),
            pltpu.VMEM((OWN, B), BF16),
            pltpu.VMEM((OWN, B), F32),
            pltpu.VMEM((CHIPS, PANEL, B), BF16),
            pltpu.VMEM((HALF_CHIPS, PANEL, B), BF16),
            pltpu.VMEM((HALF_CHIPS, PANEL, B), BF16),
            pltpu.VMEM((HALF_CHIPS, PANEL, B), BF16),
            pltpu.VMEM((PANEL, HALF), BF16),
            pltpu.VMEM((PANEL, HALF), BF16),
            pltpu.VMEM((PANEL, HALF), F32),
            pltpu.VMEM((2, OWN, B), F32),
            pltpu.VMEM((2, OWN, B), F32),
            pltpu.VMEM((WINDOW, B), F32),
            pltpu.VMEM((PANEL, HALF), F32),
            pltpu.VMEM((3, PANEL, HALF), BF16),
            pltpu.VMEM((2, PANEL, HALF), BF16),
            pltpu.VMEM((4, PANEL, HALF), F32),
            pltpu.VMEM((4, PANEL, HALF), F32),
            pltpu.VMEM((2, PANEL, HALF), F32),
            pltpu.VMEM((2, PANEL, HALF), F32),
            pltpu.VMEM((2, HALF_CHIPS, 32, 128), BF16),
            pltpu.VMEM((2, HALF_CHIPS, 32, 128), BF16),
            pltpu.VMEM((2, PANEL, HALF), F32),
            dma((3,)), dma((2,)),
            dma((HALF_CHIPS, 3, 5)), dma((HALF_CHIPS, 3)),
            dma((HALF_CHIPS, 2)), dma((HALF_CHIPS, 2)),
            dma((HALF_CHIPS, 2, 5)), dma((HALF_CHIPS, 2)),
            dma((2, 2)), dma((2,)), dma((SPLIT,)),
            dma((2,)), dma((3, 2)), dma((4, 2)), dma((2, 2)), dma((2, 2)),
            dma((2, HALF_CHIPS)), dma((2, HALF_CHIPS)),
        ],
        compiler_params=pltpu.CompilerParams(
            collective_id=0, has_side_effects=True, vmem_limit_bytes=40 * 1024 * 1024),
    )(flag, weight, lower, end)


def shards(w_inv, lower_block, sigma_end, chain_break):
    sigma, cross = run_chain(chain_break, w_inv[0], lower_block[0], sigma_end)
    return (sigma[None], cross[None])


def solution(mesh):
    in_specs = (P("tm", "rows", None), P("tm", "rows", None), P("rows", None), P())
    out_specs = (P("tm", "rows", None), P("tm", "rows", None))
    return jax.shard_map(shards, mesh=mesh, in_specs=in_specs, out_specs=out_specs, check_vma=False)
```

```python
import jax
import jax.numpy as jnp
from jax import lax
from jax.experimental import pallas as pl
from jax.experimental.pallas import tpu as pltpu
from jax.sharding import PartitionSpec as P

MESH = pl.DeviceIdType.MESH
BF16 = jnp.bfloat16
F32 = jnp.float32
B = 1536
CHIPS = 32
HALF_CHIPS = 16
PANEL = 48
OWN = 24
HALF = 768
WINDOW = 256
SPLIT = 4


def dot(a, b):
    return jnp.dot(a, b, preferred_element_type=F32)


def message(product, j):
    start = PANEL * j
    tile, off = start // 128, start % 128
    lanes = lax.broadcasted_iota(jnp.int32, (PANEL, 128), 1)
    block = product[:, tile * 128:(tile + 1) * 128]
    if off:
        block = pltpu.roll(block, 128 - off, 1)
        if off + PANEL > 128:
            after = pltpu.roll(product[:, (tile + 1) * 128:(tile + 2) * 128], 128 - off, 1)
            block = jnp.where(lanes < 128 - off, block, after)
    top = jnp.where(lanes[:16] < 64, block[:16], pltpu.roll(block[16:32], 64, 1))
    return jnp.concatenate([top, block[32:48]], axis=0).astype(BF16)


class Ring:
    def __init__(self, lower, weight, sems, p, y, x, core, place, source):
        self.lower, self.weight = lower, weight
        self.sends, self.receives, self.over = sems
        self.p, self.y, self.x, self.core = p, y, x, core
        self.place, self.source = place, source
        self.sign = 1 - 2 * core

    def block(self, slot, kind, core):
        if kind == 0:
            return self.lower.at[slot]
        return self.weight.at[HALF_CHIPS * core + slot, :, HALF * (kind - 1):HALF * kind]

    def copy(self, slot, kind, way, y, x):
        block = self.block(slot, kind, self.core)
        return pltpu.make_async_remote_copy(
            src_ref=block, dst_ref=block, send_sem=self.sends.at[self.sender(slot, kind, way)],
            recv_sem=self.receives.at[slot, kind],
            device_id=(self.p, (y * 4 + x) * 2 + self.core), device_id_type=MESH)

    def sender(self, slot, kind, way):
        if kind:
            return 35 + 20 * (kind - 1) + 5 * (slot // 4) + way
        return 2 * slot + way if way < 2 else 30 + way

    def along_x(self, slot, kind, way):
        return self.copy(slot, kind, 1 + way, self.y, (self.x + way) % 4)

    def along_y(self, slot, kind, back):
        step = self.turn(slot, kind) * (-1 if back else 1)
        return self.copy(slot, kind, back, (self.y + step + 8) % 8, self.x)

    def turn(self, slot, kind):
        return self.sign * (1 - 2 * (slot % 2)) if kind == 0 else self.sign

    def across(self, block):
        chip = self.y * 4 + self.x
        return pltpu.make_async_remote_copy(
            src_ref=block, dst_ref=block, send_sem=self.over.at[0], recv_sem=self.over.at[1],
            device_id=(self.p, chip * 2 + 1 - self.core), device_id_type=MESH)

    def arrived(self, slot, kind):
        self.along_x(slot, kind, 1).wait_recv()

    def weights(self, act):
        act(1)

        @pl.when(self.core == 1)
        def _():
            act(2)

    def columns(self):
        return [(self.x + i) % 4 for i in (0, 1, 3, 2)]

    def spread(self, act, slot, kind, first):
        for way in (1, 3, 2):
            act(self.along_x(slot, kind, way))
        if kind and first:
            self.across(self.block(slot, kind, self.core)).start()

    def own_sends(self, act, first):
        def round_y(kind):
            act(self.along_y(self.place, kind, 0))
            act(self.along_y(self.place, kind, 1))

        self.spread(act, self.place, 0, first)
        self.weights(round_y)
        round_y(0)
        self.weights(lambda kind: self.spread(act, self.place, kind, first))

    def row_sends(self, act, wait):
        for column in self.columns()[1:]:
            slot = (self.y % 4) * 4 + column
            if wait:
                self.arrived(slot, 0)
            act(self.along_y(slot, 0, 0))
            act(self.along_y(slot, 0, 1))

    def lower_hop(self, act, wait, distance, pair):
        columns = [(self.x + pair) % 4, (self.x + pair + 2) % 4]
        for back in range(2 if distance < 4 else 1):
            step = self.turn(columns[0], 0) * distance * (1 if back else -1)
            origin = (self.y + step + 8) % 8

            @pl.when(origin // 4 == self.core)
            def _():
                for column in columns:
                    slot = (origin % 4) * 4 + column
                    if wait:
                        self.arrived(slot, 0)
                    if distance < (3 if back else 4):
                        act(self.along_y(slot, 0, back))

    def weight_hop(self, act, wait, distance):
        for back in range(2 if distance < 4 else 1):
            origin = (self.y + self.sign * distance * (1 if back else -1) + 8) % 8

            @pl.when(origin // 4 == self.core)
            def _():
                slot = (origin % 4) * 4 + self.x

                def pass_on(kind):
                    if wait:
                        self.arrived(slot, kind)
                    if distance < (3 if back else 4):
                        act(self.along_y(slot, kind, back))
                    self.spread(act, slot, kind, wait)

                self.weights(pass_on)

    def weight_across(self):
        for s in range(4):
            for way in (1, 3, 2):
                slot = s * 4 + (self.x + way) % 4

                def to_sibling(kind):
                    self.arrived(slot, kind)
                    self.across(self.block(slot, kind, self.core)).start()

                self.weights(to_sibling)

    def both_ways(self, act):
        lower_rows = self.weight.at[:HALF_CHIPS, :, :HALF]
        upper_rows = self.weight.at[HALF_CHIPS:]

        @pl.when(self.core == 0)
        def _():
            act(self.across(lower_rows), self.across(upper_rows))

        @pl.when(self.core == 1)
        def _():
            act(self.across(upper_rows), self.across(lower_rows))

    def walk(self, act, wait):
        @pl.when(self.source)
        def _():
            self.own_sends(act, wait)
            self.row_sends(act, wait)

        self.weight_hop(act, wait, 1)
        self.lower_hop(act, wait, 1, 0)
        self.weight_hop(act, wait, 2)
        self.lower_hop(act, wait, 1, 1)
        self.weight_hop(act, wait, 3)
        self.lower_hop(act, wait, 2, 0)
        self.weight_hop(act, wait, 4)
        self.lower_hop(act, wait, 2, 1)
        self.lower_hop(act, wait, 3, 0)
        self.lower_hop(act, wait, 3, 1)

    def run(self, arrived):
        self.walk(lambda copy: copy.start(), True)
        self.weight_across()
        arrived()
        self.lower_hop(None, True, 4, 0)
        self.lower_hop(None, True, 4, 1)

    def finish(self):
        self.walk(lambda copy: copy.wait_send(), False)


class PlainRing(Ring):
    def __init__(self, held, sems, p, y, x, core, place, source):
        super().__init__(held, held, sems + (None,), p, y, x, core, place, source)

    def block(self, slot, kind, core):
        return self.lower.at[slot, :, HALF * kind:HALF * (kind + 1)]

    def weights(self, act):
        act(1)

    def spread(self, act, slot, kind, first):
        for way in (1, 3, 2):
            act(self.along_x(slot, kind, way))

    def weight_across(self):
        for s in range(4):
            for way in (1, 3, 2):
                self.arrived(s * 4 + (self.x + way) % 4, 1)


def chain(
    flag_ref, weight_hbm, lower_hbm, end_hbm, sigma_ref, cross_ref,
    weight_rows, lower_rows, end_ref, weight_ref, lower_ref, coupled_ref,
    through_ref, through_in, through_out, first_sigma,
    rows_there, rows_here, gram_buf, end_buf, next_buf, next_out,
    part_out, part_in, part2_out, part2_in, pack, recv, rows_out,
    load_sem, here_sem, ring_send, ring_recv, across_sem,
    through_recv, through_sem, through_hop, ahead_sem,
    end_sem, next_sem, part_sem, part2_sem, rows_sem, pack_sem,
):
    parts = 8
    p = lax.axis_index("tm")
    r = lax.axis_index("rows")
    chip, core = r // 2, r % 2
    half = chip // HALF_CHIPS
    place = chip % HALF_CHIPS
    y, x = chip // 4, chip % 4
    source_core = core == half
    sibling = (p, chip * 2 + 1 - core)

    def peer(j):
        return (p, (core * HALF_CHIPS + j) * 2 + half)

    loads = [
        pltpu.make_async_copy(src, dst, load_sem.at[k])
        for k, (src, dst) in enumerate(
            ((lower_hbm, lower_rows), (weight_hbm, weight_rows), (end_hbm, end_ref)))
    ]
    for load in loads:
        load.start()
    barrier = pltpu.get_barrier_semaphore()
    pl.semaphore_signal(barrier, 1, device_id=sibling, device_id_type=MESH)

    @pl.when(p > 0)
    def _():
        pl.semaphore_signal(barrier, 1, device_id=(p - 1, r), device_id_type=MESH)

    @pl.when(p < parts - 1)
    def _():
        pl.semaphore_signal(barrier, 1, device_id=(p + 1, r), device_id_type=MESH)

    def is_self(j):
        return jnp.logical_and(core == half, place == j)

    for around in (1, 7):
        there = ((y + around) % 8) * 4 + x
        pl.semaphore_signal(
            barrier, 1, device_id=(p, there * 2 + core), device_id_type=MESH)
    for around in (1, 2, 3):
        there = y * 4 + (x + around) % 4
        pl.semaphore_signal(
            barrier, 1, device_id=(p, there * 2 + core), device_id_type=MESH)

    @pl.when(p < SPLIT - 1)
    def _():
        pl.semaphore_signal(barrier, 1, device_id=(SPLIT, r), device_id_type=MESH)

    expected = (
        6 + jnp.where(p > 0, 1, 0) + jnp.where(p < parts - 1, 1, 0)
        + jnp.where(p == SPLIT, SPLIT - 1, 0))
    weight_ref[:HALF_CHIPS, :, HALF:] = jnp.zeros((HALF_CHIPS, PANEL, HALF), BF16)
    for load in loads:
        load.wait()
    rows_here[0] = lower_rows[...].astype(F32)
    rows_here[1] = weight_rows[...].astype(F32)
    pl.semaphore_wait(barrier, expected)

    mine = pl.ds(pl.multiple_of(core * HALF, 128), HALF)
    theirs = pl.ds(pl.multiple_of((1 - core) * HALF, 128), HALF)
    my_rows = pl.ds(pl.multiple_of(core * OWN, 8), OWN)
    their_rows = pl.ds(pl.multiple_of((1 - core) * OWN, 8), OWN)

    def to_sibling(src, dst, sems):
        return pltpu.make_async_remote_copy(
            src_ref=src, dst_ref=dst, send_sem=sems.at[0], recv_sem=sems.at[1],
            device_id=sibling, device_id_type=MESH)

    here_copy = to_sibling(rows_here, rows_there, here_sem)

    @pl.when(jnp.logical_not(source_core))
    def _():
        here_copy.start()

    end_copy = to_sibling(end_ref.at[:, theirs], end_buf.at[my_rows], end_sem)
    end_copy.start()
    end_buf[my_rows] = end_ref[:, mine]
    ring = Ring(
        lower_ref, weight_ref, (ring_send, ring_recv, across_sem),
        p, y, x, core, place, source_core)

    @pl.when(source_core)
    def _():
        here_copy.wait_recv()
        for which, there in ((0, rows_there[0]), (1, rows_there[1])):
            ours = rows_here[which]
            low = jnp.where(core == 0, ours, there)
            high = jnp.where(core == 0, there, ours)
            both = jnp.concatenate([low, high], axis=0).astype(BF16)
            if which == 0:
                lower_ref[place] = both
            else:
                weight_ref[chip] = both

    def couple(s):
        rows = pl.ds(4 * s, 4)
        left = lower_ref[rows, :, :HALF].reshape(4 * PANEL, HALF)
        right = lower_ref[rows, :, HALF:].reshape(4 * PANEL, HALF)
        for k in range(B // WINDOW):
            columns = slice(WINDOW * k, WINDOW * (k + 1))
            total = dot(right, weight_ref[HALF_CHIPS:, :, columns].reshape(HALF, WINDOW))
            if k < HALF // WINDOW:
                total = total + dot(
                    left, weight_ref[:HALF_CHIPS, :, columns].reshape(HALF, WINDOW))
            coupled_ref[rows, :, columns] = total.astype(BF16).reshape(4, PANEL, WINDOW)

    def couple_near():
        ring.both_ways(lambda ours, others: others.wait_recv())

        @pl.loop(1, 4)
        def _(i):
            couple((y + i) % 4)

    ring.run(couple_near)
    couple(y % 4)
    ring.both_ways(lambda ours, others: ours.wait_send())
    ring.finish()
    end_copy.wait_recv()
    end_b = end_buf[...].astype(BF16)
    broken = flag_ref[p] == 1
    early = p < SPLIT

    def down(src, dst, send, receive, target):
        return pltpu.make_async_remote_copy(
            src_ref=src, dst_ref=dst, send_sem=send, recv_sem=receive,
            device_id=(target, r), device_id_type=MESH)

    below = jnp.maximum(p - 1, 0)
    hops = [
        down(next_out.at[0], next_buf.at[0], next_sem.at[0, 0], next_sem.at[0, 1], below),
        None,
        down(next_out.at[1], next_buf.at[2], next_sem.at[2, 0], next_sem.at[2, 1], below),
    ]
    jumps = [
        down(next_out.at[0], next_buf.at[1], ahead_sem.at[q], next_sem.at[1, 1], q)
        for q in range(SPLIT)
    ]
    through_copy = down(
        through_out, through_in, through_hop.at[0], through_hop.at[1], below)

    def sum_halves(k, source, right_ref):
        copy = to_sibling(part_out.at[k], part_in.at[k], part_sem.at[k])
        part_out[k] = dot(source, right_ref[:, :, theirs].reshape(HALF, HALF))
        copy.start()
        own = dot(source, right_ref[:, :, mine].reshape(HALF, HALF))
        copy.wait_recv()
        return own + part_in[k]

    def pack_copy(k, j):
        return pltpu.make_async_remote_copy(
            src_ref=pack.at[k, j], dst_ref=recv.at[k, place], send_sem=pack_sem.at[k, 0],
            recv_sem=pack_sem.at[k, 1], device_id=peer(j), device_id_type=MESH)

    def messages(k, act):
        def count(n):
            return pltpu.make_async_remote_copy(
                src_ref=pack.at[k, :n], dst_ref=recv.at[k, :n], send_sem=pack_sem.at[k, 0],
                recv_sem=pack_sem.at[k, 1], device_id=sibling, device_id_type=MESH)

        @pl.when(source_core)
        def _():
            act(count(HALF_CHIPS - 1))

        @pl.when(jnp.logical_not(source_core))
        def _():
            act(count(HALF_CHIPS))

    def emit(which, value, out_ref, act):
        copy = to_sibling(
            rows_out.at[which, their_rows], out_ref.at[:, mine], rows_sem.at[which])
        if act == "start":
            rows_out[which] = value
            copy.start()
            out_ref[:, mine] = rows_out[which, my_rows]
        else:
            copy.wait()

    def step(k, source, right_ref, meanwhile):
        product = sum_halves(k, source, right_ref)
        for j in range(HALF_CHIPS):
            pack[k, j] = message(product, j)

            @pl.when(jnp.logical_not(is_self(j)))
            def _():
                pack_copy(k, j).start()

            @pl.when(is_self(j))
            def _():
                recv[k, j] = pack[k, j]

        base = meanwhile(product)
        messages(k, lambda copy: copy.wait_recv())
        first = recv[k, :, :16].reshape(HALF_CHIPS * 16, 128).T
        second = recv[k, :, 16:].reshape(HALF_CHIPS * 16, 128).T

        def update(columns):
            def rows(i):
                return right_ref[:, 16 * i:16 * i + 16, columns].reshape(HALF_CHIPS * 16, HALF)
            total = dot(first[:48], rows(0)) + dot(first[64:112], rows(1))
            total = total + dot(second[:48], rows(2))
            return total if base is None else total + base(columns)

        copy = to_sibling(part2_out.at[k], part2_in.at[k], part2_sem.at[k])
        part2_out[k] = update(theirs)
        copy.start()
        sigma = update(mine)
        copy.wait_recv()
        return sigma + part2_in[k]

    through_ring = PlainRing(
        through_ref, (ring_send, through_recv), p, y, x, core, place, source_core)
    through_half = to_sibling(through_out, through_out, through_sem.at[0])
    through_here = to_sibling(through_out, through_ref.at[place, :, mine], through_sem.at[1])
    zero = jnp.zeros((PANEL, HALF), BF16)

    @pl.when(p == SPLIT - 1)
    def _():
        @pl.when(source_core)
        def _():
            next_out[1] = jnp.where(broken, zero, coupled_ref[place, :, theirs])
            half_copy = to_sibling(next_out.at[1], through_out, through_sem.at[0])
            half_copy.start()
            through_out[...] = jnp.where(broken, zero, coupled_ref[place, :, mine])
            half_copy.wait_send()

        @pl.when(jnp.logical_not(source_core))
        def _():
            through_half.wait_recv()

        through_copy.start()

        @pl.loop(0, HALF_CHIPS)
        def _(j):
            rows = coupled_ref[j]
            through_ref[j] = jnp.where(broken, jnp.zeros_like(rows), rows)

    @pl.when(p < SPLIT - 1)
    def _():
        through_copy.wait_recv()
        rows = sum_halves(2, through_in[...], coupled_ref).astype(BF16)
        through_out[...] = jnp.where(broken, zero, rows)

        @pl.when(p > 0)
        def _():
            through_copy.start()

        @pl.when(source_core)
        def _():
            through_ref[place, :, mine] = through_out[...]

        @pl.when(jnp.logical_not(source_core))
        def _():
            through_here.start()

    def gather_through():
        @pl.when(source_core)
        def _():
            to_sibling(through_out, through_ref.at[place, :, theirs], through_sem.at[1]).wait_recv()

        through_ring.run(lambda: None)

    @pl.when(p < SPLIT - 2)
    def _():
        gather_through()

    has_above = jnp.logical_and(p != parts - 1, p != SPLIT - 1)

    @pl.when(has_above)
    def _():
        hops[0].wait_recv()

    @pl.when(jnp.logical_not(has_above))
    def _():
        next_buf[0] = zero

    use_end = jnp.logical_or(broken, p == parts - 1)

    def gram(product):
        window = jnp.minimum(chip * PANEL // 128, (B - WINDOW) // 128) * 128
        chips = pl.ds(core * HALF_CHIPS, HALF_CHIPS)
        own = weight_ref[chips, :, pl.ds(pl.multiple_of(window, 128), WINDOW)]
        own = own.reshape(HALF, WINDOW).T
        for k in range(B // WINDOW):
            columns = slice(WINDOW * k, WINDOW * (k + 1))
            gram_buf[:, columns] = dot(own, weight_ref[chips, :, columns].reshape(HALF, WINDOW))
        gram_rows = pl.ds(pl.multiple_of(chip * PANEL - window, 16), PANEL)

        @pl.when(jnp.logical_not(early))
        def _():
            emit(0, -product, cross_ref, "start")

        return lambda columns: gram_buf[gram_rows, columns]

    sigma = step(0, jnp.where(use_end, end_b, next_buf[0]), coupled_ref, gram)
    next_out[0] = sigma.astype(BF16)
    sends_down = jnp.logical_and(p > 0, p != SPLIT)

    @pl.when(sends_down)
    def _():
        hops[0].start()

    @pl.when(p == SPLIT)
    def _():
        for jump in jumps:
            jump.start()

    @pl.when(jnp.logical_not(early))
    def _():
        emit(1, sigma, sigma_ref, "start")

    @pl.when(early)
    def _():
        first_sigma[...] = sigma

        @pl.when(p == SPLIT - 2)
        def _():
            gather_through()

        jumps[0].wait_recv()
        whole = first_sigma[...] + step(1, next_buf[1], through_ref, lambda product: None)
        next_out[1] = whole.astype(BF16)

        @pl.when(p > 0)
        def _():
            hops[2].start()

        emit(1, whole, sigma_ref, "start")

        @pl.when(p < SPLIT - 1)
        def _():
            hops[2].wait_recv()

        @pl.when(p == SPLIT - 1)
        def _():
            next_buf[2] = next_buf[1]

        source = jnp.where(broken, end_b, next_buf[2])
        emit(0, -sum_halves(3, source, coupled_ref), cross_ref, "start")

    end_copy.wait_send()

    @pl.when(jnp.logical_not(source_core))
    def _():
        here_copy.wait_send()

    def sent(k):
        to_sibling(part_out.at[k], part_in.at[k], part_sem.at[k]).wait_send()

    def step_sent(k):
        sent(k)
        to_sibling(part2_out.at[k], part2_in.at[k], part2_sem.at[k]).wait_send()
        messages(k, lambda copy: copy.wait_send())

    step_sent(0)

    @pl.when(sends_down)
    def _():
        hops[0].wait_send()

    @pl.when(p == SPLIT)
    def _():
        for jump in jumps:
            jump.wait_send()

    @pl.when(early)
    def _():
        step_sent(1)
        sent(3)

        @pl.when(p > 0)
        def _():
            through_copy.wait_send()
            hops[2].wait_send()

    @pl.when(p < SPLIT - 1)
    def _():
        sent(2)
        through_ring.finish()

        @pl.when(jnp.logical_not(source_core))
        def _():
            through_here.wait_send()

    emit(0, None, cross_ref, "wait")
    emit(1, None, sigma_ref, "wait")


def run_chain(flag, weight, lower, end):
    vmem = pl.BlockSpec(memory_space=pltpu.VMEM)
    dma = pltpu.SemaphoreType.DMA
    return pl.pallas_call(
        chain,
        out_shape=[jax.ShapeDtypeStruct((OWN, B), F32)] * 2,
        in_specs=[pl.BlockSpec(memory_space=pltpu.SMEM)] + [pl.BlockSpec(memory_space=pl.ANY)] * 3,
        out_specs=[vmem, vmem],
        scratch_shapes=[
            pltpu.VMEM((OWN, B), BF16),
            pltpu.VMEM((OWN, B), BF16),
            pltpu.VMEM((OWN, B), F32),
            pltpu.VMEM((CHIPS, PANEL, B), BF16),
            pltpu.VMEM((HALF_CHIPS, PANEL, B), BF16),
            pltpu.VMEM((HALF_CHIPS, PANEL, B), BF16),
            pltpu.VMEM((HALF_CHIPS, PANEL, B), BF16),
            pltpu.VMEM((PANEL, HALF), BF16),
            pltpu.VMEM((PANEL, HALF), BF16),
            pltpu.VMEM((PANEL, HALF), F32),
            pltpu.VMEM((2, OWN, B), F32),
            pltpu.VMEM((2, OWN, B), F32),
            pltpu.VMEM((WINDOW, B), F32),
            pltpu.VMEM((PANEL, HALF), F32),
            pltpu.VMEM((3, PANEL, HALF), BF16),
            pltpu.VMEM((2, PANEL, HALF), BF16),
            pltpu.VMEM((4, PANEL, HALF), F32),
            pltpu.VMEM((4, PANEL, HALF), F32),
            pltpu.VMEM((2, PANEL, HALF), F32),
            pltpu.VMEM((2, PANEL, HALF), F32),
            pltpu.VMEM((2, HALF_CHIPS, 32, 128), BF16),
            pltpu.VMEM((2, HALF_CHIPS, 32, 128), BF16),
            pltpu.VMEM((2, PANEL, HALF), F32),
            dma((3,)), dma((2,)), dma((75,)), dma((HALF_CHIPS, 3)), dma((2,)),
            dma((HALF_CHIPS, 2)), dma((2, 2)), dma((2,)), dma((SPLIT,)),
            dma((2,)), dma((3, 2)), dma((4, 2)), dma((2, 2)), dma((2, 2)), dma((2, 2)),
        ],
        compiler_params=pltpu.CompilerParams(
            collective_id=0, has_side_effects=True, vmem_limit_bytes=40 * 1024 * 1024),
    )(flag, weight, lower, end)


def shards(w_inv, lower_block, sigma_end, chain_break):
    sigma, cross = run_chain(chain_break, w_inv[0], lower_block[0], sigma_end)
    return (sigma[None], cross[None])


def solution(mesh):
    in_specs = (P("tm", "rows", None), P("tm", "rows", None), P("rows", None), P())
    out_specs = (P("tm", "rows", None), P("tm", "rows", None))
    return jax.shard_map(shards, mesh=mesh, in_specs=in_specs, out_specs=out_specs, check_vma=False)
```

```python
import jax
import jax.numpy as jnp
from jax import lax
from jax.experimental import pallas as pl
from jax.experimental.pallas import tpu as pltpu
from jax.sharding import PartitionSpec as P

MESH = pl.DeviceIdType.MESH
BF16 = jnp.bfloat16
F32 = jnp.float32
B = 1536
CHIPS = 32
HALF_CHIPS = 16
PANEL = 48
OWN = 24
HALF = 768
WINDOW = 256
SPLIT = 4


def dot(a, b):
    return jnp.dot(a, b, preferred_element_type=F32)


def message(product, j):
    start = PANEL * j
    tile, off = start // 128, start % 128
    lanes = lax.broadcasted_iota(jnp.int32, (PANEL, 128), 1)
    block = product[:, tile * 128:(tile + 1) * 128]
    if off:
        block = pltpu.roll(block, 128 - off, 1)
        if off + PANEL > 128:
            after = pltpu.roll(product[:, (tile + 1) * 128:(tile + 2) * 128], 128 - off, 1)
            block = jnp.where(lanes < 128 - off, block, after)
    top = jnp.where(lanes[:16] < 64, block[:16], pltpu.roll(block[16:32], 64, 1))
    return jnp.concatenate([top, block[32:48]], axis=0).astype(BF16)


class Ring:
    def __init__(self, lower, weight, sems, p, y, x, core, place, source):
        self.lower, self.weight = lower, weight
        self.sends, self.receives, self.over = sems
        self.p, self.y, self.x, self.core = p, y, x, core
        self.place, self.source = place, source
        self.sign = 1 - 2 * core

    def block(self, slot, kind, core):
        if kind == 0:
            return self.lower.at[slot]
        return self.weight.at[HALF_CHIPS * core + slot, :, HALF * (kind - 1):HALF * kind]

    def copy(self, slot, kind, way, y, x):
        block = self.block(slot, kind, self.core)
        return pltpu.make_async_remote_copy(
            src_ref=block, dst_ref=block, send_sem=self.sends.at[self.sender(slot, kind, way)],
            recv_sem=self.receives.at[slot, kind],
            device_id=(self.p, (y * 4 + x) * 2 + self.core), device_id_type=MESH)

    def sender(self, slot, kind, way):
        if kind:
            return 35 + 20 * (kind - 1) + 5 * (slot // 4) + way
        return 2 * slot + way if way < 2 else 30 + way

    def along_x(self, slot, kind, way):
        return self.copy(slot, kind, 1 + way, self.y, (self.x + way) % 4)

    def along_y(self, slot, kind, back):
        step = self.turn(slot, kind) * (-1 if back else 1)
        return self.copy(slot, kind, back, (self.y + step + 8) % 8, self.x)

    def turn(self, slot, kind):
        return self.sign * (1 - 2 * (slot % 2)) if kind == 0 else self.sign

    def across(self, block):
        chip = self.y * 4 + self.x
        return pltpu.make_async_remote_copy(
            src_ref=block, dst_ref=block, send_sem=self.over.at[0], recv_sem=self.over.at[1],
            device_id=(self.p, chip * 2 + 1 - self.core), device_id_type=MESH)

    def arrived(self, slot, kind):
        self.along_x(slot, kind, 1).wait_recv()

    def weights(self, act):
        act(1)

        @pl.when(self.core == 1)
        def _():
            act(2)

    def columns(self):
        return [(self.x + i) % 4 for i in (0, 1, 3, 2)]

    def spread(self, act, slot, kind, first):
        for way in (1, 3, 2):
            act(self.along_x(slot, kind, way))
        if kind and first:
            self.across(self.block(slot, kind, self.core)).start()

    def own_sends(self, act, first):
        def round_y(kind):
            act(self.along_y(self.place, kind, 0))
            act(self.along_y(self.place, kind, 1))

        self.spread(act, self.place, 0, first)
        self.weights(round_y)
        round_y(0)
        self.weights(lambda kind: self.spread(act, self.place, kind, first))

    def row_sends(self, act, wait):
        for column in self.columns()[1:]:
            slot = (self.y % 4) * 4 + column
            if wait:
                self.arrived(slot, 0)
            act(self.along_y(slot, 0, 0))
            act(self.along_y(slot, 0, 1))

    def lower_hop(self, act, wait, distance, pair):
        columns = [(self.x + pair) % 4, (self.x + pair + 2) % 4]
        for back in range(2 if distance < 4 else 1):
            step = self.turn(columns[0], 0) * distance * (1 if back else -1)
            origin = (self.y + step + 8) % 8

            @pl.when(origin // 4 == self.core)
            def _():
                for column in columns:
                    slot = (origin % 4) * 4 + column
                    if wait:
                        self.arrived(slot, 0)
                    if distance < (3 if back else 4):
                        act(self.along_y(slot, 0, back))

    def weight_hop(self, act, wait, distance):
        for back in range(2 if distance < 4 else 1):
            origin = (self.y + self.sign * distance * (1 if back else -1) + 8) % 8

            @pl.when(origin // 4 == self.core)
            def _():
                slot = (origin % 4) * 4 + self.x

                def pass_on(kind):
                    if wait:
                        self.arrived(slot, kind)
                    if distance < (3 if back else 4):
                        act(self.along_y(slot, kind, back))
                    self.spread(act, slot, kind, wait)

                self.weights(pass_on)

    def weight_across(self):
        for s in range(4):
            for way in (1, 3, 2):
                slot = s * 4 + (self.x + way) % 4

                def to_sibling(kind):
                    self.arrived(slot, kind)
                    self.across(self.block(slot, kind, self.core)).start()

                self.weights(to_sibling)

    def both_ways(self, act):
        lower_rows = self.weight.at[:HALF_CHIPS, :, :HALF]
        upper_rows = self.weight.at[HALF_CHIPS:]

        @pl.when(self.core == 0)
        def _():
            act(self.across(lower_rows), self.across(upper_rows))

        @pl.when(self.core == 1)
        def _():
            act(self.across(upper_rows), self.across(lower_rows))

    def walk(self, act, wait):
        @pl.when(self.source)
        def _():
            self.own_sends(act, wait)
            self.row_sends(act, wait)

        self.weight_hop(act, wait, 1)
        self.weight_hop(act, wait, 2)
        self.lower_hop(act, wait, 1, 0)
        self.lower_hop(act, wait, 1, 1)
        self.weight_hop(act, wait, 3)
        self.lower_hop(act, wait, 2, 0)
        self.lower_hop(act, wait, 2, 1)
        self.weight_hop(act, wait, 4)
        self.lower_hop(act, wait, 3, 0)
        self.lower_hop(act, wait, 3, 1)

    def run(self, arrived):
        self.walk(lambda copy: copy.start(), True)
        self.weight_across()
        arrived()
        self.lower_hop(None, True, 4, 0)
        self.lower_hop(None, True, 4, 1)

    def finish(self):
        self.walk(lambda copy: copy.wait_send(), False)


class PlainRing(Ring):
    def __init__(self, held, sems, p, y, x, core, place, source):
        super().__init__(held, held, sems + (None,), p, y, x, core, place, source)

    def block(self, slot, kind, core):
        return self.lower.at[slot, :, HALF * kind:HALF * (kind + 1)]

    def weights(self, act):
        act(1)

    def spread(self, act, slot, kind, first):
        for way in (1, 3, 2):
            act(self.along_x(slot, kind, way))

    def weight_across(self):
        for s in range(4):
            for way in (1, 3, 2):
                self.arrived(s * 4 + (self.x + way) % 4, 1)


def chain(
    flag_ref, weight_hbm, lower_hbm, end_hbm, sigma_ref, cross_ref,
    weight_rows, lower_rows, end_ref, weight_ref, lower_ref, coupled_ref,
    through_ref, through_in, through_out, first_sigma, cross_part, cross_in,
    rows_there, rows_here, gram_buf, end_buf, next_buf, next_out,
    part_out, part_in, part2_out, part2_in, pack, recv, rows_out,
    load_sem, here_sem, ring_send, ring_recv, across_sem,
    through_recv, through_sem, through_hop, ahead_sem,
    end_sem, next_sem, part_sem, part2_sem, rows_sem, pack_sem,
):
    parts = 8
    p = lax.axis_index("tm")
    r = lax.axis_index("rows")
    chip, core = r // 2, r % 2
    half = chip // HALF_CHIPS
    place = chip % HALF_CHIPS
    y, x = chip // 4, chip % 4
    source_core = core == half
    sibling = (p, chip * 2 + 1 - core)

    def peer(j):
        return (p, (core * HALF_CHIPS + j) * 2 + half)

    loads = [
        pltpu.make_async_copy(src, dst, load_sem.at[k])
        for k, (src, dst) in enumerate(
            ((lower_hbm, lower_rows), (weight_hbm, weight_rows), (end_hbm, end_ref)))
    ]
    for load in loads:
        load.start()
    barrier = pltpu.get_barrier_semaphore()
    pl.semaphore_signal(barrier, 1, device_id=sibling, device_id_type=MESH)

    @pl.when(p > 0)
    def _():
        pl.semaphore_signal(barrier, 1, device_id=(p - 1, r), device_id_type=MESH)

    @pl.when(p < parts - 1)
    def _():
        pl.semaphore_signal(barrier, 1, device_id=(p + 1, r), device_id_type=MESH)

    def is_self(j):
        return jnp.logical_and(core == half, place == j)

    for around in (1, 7):
        there = ((y + around) % 8) * 4 + x
        pl.semaphore_signal(
            barrier, 1, device_id=(p, there * 2 + core), device_id_type=MESH)
    for around in (1, 2, 3):
        there = y * 4 + (x + around) % 4
        pl.semaphore_signal(
            barrier, 1, device_id=(p, there * 2 + core), device_id_type=MESH)

    @pl.when(p < SPLIT - 1)
    def _():
        pl.semaphore_signal(barrier, 1, device_id=(SPLIT, r), device_id_type=MESH)

    expected = (
        6 + jnp.where(p > 0, 1, 0) + jnp.where(p < parts - 1, 1, 0)
        + jnp.where(p == SPLIT, SPLIT - 1, 0))
    weight_ref[:HALF_CHIPS, :, HALF:] = jnp.zeros((HALF_CHIPS, PANEL, HALF), BF16)
    for load in loads:
        load.wait()
    rows_here[0] = lower_rows[...].astype(F32)
    rows_here[1] = weight_rows[...].astype(F32)
    pl.semaphore_wait(barrier, expected)

    mine = pl.ds(pl.multiple_of(core * HALF, 128), HALF)
    theirs = pl.ds(pl.multiple_of((1 - core) * HALF, 128), HALF)
    my_rows = pl.ds(pl.multiple_of(core * OWN, 8), OWN)
    their_rows = pl.ds(pl.multiple_of((1 - core) * OWN, 8), OWN)

    def to_sibling(src, dst, sems):
        return pltpu.make_async_remote_copy(
            src_ref=src, dst_ref=dst, send_sem=sems.at[0], recv_sem=sems.at[1],
            device_id=sibling, device_id_type=MESH)

    here_copy = to_sibling(rows_here, rows_there, here_sem)

    @pl.when(jnp.logical_not(source_core))
    def _():
        here_copy.start()

    end_copy = to_sibling(end_ref.at[:, theirs], end_buf.at[my_rows], end_sem)
    end_copy.start()
    end_buf[my_rows] = end_ref[:, mine]
    ring = Ring(
        lower_ref, weight_ref, (ring_send, ring_recv, across_sem),
        p, y, x, core, place, source_core)

    @pl.when(source_core)
    def _():
        here_copy.wait_recv()
        for which, there in ((0, rows_there[0]), (1, rows_there[1])):
            ours = rows_here[which]
            low = jnp.where(core == 0, ours, there)
            high = jnp.where(core == 0, there, ours)
            both = jnp.concatenate([low, high], axis=0).astype(BF16)
            if which == 0:
                lower_ref[place] = both
            else:
                weight_ref[chip] = both

    def couple(s):
        rows = pl.ds(4 * s, 4)
        left = lower_ref[rows, :, :HALF].reshape(4 * PANEL, HALF)
        right = lower_ref[rows, :, HALF:].reshape(4 * PANEL, HALF)
        for k in range(B // WINDOW):
            columns = slice(WINDOW * k, WINDOW * (k + 1))
            total = dot(right, weight_ref[HALF_CHIPS:, :, columns].reshape(HALF, WINDOW))
            if k < HALF // WINDOW:
                total = total + dot(
                    left, weight_ref[:HALF_CHIPS, :, columns].reshape(HALF, WINDOW))
            coupled_ref[rows, :, columns] = total.astype(BF16).reshape(4, PANEL, WINDOW)

    def couple_near():
        ring.both_ways(lambda ours, others: others.wait_recv())

        @pl.loop(1, 4)
        def _(i):
            couple((y + i) % 4)

    ring.run(couple_near)
    couple(y % 4)
    ring.both_ways(lambda ours, others: ours.wait_send())
    ring.finish()
    end_copy.wait_recv()
    end_b = end_buf[...].astype(BF16)
    broken = flag_ref[p] == 1
    early = p < SPLIT

    def down(src, dst, send, receive, target):
        return pltpu.make_async_remote_copy(
            src_ref=src, dst_ref=dst, send_sem=send, recv_sem=receive,
            device_id=(target, r), device_id_type=MESH)

    below = jnp.maximum(p - 1, 0)
    hops = [
        down(next_out.at[0], next_buf.at[0], next_sem.at[0, 0], next_sem.at[0, 1], below),
        None,
        down(next_out.at[1], next_buf.at[2], next_sem.at[2, 0], next_sem.at[2, 1], below),
    ]
    jumps = [
        down(next_out.at[0], next_buf.at[1], ahead_sem.at[q], next_sem.at[1, 1], q)
        for q in range(SPLIT)
    ]
    through_copy = down(
        through_out, through_in, through_hop.at[0], through_hop.at[1], below)

    def sum_halves(k, source, right_ref):
        copy = to_sibling(part_out.at[k], part_in.at[k], part_sem.at[k])
        part_out[k] = dot(source, right_ref[:, :, theirs].reshape(HALF, HALF))
        copy.start()
        own = dot(source, right_ref[:, :, mine].reshape(HALF, HALF))
        copy.wait_recv()
        return own + part_in[k]

    def pack_copy(k, j):
        return pltpu.make_async_remote_copy(
            src_ref=pack.at[k, j], dst_ref=recv.at[k, place], send_sem=pack_sem.at[k, 0],
            recv_sem=pack_sem.at[k, 1], device_id=peer(j), device_id_type=MESH)

    def messages(k, act):
        def count(n):
            return pltpu.make_async_remote_copy(
                src_ref=pack.at[k, :n], dst_ref=recv.at[k, :n], send_sem=pack_sem.at[k, 0],
                recv_sem=pack_sem.at[k, 1], device_id=sibling, device_id_type=MESH)

        @pl.when(source_core)
        def _():
            act(count(HALF_CHIPS - 1))

        @pl.when(jnp.logical_not(source_core))
        def _():
            act(count(HALF_CHIPS))

    def emit(which, value, out_ref, act):
        copy = to_sibling(
            rows_out.at[which, their_rows], out_ref.at[:, mine], rows_sem.at[which])
        if act == "start":
            rows_out[which] = value
            copy.start()
            out_ref[:, mine] = rows_out[which, my_rows]
        else:
            copy.wait()

    def step(k, source, right_ref, meanwhile):
        product = sum_halves(k, source, right_ref)
        for j in range(HALF_CHIPS):
            pack[k, j] = message(product, j)

        for j in range(HALF_CHIPS):
            @pl.when(jnp.logical_not(is_self(j)))
            def _():
                pack_copy(k, j).start()

        @pl.when(source_core)
        def _():
            recv[k, place] = pack[k, place]

        base = meanwhile(product)
        messages(k, lambda copy: copy.wait_recv())
        first = recv[k, :, :16].reshape(HALF_CHIPS * 16, 128).T
        second = recv[k, :, 16:].reshape(HALF_CHIPS * 16, 128).T

        def update(columns):
            def rows(i):
                return right_ref[:, 16 * i:16 * i + 16, columns].reshape(HALF_CHIPS * 16, HALF)
            total = dot(first[:48], rows(0)) + dot(first[64:112], rows(1))
            total = total + dot(second[:48], rows(2))
            return total if base is None else total + base(columns)

        copy = to_sibling(part2_out.at[k], part2_in.at[k], part2_sem.at[k])
        part2_out[k] = update(theirs)
        copy.start()
        sigma = update(mine)
        copy.wait_recv()
        return sigma + part2_in[k]

    through_ring = PlainRing(
        through_ref, (ring_send, through_recv), p, y, x, core, place, source_core)
    through_half = to_sibling(through_out, through_out, through_sem.at[0])
    through_here = to_sibling(through_out, through_ref.at[place, :, mine], through_sem.at[1])
    zero = jnp.zeros((PANEL, HALF), BF16)

    @pl.when(p == SPLIT - 1)
    def _():
        @pl.when(source_core)
        def _():
            next_out[1] = jnp.where(broken, zero, coupled_ref[place, :, theirs])
            half_copy = to_sibling(next_out.at[1], through_out, through_sem.at[0])
            half_copy.start()
            through_out[...] = jnp.where(broken, zero, coupled_ref[place, :, mine])
            half_copy.wait_send()

        @pl.when(jnp.logical_not(source_core))
        def _():
            through_half.wait_recv()

        through_copy.start()

        @pl.loop(0, HALF_CHIPS)
        def _(j):
            rows = coupled_ref[j]
            through_ref[j] = jnp.where(broken, jnp.zeros_like(rows), rows)

    @pl.when(p < SPLIT - 1)
    def _():
        through_copy.wait_recv()
        rows = sum_halves(2, through_in[...], coupled_ref).astype(BF16)
        through_out[...] = jnp.where(broken, zero, rows)

        @pl.when(p > 0)
        def _():
            through_copy.start()

        @pl.when(source_core)
        def _():
            through_ref[place, :, mine] = through_out[...]

        @pl.when(jnp.logical_not(source_core))
        def _():
            through_here.start()

    def gather_through():
        @pl.when(source_core)
        def _():
            to_sibling(through_out, through_ref.at[place, :, theirs], through_sem.at[1]).wait_recv()

        through_ring.run(lambda: None)

    @pl.when(p < SPLIT - 2)
    def _():
        gather_through()

    has_above = jnp.logical_and(p != parts - 1, p != SPLIT - 1)

    @pl.when(has_above)
    def _():
        hops[0].wait_recv()

    @pl.when(jnp.logical_not(has_above))
    def _():
        next_buf[0] = zero

    use_end = jnp.logical_or(broken, p == parts - 1)

    def gram(product):
        window = jnp.minimum(chip * PANEL // 128, (B - WINDOW) // 128) * 128
        chips = pl.ds(core * HALF_CHIPS, HALF_CHIPS)
        own = weight_ref[chips, :, pl.ds(pl.multiple_of(window, 128), WINDOW)]
        own = own.reshape(HALF, WINDOW).T
        for k in range(B // WINDOW):
            columns = slice(WINDOW * k, WINDOW * (k + 1))
            gram_buf[:, columns] = dot(own, weight_ref[chips, :, columns].reshape(HALF, WINDOW))
        gram_rows = pl.ds(pl.multiple_of(chip * PANEL - window, 16), PANEL)

        @pl.when(jnp.logical_not(early))
        def _():
            emit(0, -product, cross_ref, "start")

        return lambda columns: gram_buf[gram_rows, columns]

    sigma = step(0, jnp.where(use_end, end_b, next_buf[0]), coupled_ref, gram)
    next_out[0] = sigma.astype(BF16)
    sends_down = jnp.logical_and(p > 0, p != SPLIT)

    @pl.when(sends_down)
    def _():
        hops[0].start()

    @pl.when(p == SPLIT)
    def _():
        for q in (1, 2, 3, 0):
            jumps[q].start()

    @pl.when(jnp.logical_not(early))
    def _():
        emit(1, sigma, sigma_ref, "start")

    @pl.when(early)
    def _():
        first_sigma[...] = sigma

        @pl.when(p == SPLIT - 2)
        def _():
            gather_through()

        jumps[0].wait_recv()
        whole = first_sigma[...] + step(1, next_buf[1], through_ref, lambda product: None)
        next_out[1] = whole.astype(BF16)

        @pl.when(p > 0)
        def _():
            hops[2].start()

        emit(1, whole, sigma_ref, "start")

        @pl.when(p < SPLIT - 1)
        def _():
            hops[2].wait_recv()

        @pl.when(p == SPLIT - 1)
        def _():
            next_buf[2] = next_buf[1]

        source = jnp.where(broken, end_b, next_buf[2])
        for k in range(2):
            columns = slice(HALF * k, HALF * (k + 1))
            cross_part[:, columns] = -dot(
                source, coupled_ref[:, :, columns].reshape(HALF, HALF))
        cross_copy = to_sibling(cross_part.at[their_rows], cross_in, rows_sem.at[0])
        cross_copy.start()
        cross_copy.wait_recv()
        cross_ref[...] = cross_part[my_rows] + cross_in[...]

    end_copy.wait_send()

    @pl.when(jnp.logical_not(source_core))
    def _():
        here_copy.wait_send()

    def sent(k):
        to_sibling(part_out.at[k], part_in.at[k], part_sem.at[k]).wait_send()

    def step_sent(k):
        sent(k)
        to_sibling(part2_out.at[k], part2_in.at[k], part2_sem.at[k]).wait_send()
        messages(k, lambda copy: copy.wait_send())

    step_sent(0)

    @pl.when(sends_down)
    def _():
        hops[0].wait_send()

    @pl.when(p == SPLIT)
    def _():
        for jump in jumps:
            jump.wait_send()

    @pl.when(early)
    def _():
        step_sent(1)
        to_sibling(cross_part.at[their_rows], cross_in, rows_sem.at[0]).wait_send()

        @pl.when(p > 0)
        def _():
            through_copy.wait_send()
            hops[2].wait_send()

    @pl.when(p < SPLIT - 1)
    def _():
        sent(2)
        through_ring.finish()

        @pl.when(jnp.logical_not(source_core))
        def _():
            through_here.wait_send()

    @pl.when(jnp.logical_not(early))
    def _():
        emit(0, None, cross_ref, "wait")

    emit(1, None, sigma_ref, "wait")


def run_chain(flag, weight, lower, end):
    vmem = pl.BlockSpec(memory_space=pltpu.VMEM)
    dma = pltpu.SemaphoreType.DMA
    return pl.pallas_call(
        chain,
        out_shape=[jax.ShapeDtypeStruct((OWN, B), F32)] * 2,
        in_specs=[pl.BlockSpec(memory_space=pltpu.SMEM)] + [pl.BlockSpec(memory_space=pl.ANY)] * 3,
        out_specs=[vmem, vmem],
        scratch_shapes=[
            pltpu.VMEM((OWN, B), BF16),
            pltpu.VMEM((OWN, B), BF16),
            pltpu.VMEM((OWN, B), F32),
            pltpu.VMEM((CHIPS, PANEL, B), BF16),
            pltpu.VMEM((HALF_CHIPS, PANEL, B), BF16),
            pltpu.VMEM((HALF_CHIPS, PANEL, B), BF16),
            pltpu.VMEM((HALF_CHIPS, PANEL, B), BF16),
            pltpu.VMEM((PANEL, HALF), BF16),
            pltpu.VMEM((PANEL, HALF), BF16),
            pltpu.VMEM((PANEL, HALF), F32),
            pltpu.VMEM((PANEL, B), F32),
            pltpu.VMEM((OWN, B), F32),
            pltpu.VMEM((2, OWN, B), F32),
            pltpu.VMEM((2, OWN, B), F32),
            pltpu.VMEM((WINDOW, B), F32),
            pltpu.VMEM((PANEL, HALF), F32),
            pltpu.VMEM((3, PANEL, HALF), BF16),
            pltpu.VMEM((2, PANEL, HALF), BF16),
            pltpu.VMEM((3, PANEL, HALF), F32),
            pltpu.VMEM((3, PANEL, HALF), F32),
            pltpu.VMEM((2, PANEL, HALF), F32),
            pltpu.VMEM((2, PANEL, HALF), F32),
            pltpu.VMEM((2, HALF_CHIPS, 32, 128), BF16),
            pltpu.VMEM((2, HALF_CHIPS, 32, 128), BF16),
            pltpu.VMEM((2, PANEL, HALF), F32),
            dma((3,)), dma((2,)), dma((75,)), dma((HALF_CHIPS, 3)), dma((2,)),
            dma((HALF_CHIPS, 2)), dma((2, 2)), dma((2,)), dma((SPLIT,)),
            dma((2,)), dma((3, 2)), dma((3, 2)), dma((2, 2)), dma((2, 2)), dma((2, 2)),
        ],
        compiler_params=pltpu.CompilerParams(
            collective_id=0, has_side_effects=True, vmem_limit_bytes=40 * 1024 * 1024),
    )(flag, weight, lower, end)


def shards(w_inv, lower_block, sigma_end, chain_break):
    sigma, cross = run_chain(chain_break, w_inv[0], lower_block[0], sigma_end)
    return (sigma[None], cross[None])


def solution(mesh):
    in_specs = (P("tm", "rows", None), P("tm", "rows", None), P("rows", None), P())
    out_specs = (P("tm", "rows", None), P("tm", "rows", None))
    return jax.shard_map(shards, mesh=mesh, in_specs=in_specs, out_specs=out_specs, check_vma=False)
```

```python
import jax
import jax.numpy as jnp
from jax import lax
from jax.experimental import pallas as pl
from jax.experimental.pallas import tpu as pltpu
from jax.sharding import PartitionSpec as P

MESH = pl.DeviceIdType.MESH
BF16 = jnp.bfloat16
F32 = jnp.float32
B = 1536
CHIPS = 32
HALF_CHIPS = 16
PANEL = 48
OWN = 24
HALF = 768
WINDOW = 256
SPLIT = 4
STEP = 384
LEFT = 1152


def dot(a, b):
    return jnp.dot(a, b, preferred_element_type=F32)


def message(product, j):
    start = PANEL * j
    tile, off = start // 128, start % 128
    lanes = lax.broadcasted_iota(jnp.int32, (PANEL, 128), 1)
    block = product[:, tile * 128:(tile + 1) * 128]
    if off:
        block = pltpu.roll(block, 128 - off, 1)
        if off + PANEL > 128:
            after = pltpu.roll(product[:, (tile + 1) * 128:(tile + 2) * 128], 128 - off, 1)
            block = jnp.where(lanes < 128 - off, block, after)
    top = jnp.where(lanes[:16] < 64, block[:16], pltpu.roll(block[16:32], 64, 1))
    return jnp.concatenate([top, block[32:48]], axis=0).astype(BF16)


class Ring:
    later = (1, 2)

    def __init__(self, lower, weight, sems, p, y, x, core, place, source):
        self.lower, self.weight = lower, weight
        self.sends, self.receives, self.over = sems
        self.p, self.y, self.x, self.core = p, y, x, core
        self.place, self.source = place, source
        self.sign = 1 - 2 * core

    def block(self, slot, kind, pair):
        if kind == 1:
            return self.weight.at[HALF_CHIPS * self.core + slot, :, :STEP * (pair + 1)]
        return self.lower.at[slot, :, slice(0, LEFT) if kind == 0 else slice(LEFT, B)]

    def copy(self, slot, kind, pair, way, y, x):
        block = self.block(slot, kind, pair)
        return pltpu.make_async_remote_copy(
            src_ref=block, dst_ref=block, send_sem=self.sends.at[self.sender(slot, kind, way)],
            recv_sem=self.receives.at[slot, kind],
            device_id=(self.p, (y * 4 + x) * 2 + self.core), device_id_type=MESH)

    def sender(self, slot, kind, way):
        if kind:
            return 35 + 20 * (kind - 1) + 5 * (slot // 4) + way
        return 2 * slot + way if way < 2 else 30 + way

    def along_x(self, slot, kind, pair, way):
        return self.copy(slot, kind, pair, 1 + way, self.y, (self.x + way) % 4)

    def along_y(self, slot, kind, pair, back):
        step = self.turn(slot, kind) * (-1 if back else 1)
        return self.copy(slot, kind, pair, back, (self.y + step + 8) % 8, self.x)

    def turn(self, slot, kind):
        return self.sign * (1 - 2 * (slot % 2)) if kind == 0 else self.sign

    def across(self, block):
        chip = self.y * 4 + self.x
        return pltpu.make_async_remote_copy(
            src_ref=block, dst_ref=block, send_sem=self.over.at[0], recv_sem=self.over.at[1],
            device_id=(self.p, chip * 2 + 1 - self.core), device_id_type=MESH)

    def cross(self, slot, kind, pair):
        if kind == 1:
            self.across(self.block(slot, kind, pair)).start()

    def arrived(self, slot, kind, pair):
        self.along_x(slot, kind, pair, 1).wait_recv()

    def of_row(self, origin, act):
        for pair in range(4):
            @pl.when(jnp.logical_and(origin // 2 == pair, self.core == pair // 2))
            def _():
                act(pair)

    def spread(self, act, slot, kind, pair, first):
        for way in (1, 3, 2):
            act(self.along_x(slot, kind, pair, way))
        if first:
            self.cross(slot, kind, pair)

    def round_y(self, act, slot, kind, pair):
        act(self.along_y(slot, kind, pair, 0))
        act(self.along_y(slot, kind, pair, 1))

    def own_sends(self, act, first):
        def begin(pair):
            for kind in self.later:
                self.round_y(act, self.place, kind, pair)

        def go_on(pair):
            for kind in self.later:
                self.spread(act, self.place, kind, pair, first)

        self.spread(act, self.place, 0, None, False)
        self.of_row(self.y, begin)
        self.round_y(act, self.place, 0, None)
        self.of_row(self.y, go_on)

    def row_sends(self, act, wait):
        for around in (1, 3, 2):
            slot = (self.y % 4) * 4 + (self.x + around) % 4
            if wait:
                self.arrived(slot, 0, None)
            self.round_y(act, slot, 0, None)

    def lower_hop(self, act, wait, distance, odd):
        columns = [(self.x + odd) % 4, (self.x + odd + 2) % 4]
        for back in range(2 if distance < 4 else 1):
            step = self.turn(columns[0], 0) * distance * (1 if back else -1)
            origin = (self.y + step + 8) % 8

            @pl.when(origin // 4 == self.core)
            def _():
                for column in columns:
                    slot = (origin % 4) * 4 + column
                    if wait:
                        self.arrived(slot, 0, None)
                    if distance < (3 if back else 4):
                        act(self.along_y(slot, 0, None, back))

    def weight_hop(self, act, wait, distance):
        for back in range(2 if distance < 4 else 1):
            origin = (self.y + self.sign * distance * (1 if back else -1) + 8) % 8
            slot = (origin % 4) * 4 + self.x

            def pass_on(pair):
                for kind in self.later:
                    if wait:
                        self.arrived(slot, kind, pair)
                    if distance < (3 if back else 4):
                        act(self.along_y(slot, kind, pair, back))
                    self.spread(act, slot, kind, pair, wait)

            self.of_row(origin, pass_on)

    def last_along_x(self):
        for s in range(4):
            def end(pair):
                for way in (1, 3, 2):
                    slot = s * 4 + (self.x + way) % 4
                    for kind in self.later:
                        self.arrived(slot, kind, pair)
                        self.cross(slot, kind, pair)

            self.of_row(4 * self.core + s, end)

    def both_ways(self, act):
        lower_rows = self.weight.at[:6]
        upper_rows = self.weight.at[:14]

        @pl.when(self.core == 0)
        def _():
            act(self.across(lower_rows), self.across(upper_rows))

        @pl.when(self.core == 1)
        def _():
            act(self.across(upper_rows), self.across(lower_rows))

    def walk(self, act, wait):
        @pl.when(self.source)
        def _():
            self.own_sends(act, wait)
            self.row_sends(act, wait)

        self.weight_hop(act, wait, 1)
        self.weight_hop(act, wait, 2)
        self.lower_hop(act, wait, 1, 0)
        self.lower_hop(act, wait, 1, 1)
        self.weight_hop(act, wait, 3)
        self.lower_hop(act, wait, 2, 0)
        self.lower_hop(act, wait, 2, 1)
        self.weight_hop(act, wait, 4)
        self.lower_hop(act, wait, 3, 0)
        self.lower_hop(act, wait, 3, 1)

    def run(self, arrived):
        self.walk(lambda copy: copy.start(), True)
        self.last_along_x()
        arrived()
        self.lower_hop(None, True, 4, 0)
        self.lower_hop(None, True, 4, 1)

    def finish(self):
        self.walk(lambda copy: copy.wait_send(), False)


class PlainRing(Ring):
    later = (1,)

    def __init__(self, held, sems, p, y, x, core, place, source):
        super().__init__(held, held, sems + (None,), p, y, x, core, place, source)

    def block(self, slot, kind, pair):
        return self.lower.at[slot, :, HALF * kind:HALF * (kind + 1)]

    def cross(self, slot, kind, pair):
        pass

    def of_row(self, origin, act):
        @pl.when(origin // 4 == self.core)
        def _():
            act(None)


def chain(
    flag_ref, weight_hbm, lower_hbm, end_hbm, sigma_ref, cross_ref,
    weight_rows, lower_rows, end_ref, weight_ref, lower_ref, coupled_ref,
    through_ref, through_in, through_out, first_sigma, cross_part, cross_in,
    rows_there, rows_here, gram_buf, end_buf, next_buf, next_out,
    part_out, part_in, part2_out, part2_in, pack, recv, rows_out,
    load_sem, here_sem, ring_send, ring_recv, across_sem,
    through_recv, through_sem, through_hop, ahead_sem,
    end_sem, next_sem, part_sem, part2_sem, rows_sem, pack_sem,
):
    parts = 8
    p = lax.axis_index("tm")
    r = lax.axis_index("rows")
    chip, core = r // 2, r % 2
    half = chip // HALF_CHIPS
    place = chip % HALF_CHIPS
    y, x = chip // 4, chip % 4
    source_core = core == half
    sibling = (p, chip * 2 + 1 - core)

    def peer(j):
        return (p, (core * HALF_CHIPS + j) * 2 + half)

    loads = [
        pltpu.make_async_copy(src, dst, load_sem.at[k])
        for k, (src, dst) in enumerate(
            ((lower_hbm, lower_rows), (weight_hbm, weight_rows), (end_hbm, end_ref)))
    ]
    for load in loads:
        load.start()
    barrier = pltpu.get_barrier_semaphore()
    pl.semaphore_signal(barrier, 1, device_id=sibling, device_id_type=MESH)

    @pl.when(p > 0)
    def _():
        pl.semaphore_signal(barrier, 1, device_id=(p - 1, r), device_id_type=MESH)

    @pl.when(p < parts - 1)
    def _():
        pl.semaphore_signal(barrier, 1, device_id=(p + 1, r), device_id_type=MESH)

    def is_self(j):
        return jnp.logical_and(core == half, place == j)

    for around in (1, 7):
        there = ((y + around) % 8) * 4 + x
        pl.semaphore_signal(
            barrier, 1, device_id=(p, there * 2 + core), device_id_type=MESH)
    for around in (1, 2, 3):
        there = y * 4 + (x + around) % 4
        pl.semaphore_signal(
            barrier, 1, device_id=(p, there * 2 + core), device_id_type=MESH)

    @pl.when(p < SPLIT - 1)
    def _():
        pl.semaphore_signal(barrier, 1, device_id=(SPLIT, r), device_id_type=MESH)

    expected = (
        6 + jnp.where(p > 0, 1, 0) + jnp.where(p < parts - 1, 1, 0)
        + jnp.where(p == SPLIT, SPLIT - 1, 0))
    for pair in range(3):
        weight_ref[8 * pair:8 * pair + 8, :, STEP * (pair + 1):] = jnp.zeros(
            (8, PANEL, B - STEP * (pair + 1)), BF16)
    for load in loads:
        load.wait()
    rows_here[0] = lower_rows[...].astype(F32)
    rows_here[1] = weight_rows[...].astype(F32)
    pl.semaphore_wait(barrier, expected)

    mine = pl.ds(pl.multiple_of(core * HALF, 128), HALF)
    theirs = pl.ds(pl.multiple_of((1 - core) * HALF, 128), HALF)
    my_rows = pl.ds(pl.multiple_of(core * OWN, 8), OWN)
    their_rows = pl.ds(pl.multiple_of((1 - core) * OWN, 8), OWN)

    def to_sibling(src, dst, sems):
        return pltpu.make_async_remote_copy(
            src_ref=src, dst_ref=dst, send_sem=sems.at[0], recv_sem=sems.at[1],
            device_id=sibling, device_id_type=MESH)

    here_copy = to_sibling(rows_here, rows_there, here_sem)

    @pl.when(jnp.logical_not(source_core))
    def _():
        here_copy.start()

    end_copy = to_sibling(end_ref.at[:, theirs], end_buf.at[my_rows], end_sem)
    end_copy.start()
    end_buf[my_rows] = end_ref[:, mine]
    ring = Ring(
        lower_ref, weight_ref, (ring_send, ring_recv, across_sem),
        p, y, x, core, place, source_core)

    @pl.when(source_core)
    def _():
        here_copy.wait_recv()
        for which, there in ((0, rows_there[0]), (1, rows_there[1])):
            ours = rows_here[which]
            low = jnp.where(core == 0, ours, there)
            high = jnp.where(core == 0, there, ours)
            both = jnp.concatenate([low, high], axis=0).astype(BF16)
            if which == 0:
                lower_ref[place] = both
            else:
                weight_ref[chip] = both

    def couple(s):
        rows = pl.ds(4 * s, 4)
        left = lower_ref[rows, :, :HALF].reshape(4 * PANEL, HALF)
        right = lower_ref[rows, :, HALF:].reshape(4 * PANEL, HALF)
        for k in range(B // WINDOW):
            columns = slice(WINDOW * k, WINDOW * (k + 1))
            total = dot(right, weight_ref[HALF_CHIPS:, :, columns].reshape(HALF, WINDOW))
            if k < HALF // WINDOW:
                total = total + dot(
                    left, weight_ref[:HALF_CHIPS, :, columns].reshape(HALF, WINDOW))
            coupled_ref[rows, :, columns] = total.astype(BF16).reshape(4, PANEL, WINDOW)

    def couple_near():
        ring.both_ways(lambda ours, others: others.wait_recv())

        @pl.loop(1, 4)
        def _(i):
            couple((y + i) % 4)

    ring.run(couple_near)
    couple(y % 4)
    ring.both_ways(lambda ours, others: ours.wait_send())
    ring.finish()
    end_copy.wait_recv()
    end_b = end_buf[...].astype(BF16)
    broken = flag_ref[p] == 1
    early = p < SPLIT

    def down(src, dst, send, receive, target):
        return pltpu.make_async_remote_copy(
            src_ref=src, dst_ref=dst, send_sem=send, recv_sem=receive,
            device_id=(target, r), device_id_type=MESH)

    below = jnp.maximum(p - 1, 0)
    hops = [
        down(next_out.at[0], next_buf.at[0], next_sem.at[0, 0], next_sem.at[0, 1], below),
        None,
        down(next_out.at[1], next_buf.at[2], next_sem.at[2, 0], next_sem.at[2, 1], below),
    ]
    jumps = [
        down(next_out.at[0], next_buf.at[1], ahead_sem.at[q], next_sem.at[1, 1], q)
        for q in range(SPLIT)
    ]
    through_copy = down(
        through_out, through_in, through_hop.at[0], through_hop.at[1], below)

    def sum_halves(k, source, right_ref):
        copy = to_sibling(part_out.at[k], part_in.at[k], part_sem.at[k])
        part_out[k] = dot(source, right_ref[:, :, theirs].reshape(HALF, HALF))
        copy.start()
        own = dot(source, right_ref[:, :, mine].reshape(HALF, HALF))
        copy.wait_recv()
        return own + part_in[k]

    def pack_copy(k, j):
        return pltpu.make_async_remote_copy(
            src_ref=pack.at[k, j], dst_ref=recv.at[k, place], send_sem=pack_sem.at[k, 0],
            recv_sem=pack_sem.at[k, 1], device_id=peer(j), device_id_type=MESH)

    def messages(k, act):
        def count(n):
            return pltpu.make_async_remote_copy(
                src_ref=pack.at[k, :n], dst_ref=recv.at[k, :n], send_sem=pack_sem.at[k, 0],
                recv_sem=pack_sem.at[k, 1], device_id=sibling, device_id_type=MESH)

        @pl.when(source_core)
        def _():
            act(count(HALF_CHIPS - 1))

        @pl.when(jnp.logical_not(source_core))
        def _():
            act(count(HALF_CHIPS))

    def emit(which, value, out_ref, act):
        copy = to_sibling(
            rows_out.at[which, their_rows], out_ref.at[:, mine], rows_sem.at[which])
        if act == "start":
            rows_out[which] = value
            copy.start()
            out_ref[:, mine] = rows_out[which, my_rows]
        else:
            copy.wait()

    def step(k, source, right_ref, meanwhile):
        product = sum_halves(k, source, right_ref)
        for j in range(HALF_CHIPS):
            pack[k, j] = message(product, j)

        for j in range(HALF_CHIPS):
            @pl.when(jnp.logical_not(is_self(j)))
            def _():
                pack_copy(k, j).start()

        @pl.when(source_core)
        def _():
            recv[k, place] = pack[k, place]

        base = meanwhile(product)
        messages(k, lambda copy: copy.wait_recv())
        first = recv[k, :, :16].reshape(HALF_CHIPS * 16, 128).T
        second = recv[k, :, 16:].reshape(HALF_CHIPS * 16, 128).T

        def update(columns):
            def rows(i):
                return right_ref[:, 16 * i:16 * i + 16, columns].reshape(HALF_CHIPS * 16, HALF)
            total = dot(first[:48], rows(0)) + dot(first[64:112], rows(1))
            total = total + dot(second[:48], rows(2))
            return total if base is None else total + base(columns)

        copy = to_sibling(part2_out.at[k], part2_in.at[k], part2_sem.at[k])
        part2_out[k] = update(theirs)
        copy.start()
        sigma = update(mine)
        copy.wait_recv()
        return sigma + part2_in[k]

    through_ring = PlainRing(
        through_ref, (ring_send, through_recv), p, y, x, core, place, source_core)
    through_half = to_sibling(through_out, through_out, through_sem.at[0])
    through_here = to_sibling(through_out, through_ref.at[place, :, mine], through_sem.at[1])
    zero = jnp.zeros((PANEL, HALF), BF16)

    @pl.when(p == SPLIT - 1)
    def _():
        @pl.when(source_core)
        def _():
            next_out[1] = jnp.where(broken, zero, coupled_ref[place, :, theirs])
            half_copy = to_sibling(next_out.at[1], through_out, through_sem.at[0])
            half_copy.start()
            through_out[...] = jnp.where(broken, zero, coupled_ref[place, :, mine])
            half_copy.wait_send()

        @pl.when(jnp.logical_not(source_core))
        def _():
            through_half.wait_recv()

        through_copy.start()

        @pl.loop(0, HALF_CHIPS)
        def _(j):
            rows = coupled_ref[j]
            through_ref[j] = jnp.where(broken, jnp.zeros_like(rows), rows)

    @pl.when(p < SPLIT - 1)
    def _():
        through_copy.wait_recv()
        rows = sum_halves(2, through_in[...], coupled_ref).astype(BF16)
        through_out[...] = jnp.where(broken, zero, rows)

        @pl.when(p > 0)
        def _():
            through_copy.start()

        @pl.when(source_core)
        def _():
            through_ref[place, :, mine] = through_out[...]

        @pl.when(jnp.logical_not(source_core))
        def _():
            through_here.start()

    def gather_through():
        @pl.when(source_core)
        def _():
            to_sibling(through_out, through_ref.at[place, :, theirs], through_sem.at[1]).wait_recv()

        through_ring.run(lambda: None)

    @pl.when(p < SPLIT - 2)
    def _():
        gather_through()

    has_above = jnp.logical_and(p != parts - 1, p != SPLIT - 1)

    @pl.when(has_above)
    def _():
        hops[0].wait_recv()

    @pl.when(jnp.logical_not(has_above))
    def _():
        next_buf[0] = zero

    use_end = jnp.logical_or(broken, p == parts - 1)

    def gram(product):
        window = jnp.minimum(chip * PANEL // 128, (B - WINDOW) // 128) * 128
        chips = pl.ds(core * HALF_CHIPS, HALF_CHIPS)
        own = weight_ref[chips, :, pl.ds(pl.multiple_of(window, 128), WINDOW)]
        own = own.reshape(HALF, WINDOW).T
        for k in range(B // WINDOW):
            columns = slice(WINDOW * k, WINDOW * (k + 1))
            gram_buf[:, columns] = dot(own, weight_ref[chips, :, columns].reshape(HALF, WINDOW))
        gram_rows = pl.ds(pl.multiple_of(chip * PANEL - window, 16), PANEL)

        @pl.when(jnp.logical_not(early))
        def _():
            emit(0, -product, cross_ref, "start")

        return lambda columns: gram_buf[gram_rows, columns]

    sigma = step(0, jnp.where(use_end, end_b, next_buf[0]), coupled_ref, gram)
    next_out[0] = sigma.astype(BF16)
    sends_down = jnp.logical_and(p > 0, p != SPLIT)

    @pl.when(sends_down)
    def _():
        hops[0].start()

    @pl.when(p == SPLIT)
    def _():
        for q in (1, 2, 3, 0):
            jumps[q].start()

    @pl.when(jnp.logical_not(early))
    def _():
        emit(1, sigma, sigma_ref, "start")

    @pl.when(early)
    def _():
        first_sigma[...] = sigma

        @pl.when(p == SPLIT - 2)
        def _():
            gather_through()

        jumps[0].wait_recv()
        whole = first_sigma[...] + step(1, next_buf[1], through_ref, lambda product: None)
        next_out[1] = whole.astype(BF16)

        @pl.when(p > 0)
        def _():
            hops[2].start()

        emit(1, whole, sigma_ref, "start")

        @pl.when(p < SPLIT - 1)
        def _():
            hops[2].wait_recv()

        @pl.when(p == SPLIT - 1)
        def _():
            next_buf[2] = next_buf[1]

        source = jnp.where(broken, end_b, next_buf[2])
        for k in range(2):
            columns = slice(HALF * k, HALF * (k + 1))
            cross_part[:, columns] = -dot(
                source, coupled_ref[:, :, columns].reshape(HALF, HALF))
        cross_copy = to_sibling(cross_part.at[their_rows], cross_in, rows_sem.at[0])
        cross_copy.start()
        cross_copy.wait_recv()
        cross_ref[...] = cross_part[my_rows] + cross_in[...]

    end_copy.wait_send()

    @pl.when(jnp.logical_not(source_core))
    def _():
        here_copy.wait_send()

    def sent(k):
        to_sibling(part_out.at[k], part_in.at[k], part_sem.at[k]).wait_send()

    def step_sent(k):
        sent(k)
        to_sibling(part2_out.at[k], part2_in.at[k], part2_sem.at[k]).wait_send()
        messages(k, lambda copy: copy.wait_send())

    step_sent(0)

    @pl.when(sends_down)
    def _():
        hops[0].wait_send()

    @pl.when(p == SPLIT)
    def _():
        for jump in jumps:
            jump.wait_send()

    @pl.when(early)
    def _():
        step_sent(1)
        to_sibling(cross_part.at[their_rows], cross_in, rows_sem.at[0]).wait_send()

        @pl.when(p > 0)
        def _():
            through_copy.wait_send()
            hops[2].wait_send()

    @pl.when(p < SPLIT - 1)
    def _():
        sent(2)
        through_ring.finish()

        @pl.when(jnp.logical_not(source_core))
        def _():
            through_here.wait_send()

    @pl.when(jnp.logical_not(early))
    def _():
        emit(0, None, cross_ref, "wait")

    emit(1, None, sigma_ref, "wait")


def run_chain(flag, weight, lower, end):
    vmem = pl.BlockSpec(memory_space=pltpu.VMEM)
    dma = pltpu.SemaphoreType.DMA
    return pl.pallas_call(
        chain,
        out_shape=[jax.ShapeDtypeStruct((OWN, B), F32)] * 2,
        in_specs=[pl.BlockSpec(memory_space=pltpu.SMEM)] + [pl.BlockSpec(memory_space=pl.ANY)] * 3,
        out_specs=[vmem, vmem],
        scratch_shapes=[
            pltpu.VMEM((OWN, B), BF16),
            pltpu.VMEM((OWN, B), BF16),
            pltpu.VMEM((OWN, B), F32),
            pltpu.VMEM((CHIPS, PANEL, B), BF16),
            pltpu.VMEM((HALF_CHIPS, PANEL, B), BF16),
            pltpu.VMEM((HALF_CHIPS, PANEL, B), BF16),
            pltpu.VMEM((HALF_CHIPS, PANEL, B), BF16),
            pltpu.VMEM((PANEL, HALF), BF16),
            pltpu.VMEM((PANEL, HALF), BF16),
            pltpu.VMEM((PANEL, HALF), F32),
            pltpu.VMEM((PANEL, B), F32),
            pltpu.VMEM((OWN, B), F32),
            pltpu.VMEM((2, OWN, B), F32),
            pltpu.VMEM((2, OWN, B), F32),
            pltpu.VMEM((WINDOW, B), F32),
            pltpu.VMEM((PANEL, HALF), F32),
            pltpu.VMEM((3, PANEL, HALF), BF16),
            pltpu.VMEM((2, PANEL, HALF), BF16),
            pltpu.VMEM((3, PANEL, HALF), F32),
            pltpu.VMEM((3, PANEL, HALF), F32),
            pltpu.VMEM((2, PANEL, HALF), F32),
            pltpu.VMEM((2, PANEL, HALF), F32),
            pltpu.VMEM((2, HALF_CHIPS, 32, 128), BF16),
            pltpu.VMEM((2, HALF_CHIPS, 32, 128), BF16),
            pltpu.VMEM((2, PANEL, HALF), F32),
            dma((3,)), dma((2,)), dma((75,)), dma((HALF_CHIPS, 3)), dma((2,)),
            dma((HALF_CHIPS, 2)), dma((2, 2)), dma((2,)), dma((SPLIT,)),
            dma((2,)), dma((3, 2)), dma((3, 2)), dma((2, 2)), dma((2, 2)), dma((2, 2)),
        ],
        compiler_params=pltpu.CompilerParams(
            collective_id=0, has_side_effects=True, vmem_limit_bytes=40 * 1024 * 1024),
    )(flag, weight, lower, end)


def shards(w_inv, lower_block, sigma_end, chain_break):
    sigma, cross = run_chain(chain_break, w_inv[0], lower_block[0], sigma_end)
    return (sigma[None], cross[None])


def solution(mesh):
    in_specs = (P("tm", "rows", None), P("tm", "rows", None), P("rows", None), P())
    out_specs = (P("tm", "rows", None), P("tm", "rows", None))
    return jax.shard_map(shards, mesh=mesh, in_specs=in_specs, out_specs=out_specs, check_vma=False)
```

```python
import jax
import jax.numpy as jnp
from jax import lax
from jax.experimental import pallas as pl
from jax.experimental.pallas import tpu as pltpu
from jax.sharding import PartitionSpec as P

MESH = pl.DeviceIdType.MESH
BF16 = jnp.bfloat16
F32 = jnp.float32
B = 1536
CHIPS = 32
HALF_CHIPS = 16
PANEL = 48
OWN = 24
HALF = 768
WINDOW = 256
SPLIT = 4
STEP = 384
LEFT = 1152


def dot(a, b):
    return jnp.dot(a, b, preferred_element_type=F32)


def message(product, j):
    start = PANEL * j
    tile, off = start // 128, start % 128
    lanes = lax.broadcasted_iota(jnp.int32, (PANEL, 128), 1)
    block = product[:, tile * 128:(tile + 1) * 128]
    if off:
        block = pltpu.roll(block, 128 - off, 1)
        if off + PANEL > 128:
            after = pltpu.roll(product[:, (tile + 1) * 128:(tile + 2) * 128], 128 - off, 1)
            block = jnp.where(lanes < 128 - off, block, after)
    top = jnp.where(lanes[:16] < 64, block[:16], pltpu.roll(block[16:32], 64, 1))
    return jnp.concatenate([top, block[32:48]], axis=0).astype(BF16)


class Ring:
    later = (1, 2)

    def __init__(self, lower, weight, sems, p, y, x, core, place, source):
        self.lower, self.weight = lower, weight
        self.sends, self.receives, self.over = sems
        self.p, self.y, self.x, self.core = p, y, x, core
        self.place, self.source = place, source
        self.sign = 1 - 2 * core

    def block(self, slot, kind, pair):
        if kind == 1:
            return self.weight.at[HALF_CHIPS * self.core + slot, :, :STEP * (pair + 1)]
        return self.lower.at[slot, :, slice(0, LEFT) if kind == 0 else slice(LEFT, B)]

    def copy(self, slot, kind, pair, way, y, x):
        block = self.block(slot, kind, pair)
        return pltpu.make_async_remote_copy(
            src_ref=block, dst_ref=block, send_sem=self.sends.at[self.sender(slot, kind, way)],
            recv_sem=self.receives.at[slot, kind],
            device_id=(self.p, (y * 4 + x) * 2 + self.core), device_id_type=MESH)

    def sender(self, slot, kind, way):
        if kind:
            return 35 + 20 * (kind - 1) + 5 * (slot // 4) + way
        return 2 * slot + way if way < 2 else 30 + way

    def along_x(self, slot, kind, pair, way):
        return self.copy(slot, kind, pair, 1 + way, self.y, (self.x + way) % 4)

    def along_y(self, slot, kind, pair, back):
        step = self.turn(slot, kind) * (-1 if back else 1)
        return self.copy(slot, kind, pair, back, (self.y + step + 8) % 8, self.x)

    def turn(self, slot, kind):
        return self.sign * (1 - 2 * (slot % 2)) if kind == 0 else self.sign

    def across(self, block):
        chip = self.y * 4 + self.x
        return pltpu.make_async_remote_copy(
            src_ref=block, dst_ref=block, send_sem=self.over.at[0], recv_sem=self.over.at[1],
            device_id=(self.p, chip * 2 + 1 - self.core), device_id_type=MESH)

    def cross(self, slot, kind, pair):
        if kind == 1:
            self.across(self.block(slot, kind, pair)).start()

    def arrived(self, slot, kind, pair):
        self.along_x(slot, kind, pair, 1).wait_recv()

    def of_row(self, origin, act):
        for pair in range(4):
            @pl.when(jnp.logical_and(origin // 2 == pair, self.core == pair // 2))
            def _():
                act(pair)

    def spread(self, act, slot, kind, pair, first):
        for way in (1, 3, 2):
            act(self.along_x(slot, kind, pair, way))
        if first:
            self.cross(slot, kind, pair)

    def round_y(self, act, slot, kind, pair):
        act(self.along_y(slot, kind, pair, 0))
        act(self.along_y(slot, kind, pair, 1))

    def own_sends(self, act, first):
        def begin(pair):
            for kind in self.later:
                self.round_y(act, self.place, kind, pair)

        def go_on(pair):
            for kind in self.later:
                self.spread(act, self.place, kind, pair, first)

        self.spread(act, self.place, 0, None, False)
        self.of_row(self.y, begin)
        self.round_y(act, self.place, 0, None)
        self.of_row(self.y, go_on)

    def row_sends(self, act, wait):
        for around in (1, 3, 2):
            slot = (self.y % 4) * 4 + (self.x + around) % 4
            if wait:
                self.arrived(slot, 0, None)
            self.round_y(act, slot, 0, None)

    def lower_hop(self, act, wait, distance, odd):
        columns = [(self.x + odd) % 4, (self.x + odd + 2) % 4]
        for back in range(2 if distance < 4 else 1):
            step = self.turn(columns[0], 0) * distance * (1 if back else -1)
            origin = (self.y + step + 8) % 8

            @pl.when(origin // 4 == self.core)
            def _():
                for column in columns:
                    slot = (origin % 4) * 4 + column
                    if wait:
                        self.arrived(slot, 0, None)
                    if distance < (3 if back else 4):
                        act(self.along_y(slot, 0, None, back))

    def weight_hop(self, act, wait, distance):
        for back in range(2 if distance < 4 else 1):
            origin = (self.y + self.sign * distance * (1 if back else -1) + 8) % 8
            slot = (origin % 4) * 4 + self.x

            def pass_on(pair):
                for kind in self.later:
                    if wait:
                        self.arrived(slot, kind, pair)
                    if distance < (3 if back else 4):
                        act(self.along_y(slot, kind, pair, back))
                    self.spread(act, slot, kind, pair, wait)

            self.of_row(origin, pass_on)

    def last_along_x(self):
        for s in range(4):
            def end(pair):
                for way in (1, 3, 2):
                    slot = s * 4 + (self.x + way) % 4
                    for kind in self.later:
                        self.arrived(slot, kind, pair)
                        self.cross(slot, kind, pair)

            self.of_row(4 * self.core + s, end)

    def both_ways(self, act):
        lower_rows = self.weight.at[:6]
        upper_rows = self.weight.at[:14]

        @pl.when(self.core == 0)
        def _():
            act(self.across(lower_rows), self.across(upper_rows))

        @pl.when(self.core == 1)
        def _():
            act(self.across(upper_rows), self.across(lower_rows))

    def walk(self, act, wait):
        @pl.when(self.source)
        def _():
            self.own_sends(act, wait)
            self.row_sends(act, wait)

        self.weight_hop(act, wait, 1)
        self.weight_hop(act, wait, 2)
        self.lower_hop(act, wait, 1, 0)
        self.lower_hop(act, wait, 1, 1)
        self.weight_hop(act, wait, 3)
        self.lower_hop(act, wait, 2, 0)
        self.lower_hop(act, wait, 2, 1)
        self.weight_hop(act, wait, 4)
        self.lower_hop(act, wait, 3, 0)
        self.lower_hop(act, wait, 3, 1)

    def run(self, arrived):
        self.walk(lambda copy: copy.start(), True)
        self.last_along_x()
        arrived()
        self.lower_hop(None, True, 4, 0)
        self.lower_hop(None, True, 4, 1)

    def finish(self):
        self.walk(lambda copy: copy.wait_send(), False)


class PlainRing(Ring):
    later = (1,)

    def __init__(self, held, sems, p, y, x, core, place, source):
        super().__init__(held, held, sems + (None,), p, y, x, core, place, source)

    def block(self, slot, kind, pair):
        return self.lower.at[slot, :, HALF * kind:HALF * (kind + 1)]

    def cross(self, slot, kind, pair):
        pass

    def of_row(self, origin, act):
        @pl.when(origin // 4 == self.core)
        def _():
            act(None)


def chain(
    flag_ref, weight_hbm, lower_hbm, end_hbm, sigma_ref, cross_ref,
    weight_rows, lower_rows, end_ref, weight_ref, lower_ref, coupled_ref,
    through_ref, through_in, through_out, first_sigma, cross_part, cross_in,
    rows_there, rows_here, gram_buf, end_buf, next_buf, next_out,
    part_out, part_in, part2_out, part2_in, pack, recv, rows_out,
    load_sem, here_sem, ring_send, ring_recv, across_sem,
    through_recv, through_sem, through_hop, ahead_sem,
    end_sem, next_sem, part_sem, part2_sem, rows_sem, pack_sem,
):
    parts = 8
    p = lax.axis_index("tm")
    r = lax.axis_index("rows")
    chip, core = r // 2, r % 2
    half = chip // HALF_CHIPS
    place = chip % HALF_CHIPS
    y, x = chip // 4, chip % 4
    source_core = core == half
    sibling = (p, chip * 2 + 1 - core)

    def peer(j):
        return (p, (core * HALF_CHIPS + j) * 2 + half)

    loads = [
        pltpu.make_async_copy(src, dst, load_sem.at[k])
        for k, (src, dst) in enumerate(
            ((lower_hbm, lower_rows), (weight_hbm, weight_rows), (end_hbm, end_ref)))
    ]
    for load in loads:
        load.start()
    barrier = pltpu.get_barrier_semaphore()
    pl.semaphore_signal(barrier, 1, device_id=sibling, device_id_type=MESH)

    @pl.when(p > 0)
    def _():
        pl.semaphore_signal(barrier, 1, device_id=(p - 1, r), device_id_type=MESH)

    @pl.when(p < parts - 1)
    def _():
        pl.semaphore_signal(barrier, 1, device_id=(p + 1, r), device_id_type=MESH)

    def is_self(j):
        return jnp.logical_and(core == half, place == j)

    for around in (1, 7):
        there = ((y + around) % 8) * 4 + x
        pl.semaphore_signal(
            barrier, 1, device_id=(p, there * 2 + core), device_id_type=MESH)
    for around in (1, 2, 3):
        there = y * 4 + (x + around) % 4
        pl.semaphore_signal(
            barrier, 1, device_id=(p, there * 2 + core), device_id_type=MESH)

    @pl.when(p < SPLIT - 1)
    def _():
        pl.semaphore_signal(barrier, 1, device_id=(SPLIT, r), device_id_type=MESH)

    expected = (
        6 + jnp.where(p > 0, 1, 0) + jnp.where(p < parts - 1, 1, 0)
        + jnp.where(p == SPLIT, SPLIT - 1, 0))
    for pair in range(3):
        weight_ref[8 * pair:8 * pair + 8, :, STEP * (pair + 1):] = jnp.zeros(
            (8, PANEL, B - STEP * (pair + 1)), BF16)
    for load in loads:
        load.wait()
    rows_here[0] = lower_rows[...].astype(F32)
    rows_here[1] = weight_rows[...].astype(F32)
    pl.semaphore_wait(barrier, expected)

    mine = pl.ds(pl.multiple_of(core * HALF, 128), HALF)
    theirs = pl.ds(pl.multiple_of((1 - core) * HALF, 128), HALF)
    my_rows = pl.ds(pl.multiple_of(core * OWN, 8), OWN)
    their_rows = pl.ds(pl.multiple_of((1 - core) * OWN, 8), OWN)

    def to_sibling(src, dst, sems):
        return pltpu.make_async_remote_copy(
            src_ref=src, dst_ref=dst, send_sem=sems.at[0], recv_sem=sems.at[1],
            device_id=sibling, device_id_type=MESH)

    here_copy = to_sibling(rows_here, rows_there, here_sem)

    @pl.when(jnp.logical_not(source_core))
    def _():
        here_copy.start()

    end_copy = to_sibling(end_ref.at[:, theirs], end_buf.at[my_rows], end_sem)
    end_copy.start()
    end_buf[my_rows] = end_ref[:, mine]
    ring = Ring(
        lower_ref, weight_ref, (ring_send, ring_recv, across_sem),
        p, y, x, core, place, source_core)

    @pl.when(source_core)
    def _():
        here_copy.wait_recv()
        for which, there in ((0, rows_there[0]), (1, rows_there[1])):
            ours = rows_here[which]
            low = jnp.where(core == 0, ours, there)
            high = jnp.where(core == 0, there, ours)
            both = jnp.concatenate([low, high], axis=0).astype(BF16)
            if which == 0:
                lower_ref[place] = both
            else:
                weight_ref[chip] = both

    def couple(s):
        rows = pl.ds(4 * s, 4)
        left = lower_ref[rows, :, :HALF].reshape(4 * PANEL, HALF)
        right = lower_ref[rows, :, HALF:].reshape(4 * PANEL, HALF)
        for k in range(B // WINDOW):
            columns = slice(WINDOW * k, WINDOW * (k + 1))
            total = dot(right, weight_ref[HALF_CHIPS:, :, columns].reshape(HALF, WINDOW))
            if k < HALF // WINDOW:
                total = total + dot(
                    left, weight_ref[:HALF_CHIPS, :, columns].reshape(HALF, WINDOW))
            coupled_ref[rows, :, columns] = total.astype(BF16).reshape(4, PANEL, WINDOW)

    def couple_near():
        ring.both_ways(lambda ours, others: others.wait_recv())

        @pl.loop(1, 4)
        def _(i):
            couple((y + i) % 4)

    ring.run(couple_near)
    couple(y % 4)
    ring.both_ways(lambda ours, others: ours.wait_send())
    ring.finish()
    end_copy.wait_recv()
    end_b = end_buf[...].astype(BF16)
    broken = flag_ref[p] == 1
    early = p < SPLIT

    def down(src, dst, send, receive, target):
        return pltpu.make_async_remote_copy(
            src_ref=src, dst_ref=dst, send_sem=send, recv_sem=receive,
            device_id=(target, r), device_id_type=MESH)

    below = jnp.maximum(p - 1, 0)
    pieces = (slice(0, 512), slice(512, HALF))

    def hop(which, held, c):
        return down(
            next_out.at[held, :, pieces[c]], next_buf.at[which, :, pieces[c]],
            next_sem.at[which, 0, c], next_sem.at[which, 1, c], below)

    hops = [[hop(0, 0, 0), hop(0, 0, 1)], None, [hop(2, 1, 0), hop(2, 1, 1)]]
    jumps = [
        [
            down(
                next_out.at[0, :, piece], next_buf.at[1, :, piece],
                ahead_sem.at[q, c], next_sem.at[1, 1, c], q)
            for c, piece in enumerate(pieces)
        ]
        for q in range(SPLIT)
    ]
    through_copy = down(
        through_out, through_in, through_hop.at[0], through_hop.at[1], below)

    def sum_halves(k, source, right_ref):
        copy = to_sibling(part_out.at[k], part_in.at[k], part_sem.at[k])
        part_out[k] = dot(source, right_ref[:, :, theirs].reshape(HALF, HALF))
        copy.start()
        own = dot(source, right_ref[:, :, mine].reshape(HALF, HALF))
        copy.wait_recv()
        return own + part_in[k]

    def pack_copy(k, j):
        return pltpu.make_async_remote_copy(
            src_ref=pack.at[k, j], dst_ref=recv.at[k, place], send_sem=pack_sem.at[k, 0],
            recv_sem=pack_sem.at[k, 1], device_id=peer(j), device_id_type=MESH)

    def messages(k, act):
        def count(n):
            return pltpu.make_async_remote_copy(
                src_ref=pack.at[k, :n], dst_ref=recv.at[k, :n], send_sem=pack_sem.at[k, 0],
                recv_sem=pack_sem.at[k, 1], device_id=sibling, device_id_type=MESH)

        @pl.when(source_core)
        def _():
            act(count(HALF_CHIPS - 1))

        @pl.when(jnp.logical_not(source_core))
        def _():
            act(count(HALF_CHIPS))

    def emit(which, value, out_ref, act):
        copy = to_sibling(
            rows_out.at[which, their_rows], out_ref.at[:, mine], rows_sem.at[which])
        if act == "start":
            rows_out[which] = value
            copy.start()
            out_ref[:, mine] = rows_out[which, my_rows]
        else:
            copy.wait()

    def part2_copy(k, c):
        piece = pieces[c]
        return to_sibling(
            part2_out.at[k, :, piece], part2_in.at[k, :, piece], part2_sem.at[k, c])

    def step(k, source, right_ref, meanwhile, finish):
        product = sum_halves(k, source, right_ref)
        for j in range(HALF_CHIPS):
            pack[k, j] = message(product, j)

        for j in range(HALF_CHIPS):
            @pl.when(jnp.logical_not(is_self(j)))
            def _():
                pack_copy(k, j).start()

        @pl.when(source_core)
        def _():
            recv[k, place] = pack[k, place]

        base = meanwhile(product)
        messages(k, lambda copy: copy.wait_recv())
        first = recv[k, :, :16].reshape(HALF_CHIPS * 16, 128).T
        second = recv[k, :, 16:].reshape(HALF_CHIPS * 16, 128).T

        def update(side, piece):
            width = piece.stop - piece.start
            columns = pl.ds(pl.multiple_of(side * HALF + piece.start, 128), width)

            def rows(i):
                return right_ref[:, 16 * i:16 * i + 16, columns].reshape(HALF_CHIPS * 16, width)
            total = dot(first[:48], rows(0)) + dot(first[64:112], rows(1))
            total = total + dot(second[:48], rows(2))
            return total if base is None else total + base(columns)

        for c, piece in enumerate(pieces):
            part2_out[k, :, piece] = update(1 - core, piece)
            part2_copy(k, c).start()
        for c, piece in enumerate(pieces):
            sigma = update(core, piece)
            part2_copy(k, c).wait_recv()
            finish(c, piece, sigma + part2_in[k, :, piece])

    through_ring = PlainRing(
        through_ref, (ring_send, through_recv), p, y, x, core, place, source_core)
    through_half = to_sibling(through_out, through_out, through_sem.at[0])
    through_here = to_sibling(through_out, through_ref.at[place, :, mine], through_sem.at[1])
    zero = jnp.zeros((PANEL, HALF), BF16)

    @pl.when(p == SPLIT - 1)
    def _():
        @pl.when(source_core)
        def _():
            next_out[1] = jnp.where(broken, zero, coupled_ref[place, :, theirs])
            half_copy = to_sibling(next_out.at[1], through_out, through_sem.at[0])
            half_copy.start()
            through_out[...] = jnp.where(broken, zero, coupled_ref[place, :, mine])
            half_copy.wait_send()

        @pl.when(jnp.logical_not(source_core))
        def _():
            through_half.wait_recv()

        through_copy.start()

        @pl.loop(0, HALF_CHIPS)
        def _(j):
            rows = coupled_ref[j]
            through_ref[j] = jnp.where(broken, jnp.zeros_like(rows), rows)

    @pl.when(p < SPLIT - 1)
    def _():
        through_copy.wait_recv()
        rows = sum_halves(2, through_in[...], coupled_ref).astype(BF16)
        through_out[...] = jnp.where(broken, zero, rows)

        @pl.when(p > 0)
        def _():
            through_copy.start()

        @pl.when(source_core)
        def _():
            through_ref[place, :, mine] = through_out[...]

        @pl.when(jnp.logical_not(source_core))
        def _():
            through_here.start()

    def gather_through():
        @pl.when(source_core)
        def _():
            to_sibling(through_out, through_ref.at[place, :, theirs], through_sem.at[1]).wait_recv()

        through_ring.run(lambda: None)

    @pl.when(p < SPLIT - 2)
    def _():
        gather_through()

    has_above = jnp.logical_and(p != parts - 1, p != SPLIT - 1)

    @pl.when(has_above)
    def _():
        hops[0][0].wait_recv()
        hops[0][1].wait_recv()

    @pl.when(jnp.logical_not(has_above))
    def _():
        next_buf[0] = zero

    use_end = jnp.logical_or(broken, p == parts - 1)

    def gram(product):
        window = jnp.minimum(chip * PANEL // 128, (B - WINDOW) // 128) * 128
        chips = pl.ds(core * HALF_CHIPS, HALF_CHIPS)
        own = weight_ref[chips, :, pl.ds(pl.multiple_of(window, 128), WINDOW)]
        own = own.reshape(HALF, WINDOW).T
        for k in range(B // WINDOW):
            columns = slice(WINDOW * k, WINDOW * (k + 1))
            gram_buf[:, columns] = dot(own, weight_ref[chips, :, columns].reshape(HALF, WINDOW))
        gram_rows = pl.ds(pl.multiple_of(chip * PANEL - window, 16), PANEL)

        @pl.when(jnp.logical_not(early))
        def _():
            emit(0, -product, cross_ref, "start")

        return lambda columns: gram_buf[gram_rows, columns]

    sends_down = jnp.logical_and(p > 0, p != SPLIT)

    def pass_first(c, piece, sigma):
        next_out[0, :, piece] = sigma.astype(BF16)

        @pl.when(sends_down)
        def _():
            hops[0][c].start()

        @pl.when(p == SPLIT)
        def _():
            for q in (1, 2, 3, 0):
                jumps[q][c].start()

        first_sigma[:, piece] = sigma

    step(0, jnp.where(use_end, end_b, next_buf[0]), coupled_ref, gram, pass_first)

    @pl.when(jnp.logical_not(early))
    def _():
        emit(1, first_sigma[...], sigma_ref, "start")

    @pl.when(early)
    def _():
        @pl.when(p == SPLIT - 2)
        def _():
            gather_through()

        jumps[0][0].wait_recv()
        jumps[0][1].wait_recv()

        def pass_whole(c, piece, sigma):
            whole = first_sigma[:, piece] + sigma
            next_out[1, :, piece] = whole.astype(BF16)

            @pl.when(p > 0)
            def _():
                hops[2][c].start()

            first_sigma[:, piece] = whole

        step(1, next_buf[1], through_ref, lambda product: None, pass_whole)
        emit(1, first_sigma[...], sigma_ref, "start")

        @pl.when(p < SPLIT - 1)
        def _():
            hops[2][0].wait_recv()
            hops[2][1].wait_recv()

        @pl.when(p == SPLIT - 1)
        def _():
            next_buf[2] = next_buf[1]

        source = jnp.where(broken, end_b, next_buf[2])
        for k in range(2):
            columns = slice(HALF * k, HALF * (k + 1))
            cross_part[:, columns] = -dot(
                source, coupled_ref[:, :, columns].reshape(HALF, HALF))
        cross_copy = to_sibling(cross_part.at[their_rows], cross_in, rows_sem.at[0])
        cross_copy.start()
        cross_copy.wait_recv()
        cross_ref[...] = cross_part[my_rows] + cross_in[...]

    end_copy.wait_send()

    @pl.when(jnp.logical_not(source_core))
    def _():
        here_copy.wait_send()

    def sent(k):
        to_sibling(part_out.at[k], part_in.at[k], part_sem.at[k]).wait_send()

    def step_sent(k):
        sent(k)
        part2_copy(k, 0).wait_send()
        part2_copy(k, 1).wait_send()
        messages(k, lambda copy: copy.wait_send())

    step_sent(0)

    @pl.when(sends_down)
    def _():
        hops[0][0].wait_send()
        hops[0][1].wait_send()

    @pl.when(p == SPLIT)
    def _():
        for jump in jumps:
            jump[0].wait_send()
            jump[1].wait_send()

    @pl.when(early)
    def _():
        step_sent(1)
        to_sibling(cross_part.at[their_rows], cross_in, rows_sem.at[0]).wait_send()

        @pl.when(p > 0)
        def _():
            through_copy.wait_send()
            hops[2][0].wait_send()
            hops[2][1].wait_send()

    @pl.when(p < SPLIT - 1)
    def _():
        sent(2)
        through_ring.finish()

        @pl.when(jnp.logical_not(source_core))
        def _():
            through_here.wait_send()

    @pl.when(jnp.logical_not(early))
    def _():
        emit(0, None, cross_ref, "wait")

    emit(1, None, sigma_ref, "wait")


def run_chain(flag, weight, lower, end):
    vmem = pl.BlockSpec(memory_space=pltpu.VMEM)
    dma = pltpu.SemaphoreType.DMA
    return pl.pallas_call(
        chain,
        out_shape=[jax.ShapeDtypeStruct((OWN, B), F32)] * 2,
        in_specs=[pl.BlockSpec(memory_space=pltpu.SMEM)] + [pl.BlockSpec(memory_space=pl.ANY)] * 3,
        out_specs=[vmem, vmem],
        scratch_shapes=[
            pltpu.VMEM((OWN, B), BF16),
            pltpu.VMEM((OWN, B), BF16),
            pltpu.VMEM((OWN, B), F32),
            pltpu.VMEM((CHIPS, PANEL, B), BF16),
            pltpu.VMEM((HALF_CHIPS, PANEL, B), BF16),
            pltpu.VMEM((HALF_CHIPS, PANEL, B), BF16),
            pltpu.VMEM((HALF_CHIPS, PANEL, B), BF16),
            pltpu.VMEM((PANEL, HALF), BF16),
            pltpu.VMEM((PANEL, HALF), BF16),
            pltpu.VMEM((PANEL, HALF), F32),
            pltpu.VMEM((PANEL, B), F32),
            pltpu.VMEM((OWN, B), F32),
            pltpu.VMEM((2, OWN, B), F32),
            pltpu.VMEM((2, OWN, B), F32),
            pltpu.VMEM((WINDOW, B), F32),
            pltpu.VMEM((PANEL, HALF), F32),
            pltpu.VMEM((3, PANEL, HALF), BF16),
            pltpu.VMEM((2, PANEL, HALF), BF16),
            pltpu.VMEM((3, PANEL, HALF), F32),
            pltpu.VMEM((3, PANEL, HALF), F32),
            pltpu.VMEM((2, PANEL, HALF), F32),
            pltpu.VMEM((2, PANEL, HALF), F32),
            pltpu.VMEM((2, HALF_CHIPS, 32, 128), BF16),
            pltpu.VMEM((2, HALF_CHIPS, 32, 128), BF16),
            pltpu.VMEM((2, PANEL, HALF), F32),
            dma((3,)), dma((2,)), dma((75,)), dma((HALF_CHIPS, 3)), dma((2,)),
            dma((HALF_CHIPS, 2)), dma((2, 2)), dma((2,)), dma((SPLIT, 2)),
            dma((2,)), dma((3, 2, 2)), dma((3, 2)), dma((2, 2, 2)), dma((2, 2)), dma((2, 2)),
        ],
        compiler_params=pltpu.CompilerParams(
            collective_id=0, has_side_effects=True, vmem_limit_bytes=40 * 1024 * 1024),
    )(flag, weight, lower, end)


def shards(w_inv, lower_block, sigma_end, chain_break):
    sigma, cross = run_chain(chain_break, w_inv[0], lower_block[0], sigma_end)
    return (sigma[None], cross[None])


def solution(mesh):
    in_specs = (P("tm", "rows", None), P("tm", "rows", None), P("rows", None), P())
    out_specs = (P("tm", "rows", None), P("tm", "rows", None))
    return jax.shard_map(shards, mesh=mesh, in_specs=in_specs, out_specs=out_specs, check_vma=False)
```

```python
import jax
import jax.numpy as jnp
from jax import lax
from jax.experimental import pallas as pl
from jax.experimental.pallas import tpu as pltpu
from jax.sharding import PartitionSpec as P

MESH = pl.DeviceIdType.MESH
BF16 = jnp.bfloat16
F32 = jnp.float32
B = 1536
CHIPS = 32
HALF_CHIPS = 16
PANEL = 48
OWN = 24
HALF = 768
WINDOW = 256
SPLIT = 4
STEP = 384
LEFT = 1152


def dot(a, b):
    return jnp.dot(a, b, preferred_element_type=F32)


def message(product, j):
    start = PANEL * j
    tile, off = start // 128, start % 128
    lanes = lax.broadcasted_iota(jnp.int32, (PANEL, 128), 1)
    block = product[:, tile * 128:(tile + 1) * 128]
    if off:
        block = pltpu.roll(block, 128 - off, 1)
        if off + PANEL > 128:
            after = pltpu.roll(product[:, (tile + 1) * 128:(tile + 2) * 128], 128 - off, 1)
            block = jnp.where(lanes < 128 - off, block, after)
    top = jnp.where(lanes[:16] < 64, block[:16], pltpu.roll(block[16:32], 64, 1))
    return jnp.concatenate([top, block[32:48]], axis=0).astype(BF16)


class Ring:
    later = (1, 2)

    def __init__(self, lower, weight, sems, p, y, x, core, place, source):
        self.lower, self.weight = lower, weight
        self.sends, self.receives, self.over = sems
        self.p, self.y, self.x, self.core = p, y, x, core
        self.place, self.source = place, source
        self.sign = 1 - 2 * core

    def block(self, slot, kind, pair):
        if kind == 1:
            return self.weight.at[HALF_CHIPS * self.core + slot, :, :STEP * (pair + 1)]
        return self.lower.at[slot, :, slice(0, LEFT) if kind == 0 else slice(LEFT, B)]

    def copy(self, slot, kind, pair, way, y, x):
        block = self.block(slot, kind, pair)
        return pltpu.make_async_remote_copy(
            src_ref=block, dst_ref=block, send_sem=self.sends.at[self.sender(slot, kind, way)],
            recv_sem=self.receives.at[slot, kind],
            device_id=(self.p, (y * 4 + x) * 2 + self.core), device_id_type=MESH)

    def sender(self, slot, kind, way):
        if kind:
            return 35 + 20 * (kind - 1) + 5 * (slot // 4) + way
        return 2 * slot + way if way < 2 else 30 + way

    def along_x(self, slot, kind, pair, way):
        return self.copy(slot, kind, pair, 1 + way, self.y, (self.x + way) % 4)

    def along_y(self, slot, kind, pair, back):
        step = self.turn(slot, kind) * (-1 if back else 1)
        return self.copy(slot, kind, pair, back, (self.y + step + 8) % 8, self.x)

    def turn(self, slot, kind):
        return self.sign * (1 - 2 * (slot % 2)) if kind == 0 else self.sign

    def across(self, block):
        chip = self.y * 4 + self.x
        return pltpu.make_async_remote_copy(
            src_ref=block, dst_ref=block, send_sem=self.over.at[0], recv_sem=self.over.at[1],
            device_id=(self.p, chip * 2 + 1 - self.core), device_id_type=MESH)

    def cross(self, slot, kind, pair):
        if kind == 1:
            self.across(self.block(slot, kind, pair)).start()

    def arrived(self, slot, kind, pair):
        self.along_x(slot, kind, pair, 1).wait_recv()

    def of_row(self, origin, act):
        for pair in range(4):
            @pl.when(jnp.logical_and(origin // 2 == pair, self.core == pair // 2))
            def _():
                act(pair)

    def spread(self, act, slot, kind, pair, first):
        for way in (1, 3, 2):
            act(self.along_x(slot, kind, pair, way))
        if first:
            self.cross(slot, kind, pair)

    def round_y(self, act, slot, kind, pair):
        act(self.along_y(slot, kind, pair, 0))
        act(self.along_y(slot, kind, pair, 1))

    def own_sends(self, act, first):
        def begin(pair):
            for kind in self.later:
                self.round_y(act, self.place, kind, pair)

        def go_on(pair):
            for kind in self.later:
                self.spread(act, self.place, kind, pair, first)

        self.spread(act, self.place, 0, None, False)
        self.of_row(self.y, begin)
        self.round_y(act, self.place, 0, None)
        self.of_row(self.y, go_on)

    def row_sends(self, act, wait):
        for around in (1, 3, 2):
            slot = (self.y % 4) * 4 + (self.x + around) % 4
            if wait:
                self.arrived(slot, 0, None)
            self.round_y(act, slot, 0, None)

    def lower_hop(self, act, wait, distance, odd):
        columns = [(self.x + odd) % 4, (self.x + odd + 2) % 4]
        for back in range(2 if distance < 4 else 1):
            step = self.turn(columns[0], 0) * distance * (1 if back else -1)
            origin = (self.y + step + 8) % 8

            @pl.when(origin // 4 == self.core)
            def _():
                for column in columns:
                    slot = (origin % 4) * 4 + column
                    if wait:
                        self.arrived(slot, 0, None)
                    if distance < (3 if back else 4):
                        act(self.along_y(slot, 0, None, back))

    def weight_hop(self, act, wait, distance):
        for back in range(2 if distance < 4 else 1):
            origin = (self.y + self.sign * distance * (1 if back else -1) + 8) % 8
            slot = (origin % 4) * 4 + self.x

            def pass_on(pair):
                for kind in self.later:
                    if wait:
                        self.arrived(slot, kind, pair)
                    if distance < (3 if back else 4):
                        act(self.along_y(slot, kind, pair, back))
                    self.spread(act, slot, kind, pair, wait)

            self.of_row(origin, pass_on)

    def last_along_x(self):
        for s in range(4):
            def end(pair):
                for way in (1, 3, 2):
                    slot = s * 4 + (self.x + way) % 4
                    for kind in self.later:
                        self.arrived(slot, kind, pair)
                        self.cross(slot, kind, pair)

            self.of_row(4 * self.core + s, end)

    def both_ways(self, act):
        lower_rows = self.weight.at[:6]
        upper_rows = self.weight.at[:14]

        @pl.when(self.core == 0)
        def _():
            act(self.across(lower_rows), self.across(upper_rows))

        @pl.when(self.core == 1)
        def _():
            act(self.across(upper_rows), self.across(lower_rows))

    def walk(self, act, wait):
        @pl.when(self.source)
        def _():
            self.own_sends(act, wait)
            self.row_sends(act, wait)

        self.weight_hop(act, wait, 1)
        self.weight_hop(act, wait, 2)
        self.lower_hop(act, wait, 1, 0)
        self.lower_hop(act, wait, 1, 1)
        self.weight_hop(act, wait, 3)
        self.lower_hop(act, wait, 2, 0)
        self.lower_hop(act, wait, 2, 1)
        self.weight_hop(act, wait, 4)
        self.lower_hop(act, wait, 3, 0)
        self.lower_hop(act, wait, 3, 1)

    def run(self, arrived):
        self.walk(lambda copy: copy.start(), True)
        self.last_along_x()
        arrived()
        self.lower_hop(None, True, 4, 0)
        self.lower_hop(None, True, 4, 1)

    def finish(self):
        self.walk(lambda copy: copy.wait_send(), False)


class PlainRing(Ring):
    later = (1,)

    def __init__(self, held, sems, p, y, x, core, place, source):
        super().__init__(held, held, sems + (None,), p, y, x, core, place, source)

    def block(self, slot, kind, pair):
        return self.lower.at[slot, :, HALF * kind:HALF * (kind + 1)]

    def cross(self, slot, kind, pair):
        pass

    def of_row(self, origin, act):
        @pl.when(origin // 4 == self.core)
        def _():
            act(None)


def chain(
    flag_ref, weight_hbm, lower_hbm, end_hbm, sigma_ref, cross_ref,
    weight_rows, lower_rows, end_ref, weight_ref, lower_ref, coupled_ref,
    through_ref, through_in, through_out, first_sigma, cross_part, cross_in,
    rows_there, rows_here, gram_buf, end_buf, next_buf, next_out,
    part_out, part_in, part2_out, part2_in, pack, recv, rows_out,
    load_sem, here_sem, ring_send, ring_recv, across_sem,
    through_recv, through_sem, through_hop, ahead_sem,
    end_sem, next_sem, part_sem, part2_sem, rows_sem, pack_sem,
):
    parts = 8
    p = lax.axis_index("tm")
    r = lax.axis_index("rows")
    chip, core = r // 2, r % 2
    half = chip // HALF_CHIPS
    place = chip % HALF_CHIPS
    y, x = chip // 4, chip % 4
    source_core = core == half
    sibling = (p, chip * 2 + 1 - core)

    def peer(j):
        return (p, (core * HALF_CHIPS + j) * 2 + half)

    loads = [
        pltpu.make_async_copy(src, dst, load_sem.at[k])
        for k, (src, dst) in enumerate(
            ((lower_hbm, lower_rows), (weight_hbm, weight_rows), (end_hbm, end_ref)))
    ]
    for load in loads:
        load.start()
    barrier = pltpu.get_barrier_semaphore()
    pl.semaphore_signal(barrier, 1, device_id=sibling, device_id_type=MESH)

    @pl.when(p > 0)
    def _():
        pl.semaphore_signal(barrier, 1, device_id=(p - 1, r), device_id_type=MESH)

    @pl.when(p < parts - 1)
    def _():
        pl.semaphore_signal(barrier, 1, device_id=(p + 1, r), device_id_type=MESH)

    def is_self(j):
        return jnp.logical_and(core == half, place == j)

    for around in (1, 7):
        there = ((y + around) % 8) * 4 + x
        pl.semaphore_signal(
            barrier, 1, device_id=(p, there * 2 + core), device_id_type=MESH)
    for around in (1, 2, 3):
        there = y * 4 + (x + around) % 4
        pl.semaphore_signal(
            barrier, 1, device_id=(p, there * 2 + core), device_id_type=MESH)

    @pl.when(p < SPLIT - 1)
    def _():
        pl.semaphore_signal(barrier, 1, device_id=(SPLIT, r), device_id_type=MESH)

    expected = (
        6 + jnp.where(p > 0, 1, 0) + jnp.where(p < parts - 1, 1, 0)
        + jnp.where(p == SPLIT, SPLIT - 1, 0))
    for pair in range(3):
        weight_ref[8 * pair:8 * pair + 8, :, STEP * (pair + 1):] = jnp.zeros(
            (8, PANEL, B - STEP * (pair + 1)), BF16)
    for load in loads:
        load.wait()
    rows_here[0] = lower_rows[...].astype(F32)
    rows_here[1] = weight_rows[...].astype(F32)
    pl.semaphore_wait(barrier, expected)

    mine = pl.ds(pl.multiple_of(core * HALF, 128), HALF)
    theirs = pl.ds(pl.multiple_of((1 - core) * HALF, 128), HALF)
    my_rows = pl.ds(pl.multiple_of(core * OWN, 8), OWN)
    their_rows = pl.ds(pl.multiple_of((1 - core) * OWN, 8), OWN)

    def to_sibling(src, dst, sems):
        return pltpu.make_async_remote_copy(
            src_ref=src, dst_ref=dst, send_sem=sems.at[0], recv_sem=sems.at[1],
            device_id=sibling, device_id_type=MESH)

    here_copy = to_sibling(rows_here, rows_there, here_sem)

    @pl.when(jnp.logical_not(source_core))
    def _():
        here_copy.start()

    end_copy = to_sibling(end_ref.at[:, theirs], end_buf.at[my_rows], end_sem)
    end_copy.start()
    end_buf[my_rows] = end_ref[:, mine]
    ring = Ring(
        lower_ref, weight_ref, (ring_send, ring_recv, across_sem),
        p, y, x, core, place, source_core)

    @pl.when(source_core)
    def _():
        here_copy.wait_recv()
        for which, there in ((0, rows_there[0]), (1, rows_there[1])):
            ours = rows_here[which]
            low = jnp.where(core == 0, ours, there)
            high = jnp.where(core == 0, there, ours)
            both = jnp.concatenate([low, high], axis=0).astype(BF16)
            if which == 0:
                lower_ref[place] = both
            else:
                weight_ref[chip] = both

    def couple(s):
        rows = pl.ds(4 * s, 4)
        left = lower_ref[rows, :, :HALF].reshape(4 * PANEL, HALF)
        right = lower_ref[rows, :, HALF:].reshape(4 * PANEL, HALF)
        for k in range(B // WINDOW):
            columns = slice(WINDOW * k, WINDOW * (k + 1))
            total = dot(right, weight_ref[HALF_CHIPS:, :, columns].reshape(HALF, WINDOW))
            if k < HALF // WINDOW:
                total = total + dot(
                    left, weight_ref[:HALF_CHIPS, :, columns].reshape(HALF, WINDOW))
            coupled_ref[rows, :, columns] = total.astype(BF16).reshape(4, PANEL, WINDOW)

    def couple_near():
        ring.both_ways(lambda ours, others: others.wait_recv())

        @pl.loop(1, 4)
        def _(i):
            couple((y + i) % 4)

    ring.run(couple_near)
    couple(y % 4)

    def ring_sent():
        ring.both_ways(lambda ours, others: ours.wait_send())
        ring.finish()

    end_copy.wait_recv()
    end_b = end_buf[...].astype(BF16)
    broken = flag_ref[p] == 1
    early = p < SPLIT

    def down(src, dst, send, receive, target):
        return pltpu.make_async_remote_copy(
            src_ref=src, dst_ref=dst, send_sem=send, recv_sem=receive,
            device_id=(target, r), device_id_type=MESH)

    below = jnp.maximum(p - 1, 0)
    hops = [
        down(next_out.at[0], next_buf.at[0], next_sem.at[0, 0], next_sem.at[0, 1], below),
        None,
        down(next_out.at[1], next_buf.at[2], next_sem.at[2, 0], next_sem.at[2, 1], below),
    ]
    jumps = [
        down(next_out.at[0], next_buf.at[1], ahead_sem.at[q], next_sem.at[1, 1], q)
        for q in range(SPLIT)
    ]
    through_copy = down(
        through_out, through_in, through_hop.at[0], through_hop.at[1], below)

    def sum_halves(k, source, right_ref):
        copy = to_sibling(part_out.at[k], part_in.at[k], part_sem.at[k])
        part_out[k] = dot(source, right_ref[:, :, theirs].reshape(HALF, HALF))
        copy.start()
        own = dot(source, right_ref[:, :, mine].reshape(HALF, HALF))
        copy.wait_recv()
        return own + part_in[k]

    def pack_copy(k, j):
        return pltpu.make_async_remote_copy(
            src_ref=pack.at[k, j], dst_ref=recv.at[k, place], send_sem=pack_sem.at[k, 0],
            recv_sem=pack_sem.at[k, 1], device_id=peer(j), device_id_type=MESH)

    def messages(k, act):
        def count(n):
            return pltpu.make_async_remote_copy(
                src_ref=pack.at[k, :n], dst_ref=recv.at[k, :n], send_sem=pack_sem.at[k, 0],
                recv_sem=pack_sem.at[k, 1], device_id=sibling, device_id_type=MESH)

        @pl.when(source_core)
        def _():
            act(count(HALF_CHIPS - 1))

        @pl.when(jnp.logical_not(source_core))
        def _():
            act(count(HALF_CHIPS))

    def emit(which, value, out_ref, act):
        copy = to_sibling(
            rows_out.at[which, their_rows], out_ref.at[:, mine], rows_sem.at[which])
        if act == "start":
            rows_out[which] = value
            copy.start()
            out_ref[:, mine] = rows_out[which, my_rows]
        else:
            copy.wait()

    def step(k, source, right_ref, meanwhile):
        product = sum_halves(k, source, right_ref)
        for j in range(HALF_CHIPS):
            pack[k, j] = message(product, j)

        for j in range(HALF_CHIPS):
            @pl.when(jnp.logical_not(is_self(j)))
            def _():
                pack_copy(k, j).start()

        @pl.when(source_core)
        def _():
            recv[k, place] = pack[k, place]

        base = meanwhile(product)
        messages(k, lambda copy: copy.wait_recv())
        first = recv[k, :, :16].reshape(HALF_CHIPS * 16, 128).T
        second = recv[k, :, 16:].reshape(HALF_CHIPS * 16, 128).T

        def update(columns):
            def rows(i):
                return right_ref[:, 16 * i:16 * i + 16, columns].reshape(HALF_CHIPS * 16, HALF)
            total = dot(first[:48], rows(0)) + dot(first[64:112], rows(1))
            total = total + dot(second[:48], rows(2))
            return total if base is None else total + base(columns)

        copy = to_sibling(part2_out.at[k], part2_in.at[k], part2_sem.at[k])
        part2_out[k] = update(theirs)
        copy.start()
        sigma = update(mine)
        copy.wait_recv()
        return sigma + part2_in[k]

    through_ring = PlainRing(
        through_ref, (ring_send, through_recv), p, y, x, core, place, source_core)
    through_half = to_sibling(through_out, through_out, through_sem.at[0])
    through_here = to_sibling(through_out, through_ref.at[place, :, mine], through_sem.at[1])
    zero = jnp.zeros((PANEL, HALF), BF16)

    @pl.when(p == SPLIT - 1)
    def _():
        @pl.when(source_core)
        def _():
            next_out[1] = jnp.where(broken, zero, coupled_ref[place, :, theirs])
            half_copy = to_sibling(next_out.at[1], through_out, through_sem.at[0])
            half_copy.start()
            through_out[...] = jnp.where(broken, zero, coupled_ref[place, :, mine])
            half_copy.wait_send()

        @pl.when(jnp.logical_not(source_core))
        def _():
            through_half.wait_recv()

        through_copy.start()

        @pl.loop(0, HALF_CHIPS)
        def _(j):
            rows = coupled_ref[j]
            through_ref[j] = jnp.where(broken, jnp.zeros_like(rows), rows)

    @pl.when(p < SPLIT - 1)
    def _():
        through_copy.wait_recv()
        rows = sum_halves(2, through_in[...], coupled_ref).astype(BF16)
        through_out[...] = jnp.where(broken, zero, rows)

        @pl.when(p > 0)
        def _():
            through_copy.start()

        @pl.when(source_core)
        def _():
            through_ref[place, :, mine] = through_out[...]

        @pl.when(jnp.logical_not(source_core))
        def _():
            through_here.start()

    def gather_through():
        ring_sent()

        @pl.when(source_core)
        def _():
            to_sibling(through_out, through_ref.at[place, :, theirs], through_sem.at[1]).wait_recv()

        through_ring.run(lambda: None)

    @pl.when(p < SPLIT - 2)
    def _():
        gather_through()

    has_above = jnp.logical_and(p != parts - 1, p != SPLIT - 1)

    @pl.when(has_above)
    def _():
        hops[0].wait_recv()

    @pl.when(jnp.logical_not(has_above))
    def _():
        next_buf[0] = zero

    use_end = jnp.logical_or(broken, p == parts - 1)

    def settle(product):
        @pl.when(p < SPLIT - 1)
        def _():
            through_ring.finish()

        @pl.when(p == SPLIT - 1)
        def _():
            ring_sent()

    def gram(product):
        window = jnp.minimum(chip * PANEL // 128, (B - WINDOW) // 128) * 128
        chips = pl.ds(core * HALF_CHIPS, HALF_CHIPS)
        own = weight_ref[chips, :, pl.ds(pl.multiple_of(window, 128), WINDOW)]
        own = own.reshape(HALF, WINDOW).T
        for k in range(B // WINDOW):
            columns = slice(WINDOW * k, WINDOW * (k + 1))
            gram_buf[:, columns] = dot(own, weight_ref[chips, :, columns].reshape(HALF, WINDOW))
        gram_rows = pl.ds(pl.multiple_of(chip * PANEL - window, 16), PANEL)

        @pl.when(jnp.logical_not(early))
        def _():
            emit(0, -product, cross_ref, "start")

        return lambda columns: gram_buf[gram_rows, columns]

    sigma = step(0, jnp.where(use_end, end_b, next_buf[0]), coupled_ref, gram)
    next_out[0] = sigma.astype(BF16)
    sends_down = jnp.logical_and(p > 0, p != SPLIT)

    @pl.when(sends_down)
    def _():
        hops[0].start()

    @pl.when(p == SPLIT)
    def _():
        for q in (1, 2, 3, 0):
            jumps[q].start()

    @pl.when(jnp.logical_not(early))
    def _():
        emit(1, sigma, sigma_ref, "start")

    @pl.when(early)
    def _():
        first_sigma[...] = sigma

        @pl.when(p == SPLIT - 2)
        def _():
            gather_through()

        jumps[0].wait_recv()
        whole = first_sigma[...] + step(1, next_buf[1], through_ref, settle)
        next_out[1] = whole.astype(BF16)

        @pl.when(p > 0)
        def _():
            hops[2].start()

        emit(1, whole, sigma_ref, "start")

        @pl.when(p < SPLIT - 1)
        def _():
            hops[2].wait_recv()

        @pl.when(p == SPLIT - 1)
        def _():
            next_buf[2] = next_buf[1]

        source = jnp.where(broken, end_b, next_buf[2])
        for k in range(2):
            columns = slice(HALF * k, HALF * (k + 1))
            cross_part[:, columns] = -dot(
                source, coupled_ref[:, :, columns].reshape(HALF, HALF))
        cross_copy = to_sibling(cross_part.at[their_rows], cross_in, rows_sem.at[0])
        cross_copy.start()
        cross_copy.wait_recv()
        cross_ref[...] = cross_part[my_rows] + cross_in[...]

    end_copy.wait_send()

    @pl.when(jnp.logical_not(source_core))
    def _():
        here_copy.wait_send()

    def sent(k):
        to_sibling(part_out.at[k], part_in.at[k], part_sem.at[k]).wait_send()

    def step_sent(k):
        sent(k)
        to_sibling(part2_out.at[k], part2_in.at[k], part2_sem.at[k]).wait_send()
        messages(k, lambda copy: copy.wait_send())

    step_sent(0)

    @pl.when(sends_down)
    def _():
        hops[0].wait_send()

    @pl.when(p == SPLIT)
    def _():
        for jump in jumps:
            jump.wait_send()

    @pl.when(early)
    def _():
        step_sent(1)
        to_sibling(cross_part.at[their_rows], cross_in, rows_sem.at[0]).wait_send()

        @pl.when(p > 0)
        def _():
            through_copy.wait_send()
            hops[2].wait_send()

    @pl.when(p < SPLIT - 1)
    def _():
        sent(2)

        @pl.when(jnp.logical_not(source_core))
        def _():
            through_here.wait_send()

    @pl.when(jnp.logical_not(early))
    def _():
        ring_sent()
        emit(0, None, cross_ref, "wait")

    emit(1, None, sigma_ref, "wait")


def run_chain(flag, weight, lower, end):
    vmem = pl.BlockSpec(memory_space=pltpu.VMEM)
    dma = pltpu.SemaphoreType.DMA
    return pl.pallas_call(
        chain,
        out_shape=[jax.ShapeDtypeStruct((OWN, B), F32)] * 2,
        in_specs=[pl.BlockSpec(memory_space=pltpu.SMEM)] + [pl.BlockSpec(memory_space=pl.ANY)] * 3,
        out_specs=[vmem, vmem],
        scratch_shapes=[
            pltpu.VMEM((OWN, B), BF16),
            pltpu.VMEM((OWN, B), BF16),
            pltpu.VMEM((OWN, B), F32),
            pltpu.VMEM((CHIPS, PANEL, B), BF16),
            pltpu.VMEM((HALF_CHIPS, PANEL, B), BF16),
            pltpu.VMEM((HALF_CHIPS, PANEL, B), BF16),
            pltpu.VMEM((HALF_CHIPS, PANEL, B), BF16),
            pltpu.VMEM((PANEL, HALF), BF16),
            pltpu.VMEM((PANEL, HALF), BF16),
            pltpu.VMEM((PANEL, HALF), F32),
            pltpu.VMEM((PANEL, B), F32),
            pltpu.VMEM((OWN, B), F32),
            pltpu.VMEM((2, OWN, B), F32),
            pltpu.VMEM((2, OWN, B), F32),
            pltpu.VMEM((WINDOW, B), F32),
            pltpu.VMEM((PANEL, HALF), F32),
            pltpu.VMEM((3, PANEL, HALF), BF16),
            pltpu.VMEM((2, PANEL, HALF), BF16),
            pltpu.VMEM((3, PANEL, HALF), F32),
            pltpu.VMEM((3, PANEL, HALF), F32),
            pltpu.VMEM((2, PANEL, HALF), F32),
            pltpu.VMEM((2, PANEL, HALF), F32),
            pltpu.VMEM((2, HALF_CHIPS, 32, 128), BF16),
            pltpu.VMEM((2, HALF_CHIPS, 32, 128), BF16),
            pltpu.VMEM((2, PANEL, HALF), F32),
            dma((3,)), dma((2,)), dma((75,)), dma((HALF_CHIPS, 3)), dma((2,)),
            dma((HALF_CHIPS, 2)), dma((2, 2)), dma((2,)), dma((SPLIT,)),
            dma((2,)), dma((3, 2)), dma((3, 2)), dma((2, 2)), dma((2, 2)), dma((2, 2)),
        ],
        compiler_params=pltpu.CompilerParams(
            collective_id=0, has_side_effects=True, vmem_limit_bytes=40 * 1024 * 1024),
    )(flag, weight, lower, end)


def shards(w_inv, lower_block, sigma_end, chain_break):
    sigma, cross = run_chain(chain_break, w_inv[0], lower_block[0], sigma_end)
    return (sigma[None], cross[None])


def solution(mesh):
    in_specs = (P("tm", "rows", None), P("tm", "rows", None), P("rows", None), P())
    out_specs = (P("tm", "rows", None), P("tm", "rows", None))
    return jax.shard_map(shards, mesh=mesh, in_specs=in_specs, out_specs=out_specs, check_vma=False)
```

```python
import jax
import jax.numpy as jnp
from jax import lax
from jax.experimental import pallas as pl
from jax.experimental.pallas import tpu as pltpu
from jax.sharding import PartitionSpec as P

MESH = pl.DeviceIdType.MESH
BF16 = jnp.bfloat16
F32 = jnp.float32
B = 1536
CHIPS = 32
HALF_CHIPS = 16
PANEL = 48
OWN = 24
HALF = 768
WINDOW = 256
SPLIT = 4
STEP = 384
LEFT = 1152


def dot(a, b):
    return jnp.dot(a, b, preferred_element_type=F32)


def message(product, j):
    start = PANEL * j
    tile, off = start // 128, start % 128
    lanes = lax.broadcasted_iota(jnp.int32, (PANEL, 128), 1)
    block = product[:, tile * 128:(tile + 1) * 128]
    if off:
        block = pltpu.roll(block, 128 - off, 1)
        if off + PANEL > 128:
            after = pltpu.roll(product[:, (tile + 1) * 128:(tile + 2) * 128], 128 - off, 1)
            block = jnp.where(lanes < 128 - off, block, after)
    top = jnp.where(lanes[:16] < 64, block[:16], pltpu.roll(block[16:32], 64, 1))
    return jnp.concatenate([top, block[32:48]], axis=0).astype(BF16)


class Ring:
    later = (1, 2)

    def __init__(self, lower, weight, sems, p, y, x, core, place, source):
        self.lower, self.weight = lower, weight
        self.sends, self.receives, self.over = sems
        self.p, self.y, self.x, self.core = p, y, x, core
        self.place, self.source = place, source
        self.sign = 1 - 2 * core

    def block(self, slot, kind, pair):
        if kind == 1:
            return self.weight.at[HALF_CHIPS * self.core + slot, :, :STEP * (pair + 1)]
        return self.lower.at[slot, :, slice(0, LEFT) if kind == 0 else slice(LEFT, B)]

    def copy(self, slot, kind, pair, way, y, x):
        block = self.block(slot, kind, pair)
        return pltpu.make_async_remote_copy(
            src_ref=block, dst_ref=block, send_sem=self.sends.at[self.sender(slot, kind, way)],
            recv_sem=self.receives.at[slot, kind],
            device_id=(self.p, (y * 4 + x) * 2 + self.core), device_id_type=MESH)

    def sender(self, slot, kind, way):
        if kind:
            return 35 + 20 * (kind - 1) + 5 * (slot // 4) + way
        return 2 * slot + way if way < 2 else 30 + way

    def along_x(self, slot, kind, pair, way):
        return self.copy(slot, kind, pair, 1 + way, self.y, (self.x + way) % 4)

    def along_y(self, slot, kind, pair, back):
        step = self.turn(slot, kind) * (-1 if back else 1)
        return self.copy(slot, kind, pair, back, (self.y + step + 8) % 8, self.x)

    def turn(self, slot, kind):
        return self.sign * (1 - 2 * (slot % 2)) if kind == 0 else self.sign

    def across(self, block):
        chip = self.y * 4 + self.x
        return pltpu.make_async_remote_copy(
            src_ref=block, dst_ref=block, send_sem=self.over.at[0], recv_sem=self.over.at[1],
            device_id=(self.p, chip * 2 + 1 - self.core), device_id_type=MESH)

    def cross(self, slot, kind, pair):
        if kind == 1:
            self.across(self.block(slot, kind, pair)).start()

    def arrived(self, slot, kind, pair):
        self.along_x(slot, kind, pair, 1).wait_recv()

    def of_row(self, origin, act):
        for pair in range(4):
            @pl.when(jnp.logical_and(origin // 2 == pair, self.core == pair // 2))
            def _():
                act(pair)

    def spread(self, act, slot, kind, pair, first):
        for way in (1, 3, 2):
            act(self.along_x(slot, kind, pair, way))
        if first:
            self.cross(slot, kind, pair)

    def round_y(self, act, slot, kind, pair):
        act(self.along_y(slot, kind, pair, 0))
        act(self.along_y(slot, kind, pair, 1))

    def own_sends(self, act, first):
        def begin(pair):
            for kind in self.later:
                self.round_y(act, self.place, kind, pair)

        def go_on(pair):
            for kind in self.later:
                self.spread(act, self.place, kind, pair, first)

        self.spread(act, self.place, 0, None, False)
        self.of_row(self.y, begin)
        self.round_y(act, self.place, 0, None)
        self.of_row(self.y, go_on)

    def row_sends(self, act, wait):
        for around in (1, 3, 2):
            slot = (self.y % 4) * 4 + (self.x + around) % 4
            if wait:
                self.arrived(slot, 0, None)
            self.round_y(act, slot, 0, None)

    def lower_hop(self, act, wait, distance, odd):
        columns = [(self.x + odd) % 4, (self.x + odd + 2) % 4]
        for back in range(2 if distance < 4 else 1):
            step = self.turn(columns[0], 0) * distance * (1 if back else -1)
            origin = (self.y + step + 8) % 8

            @pl.when(origin // 4 == self.core)
            def _():
                for column in columns:
                    slot = (origin % 4) * 4 + column
                    if wait:
                        self.arrived(slot, 0, None)
                    if distance < (3 if back else 4):
                        act(self.along_y(slot, 0, None, back))

    def weight_hop(self, act, wait, distance):
        for back in range(2 if distance < 4 else 1):
            origin = (self.y + self.sign * distance * (1 if back else -1) + 8) % 8
            slot = (origin % 4) * 4 + self.x

            def pass_on(pair):
                for kind in self.later:
                    if wait:
                        self.arrived(slot, kind, pair)
                    if distance < (3 if back else 4):
                        act(self.along_y(slot, kind, pair, back))
                    self.spread(act, slot, kind, pair, wait)

            self.of_row(origin, pass_on)

    def last_along_x(self):
        for s in range(4):
            def end(pair):
                for way in (1, 3, 2):
                    slot = s * 4 + (self.x + way) % 4
                    for kind in self.later:
                        self.arrived(slot, kind, pair)
                        self.cross(slot, kind, pair)

            self.of_row(4 * self.core + s, end)

    def both_ways(self, act):
        lower_rows = self.weight.at[:6]
        upper_rows = self.weight.at[:14]

        @pl.when(self.core == 0)
        def _():
            act(self.across(lower_rows), self.across(upper_rows))

        @pl.when(self.core == 1)
        def _():
            act(self.across(upper_rows), self.across(lower_rows))

    def walk(self, act, wait):
        @pl.when(self.source)
        def _():
            self.own_sends(act, wait)
            self.row_sends(act, wait)

        self.weight_hop(act, wait, 1)
        self.weight_hop(act, wait, 2)
        self.lower_hop(act, wait, 1, 0)
        self.lower_hop(act, wait, 1, 1)
        self.weight_hop(act, wait, 3)
        self.lower_hop(act, wait, 2, 0)
        self.lower_hop(act, wait, 2, 1)
        self.weight_hop(act, wait, 4)
        self.lower_hop(act, wait, 3, 0)
        self.lower_hop(act, wait, 3, 1)

    def run(self, arrived):
        self.walk(lambda copy: copy.start(), True)
        self.last_along_x()
        arrived()
        self.lower_hop(None, True, 4, 0)
        self.lower_hop(None, True, 4, 1)

    def finish(self):
        self.walk(lambda copy: copy.wait_send(), False)


class PlainRing(Ring):
    later = (1,)

    def __init__(self, held, sems, p, y, x, core, place, source):
        super().__init__(held, held, sems + (None,), p, y, x, core, place, source)

    def block(self, slot, kind, pair):
        return self.lower.at[slot, :, HALF * kind:HALF * (kind + 1)]

    def cross(self, slot, kind, pair):
        pass

    def of_row(self, origin, act):
        @pl.when(origin // 4 == self.core)
        def _():
            act(None)


def chain(
    flag_ref, weight_hbm, lower_hbm, end_hbm, sigma_ref, cross_ref,
    weight_rows, lower_rows, end_ref, weight_ref, lower_ref, coupled_ref,
    through_ref, through_in, through_out, first_sigma, cross_part, cross_in,
    rows_there, rows_here, gram_buf, end_buf, next_buf, next_out,
    part_out, part_in, part2_out, part2_in, pack, recv, rows_out,
    load_sem, here_sem, ring_send, ring_recv, across_sem,
    through_recv, through_sem, through_hop, ahead_sem,
    end_sem, next_sem, part_sem, part2_sem, rows_sem, pack_sem,
):
    parts = 8
    p = lax.axis_index("tm")
    r = lax.axis_index("rows")
    chip, core = r // 2, r % 2
    half = chip // HALF_CHIPS
    place = chip % HALF_CHIPS
    y, x = chip // 4, chip % 4
    source_core = core == half
    sibling = (p, chip * 2 + 1 - core)

    def peer(j):
        return (p, (core * HALF_CHIPS + j) * 2 + half)

    loads = [
        pltpu.make_async_copy(src, dst, load_sem.at[k])
        for k, (src, dst) in enumerate(
            ((lower_hbm, lower_rows), (weight_hbm, weight_rows), (end_hbm, end_ref)))
    ]
    for load in loads:
        load.start()
    barrier = pltpu.get_barrier_semaphore()
    pl.semaphore_signal(barrier, 1, device_id=sibling, device_id_type=MESH)

    @pl.when(p > 0)
    def _():
        pl.semaphore_signal(barrier, 1, device_id=(p - 1, r), device_id_type=MESH)

    @pl.when(p < parts - 1)
    def _():
        pl.semaphore_signal(barrier, 1, device_id=(p + 1, r), device_id_type=MESH)

    def is_self(j):
        return jnp.logical_and(core == half, place == j)

    for around in (1, 7):
        there = ((y + around) % 8) * 4 + x
        pl.semaphore_signal(
            barrier, 1, device_id=(p, there * 2 + core), device_id_type=MESH)
    for around in (1, 2, 3):
        there = y * 4 + (x + around) % 4
        pl.semaphore_signal(
            barrier, 1, device_id=(p, there * 2 + core), device_id_type=MESH)

    @pl.when(p < SPLIT - 1)
    def _():
        pl.semaphore_signal(barrier, 1, device_id=(SPLIT, r), device_id_type=MESH)

    expected = (
        6 + jnp.where(p > 0, 1, 0) + jnp.where(p < parts - 1, 1, 0)
        + jnp.where(p == SPLIT, SPLIT - 1, 0))
    for pair in range(3):
        weight_ref[8 * pair:8 * pair + 8, :, STEP * (pair + 1):] = jnp.zeros(
            (8, PANEL, B - STEP * (pair + 1)), BF16)
    for load in loads:
        load.wait()
    rows_here[0] = lower_rows[...].astype(F32)
    rows_here[1] = weight_rows[...].astype(F32)
    pl.semaphore_wait(barrier, expected)

    mine = pl.ds(pl.multiple_of(core * HALF, 128), HALF)
    theirs = pl.ds(pl.multiple_of((1 - core) * HALF, 128), HALF)
    my_rows = pl.ds(pl.multiple_of(core * OWN, 8), OWN)
    their_rows = pl.ds(pl.multiple_of((1 - core) * OWN, 8), OWN)

    def to_sibling(src, dst, sems):
        return pltpu.make_async_remote_copy(
            src_ref=src, dst_ref=dst, send_sem=sems.at[0], recv_sem=sems.at[1],
            device_id=sibling, device_id_type=MESH)

    here_copy = to_sibling(rows_here, rows_there, here_sem)

    @pl.when(jnp.logical_not(source_core))
    def _():
        here_copy.start()

    end_copy = to_sibling(end_ref.at[:, theirs], end_buf.at[my_rows], end_sem)
    end_copy.start()
    end_buf[my_rows] = end_ref[:, mine]
    ring = Ring(
        lower_ref, weight_ref, (ring_send, ring_recv, across_sem),
        p, y, x, core, place, source_core)

    @pl.when(source_core)
    def _():
        here_copy.wait_recv()
        for which, there in ((0, rows_there[0]), (1, rows_there[1])):
            ours = rows_here[which]
            low = jnp.where(core == 0, ours, there)
            high = jnp.where(core == 0, there, ours)
            both = jnp.concatenate([low, high], axis=0).astype(BF16)
            if which == 0:
                lower_ref[place] = both
            else:
                weight_ref[chip] = both

    def couple(s):
        rows = pl.ds(4 * s, 4)
        left = lower_ref[rows, :, :HALF].reshape(4 * PANEL, HALF)
        right = lower_ref[rows, :, HALF:].reshape(4 * PANEL, HALF)
        for k in range(B // HALF):
            columns = slice(HALF * k, HALF * (k + 1))
            total = dot(right, weight_ref[HALF_CHIPS:, :, columns].reshape(HALF, HALF))
            if k < HALF // HALF:
                total = total + dot(
                    left, weight_ref[:HALF_CHIPS, :, columns].reshape(HALF, HALF))
            coupled_ref[rows, :, columns] = total.astype(BF16).reshape(4, PANEL, HALF)

    def couple_near():
        ring.both_ways(lambda ours, others: others.wait_recv())

        @pl.loop(1, 4)
        def _(i):
            couple((y + i) % 4)

    ring.run(couple_near)
    couple(y % 4)

    def ring_sent():
        ring.both_ways(lambda ours, others: ours.wait_send())
        ring.finish()

    end_copy.wait_recv()
    end_b = end_buf[...].astype(BF16)
    broken = flag_ref[p] == 1
    early = p < SPLIT

    def down(src, dst, send, receive, target):
        return pltpu.make_async_remote_copy(
            src_ref=src, dst_ref=dst, send_sem=send, recv_sem=receive,
            device_id=(target, r), device_id_type=MESH)

    below = jnp.maximum(p - 1, 0)
    hops = [
        down(next_out.at[0], next_buf.at[0], next_sem.at[0, 0], next_sem.at[0, 1], below),
        None,
        down(next_out.at[1], next_buf.at[2], next_sem.at[2, 0], next_sem.at[2, 1], below),
    ]
    jumps = [
        down(next_out.at[0], next_buf.at[1], ahead_sem.at[q], next_sem.at[1, 1], q)
        for q in range(SPLIT)
    ]
    through_copy = down(
        through_out, through_in, through_hop.at[0], through_hop.at[1], below)

    def sum_halves(k, source, right_ref):
        copy = to_sibling(part_out.at[k], part_in.at[k], part_sem.at[k])
        part_out[k] = dot(source, right_ref[:, :, theirs].reshape(HALF, HALF))
        copy.start()
        own = dot(source, right_ref[:, :, mine].reshape(HALF, HALF))
        copy.wait_recv()
        return own + part_in[k]

    def pack_copy(k, j):
        return pltpu.make_async_remote_copy(
            src_ref=pack.at[k, j], dst_ref=recv.at[k, place], send_sem=pack_sem.at[k, 0],
            recv_sem=pack_sem.at[k, 1], device_id=peer(j), device_id_type=MESH)

    def messages(k, act):
        def count(n):
            return pltpu.make_async_remote_copy(
                src_ref=pack.at[k, :n], dst_ref=recv.at[k, :n], send_sem=pack_sem.at[k, 0],
                recv_sem=pack_sem.at[k, 1], device_id=sibling, device_id_type=MESH)

        @pl.when(source_core)
        def _():
            act(count(HALF_CHIPS - 1))

        @pl.when(jnp.logical_not(source_core))
        def _():
            act(count(HALF_CHIPS))

    def emit(which, value, out_ref, act):
        copy = to_sibling(
            rows_out.at[which, their_rows], out_ref.at[:, mine], rows_sem.at[which])
        if act == "start":
            rows_out[which] = value
            copy.start()
            out_ref[:, mine] = rows_out[which, my_rows]
        else:
            copy.wait()

    def step(k, source, right_ref, meanwhile):
        product = sum_halves(k, source, right_ref)
        for j in range(HALF_CHIPS):
            pack[k, j] = message(product, j)

        for j in range(HALF_CHIPS):
            @pl.when(jnp.logical_not(is_self(j)))
            def _():
                pack_copy(k, j).start()

        @pl.when(source_core)
        def _():
            recv[k, place] = pack[k, place]

        base = meanwhile(product)
        messages(k, lambda copy: copy.wait_recv())
        first = recv[k, :, :16].reshape(HALF_CHIPS * 16, 128).T
        second = recv[k, :, 16:].reshape(HALF_CHIPS * 16, 128).T

        def update(columns):
            def rows(i):
                return right_ref[:, 16 * i:16 * i + 16, columns].reshape(HALF_CHIPS * 16, HALF)
            total = dot(first[:48], rows(0)) + dot(first[64:112], rows(1))
            total = total + dot(second[:48], rows(2))
            return total if base is None else total + base(columns)

        copy = to_sibling(part2_out.at[k], part2_in.at[k], part2_sem.at[k])
        part2_out[k] = update(theirs)
        copy.start()
        sigma = update(mine)
        copy.wait_recv()
        return sigma + part2_in[k]

    through_ring = PlainRing(
        through_ref, (ring_send, through_recv), p, y, x, core, place, source_core)
    through_half = to_sibling(through_out, through_out, through_sem.at[0])
    through_here = to_sibling(through_out, through_ref.at[place, :, mine], through_sem.at[1])
    zero = jnp.zeros((PANEL, HALF), BF16)

    @pl.when(p == SPLIT - 1)
    def _():
        @pl.when(source_core)
        def _():
            next_out[1] = jnp.where(broken, zero, coupled_ref[place, :, theirs])
            half_copy = to_sibling(next_out.at[1], through_out, through_sem.at[0])
            half_copy.start()
            through_out[...] = jnp.where(broken, zero, coupled_ref[place, :, mine])
            half_copy.wait_send()

        @pl.when(jnp.logical_not(source_core))
        def _():
            through_half.wait_recv()

        through_copy.start()

        @pl.loop(0, HALF_CHIPS)
        def _(j):
            rows = coupled_ref[j]
            through_ref[j] = jnp.where(broken, jnp.zeros_like(rows), rows)

    @pl.when(p < SPLIT - 1)
    def _():
        through_copy.wait_recv()
        rows = sum_halves(2, through_in[...], coupled_ref).astype(BF16)
        through_out[...] = jnp.where(broken, zero, rows)

        @pl.when(p > 0)
        def _():
            through_copy.start()

        @pl.when(source_core)
        def _():
            through_ref[place, :, mine] = through_out[...]

        @pl.when(jnp.logical_not(source_core))
        def _():
            through_here.start()

    def gather_through():
        ring_sent()

        @pl.when(source_core)
        def _():
            to_sibling(through_out, through_ref.at[place, :, theirs], through_sem.at[1]).wait_recv()

        through_ring.run(lambda: None)

    @pl.when(p < SPLIT - 2)
    def _():
        gather_through()

    has_above = jnp.logical_and(p != parts - 1, p != SPLIT - 1)

    @pl.when(has_above)
    def _():
        hops[0].wait_recv()

    @pl.when(jnp.logical_not(has_above))
    def _():
        next_buf[0] = zero

    use_end = jnp.logical_or(broken, p == parts - 1)

    def cross_copy(k):
        columns = slice(HALF * k, HALF * (k + 1))
        return to_sibling(
            cross_part.at[their_rows, columns], cross_in.at[:, columns], rows_sem.at[2 * k])

    def settle(product):
        @pl.when(p < SPLIT - 1)
        def _():
            through_ring.finish()

        @pl.when(p == SPLIT - 1)
        def _():
            ring_sent()

    def gram(product):
        window = jnp.minimum(chip * PANEL // 128, (B - WINDOW) // 128) * 128
        chips = pl.ds(core * HALF_CHIPS, HALF_CHIPS)
        own = weight_ref[chips, :, pl.ds(pl.multiple_of(window, 128), WINDOW)]
        own = own.reshape(HALF, WINDOW).T
        for k in range(B // WINDOW):
            columns = slice(WINDOW * k, WINDOW * (k + 1))
            gram_buf[:, columns] = dot(own, weight_ref[chips, :, columns].reshape(HALF, WINDOW))
        gram_rows = pl.ds(pl.multiple_of(chip * PANEL - window, 16), PANEL)

        @pl.when(jnp.logical_not(early))
        def _():
            emit(0, -product, cross_ref, "start")

        return lambda columns: gram_buf[gram_rows, columns]

    sigma = step(0, jnp.where(use_end, end_b, next_buf[0]), coupled_ref, gram)
    next_out[0] = sigma.astype(BF16)
    sends_down = jnp.logical_and(p > 0, p != SPLIT)

    @pl.when(sends_down)
    def _():
        hops[0].start()

    @pl.when(p == SPLIT)
    def _():
        for q in (1, 2, 3, 0):
            jumps[q].start()

    @pl.when(jnp.logical_not(early))
    def _():
        emit(1, sigma, sigma_ref, "start")

    @pl.when(early)
    def _():
        first_sigma[...] = sigma

        @pl.when(p == SPLIT - 2)
        def _():
            gather_through()

        jumps[0].wait_recv()
        whole = first_sigma[...] + step(1, next_buf[1], through_ref, settle)
        next_out[1] = whole.astype(BF16)

        @pl.when(p > 0)
        def _():
            hops[2].start()

        emit(1, whole, sigma_ref, "start")

        @pl.when(p < SPLIT - 1)
        def _():
            hops[2].wait_recv()

        @pl.when(p == SPLIT - 1)
        def _():
            next_buf[2] = next_buf[1]

        source = jnp.where(broken, end_b, next_buf[2])
        for k in range(2):
            columns = slice(HALF * k, HALF * (k + 1))
            cross_part[:, columns] = -dot(
                source, coupled_ref[:, :, columns].reshape(HALF, HALF))
            cross_copy(k).start()
        for k in range(2):
            cross_copy(k).wait_recv()
        cross_ref[...] = cross_part[my_rows] + cross_in[...]

    end_copy.wait_send()

    @pl.when(jnp.logical_not(source_core))
    def _():
        here_copy.wait_send()

    def sent(k):
        to_sibling(part_out.at[k], part_in.at[k], part_sem.at[k]).wait_send()

    def step_sent(k):
        sent(k)
        to_sibling(part2_out.at[k], part2_in.at[k], part2_sem.at[k]).wait_send()
        messages(k, lambda copy: copy.wait_send())

    step_sent(0)

    @pl.when(sends_down)
    def _():
        hops[0].wait_send()

    @pl.when(p == SPLIT)
    def _():
        for jump in jumps:
            jump.wait_send()

    @pl.when(early)
    def _():
        step_sent(1)
        cross_copy(0).wait_send()
        cross_copy(1).wait_send()

        @pl.when(p > 0)
        def _():
            through_copy.wait_send()
            hops[2].wait_send()

    @pl.when(p < SPLIT - 1)
    def _():
        sent(2)

        @pl.when(jnp.logical_not(source_core))
        def _():
            through_here.wait_send()

    @pl.when(jnp.logical_not(early))
    def _():
        ring_sent()
        emit(0, None, cross_ref, "wait")

    emit(1, None, sigma_ref, "wait")


def run_chain(flag, weight, lower, end):
    vmem = pl.BlockSpec(memory_space=pltpu.VMEM)
    dma = pltpu.SemaphoreType.DMA
    return pl.pallas_call(
        chain,
        out_shape=[jax.ShapeDtypeStruct((OWN, B), F32)] * 2,
        in_specs=[pl.BlockSpec(memory_space=pltpu.SMEM)] + [pl.BlockSpec(memory_space=pl.ANY)] * 3,
        out_specs=[vmem, vmem],
        scratch_shapes=[
            pltpu.VMEM((OWN, B), BF16),
            pltpu.VMEM((OWN, B), BF16),
            pltpu.VMEM((OWN, B), F32),
            pltpu.VMEM((CHIPS, PANEL, B), BF16),
            pltpu.VMEM((HALF_CHIPS, PANEL, B), BF16),
            pltpu.VMEM((HALF_CHIPS, PANEL, B), BF16),
            pltpu.VMEM((HALF_CHIPS, PANEL, B), BF16),
            pltpu.VMEM((PANEL, HALF), BF16),
            pltpu.VMEM((PANEL, HALF), BF16),
            pltpu.VMEM((PANEL, HALF), F32),
            pltpu.VMEM((PANEL, B), F32),
            pltpu.VMEM((OWN, B), F32),
            pltpu.VMEM((2, OWN, B), F32),
            pltpu.VMEM((2, OWN, B), F32),
            pltpu.VMEM((WINDOW, B), F32),
            pltpu.VMEM((PANEL, HALF), F32),
            pltpu.VMEM((3, PANEL, HALF), BF16),
            pltpu.VMEM((2, PANEL, HALF), BF16),
            pltpu.VMEM((3, PANEL, HALF), F32),
            pltpu.VMEM((3, PANEL, HALF), F32),
            pltpu.VMEM((2, PANEL, HALF), F32),
            pltpu.VMEM((2, PANEL, HALF), F32),
            pltpu.VMEM((2, HALF_CHIPS, 32, 128), BF16),
            pltpu.VMEM((2, HALF_CHIPS, 32, 128), BF16),
            pltpu.VMEM((2, PANEL, HALF), F32),
            dma((3,)), dma((2,)), dma((75,)), dma((HALF_CHIPS, 3)), dma((2,)),
            dma((HALF_CHIPS, 2)), dma((2, 2)), dma((2,)), dma((SPLIT,)),
            dma((2,)), dma((3, 2)), dma((3, 2)), dma((2, 2)), dma((3, 2)), dma((2, 2)),
        ],
        compiler_params=pltpu.CompilerParams(
            collective_id=0, has_side_effects=True, vmem_limit_bytes=40 * 1024 * 1024),
    )(flag, weight, lower, end)


def shards(w_inv, lower_block, sigma_end, chain_break):
    sigma, cross = run_chain(chain_break, w_inv[0], lower_block[0], sigma_end)
    return (sigma[None], cross[None])


def solution(mesh):
    in_specs = (P("tm", "rows", None), P("tm", "rows", None), P("rows", None), P())
    out_specs = (P("tm", "rows", None), P("tm", "rows", None))
    return jax.shard_map(shards, mesh=mesh, in_specs=in_specs, out_specs=out_specs, check_vma=False)
```

```python
import jax
import jax.numpy as jnp
from jax import lax
from jax.experimental import pallas as pl
from jax.experimental.pallas import tpu as pltpu
from jax.sharding import PartitionSpec as P

MESH = pl.DeviceIdType.MESH
BF16 = jnp.bfloat16
F32 = jnp.float32
B = 1536
CHIPS = 32
HALF_CHIPS = 16
PANEL = 48
OWN = 24
HALF = 768
WINDOW = 256
SPLIT = 4
STEP = 384
LEFT = 1152


def dot(a, b):
    return jnp.dot(a, b, preferred_element_type=F32)


def message(product, j):
    start = PANEL * j
    tile, off = start // 128, start % 128
    lanes = lax.broadcasted_iota(jnp.int32, (PANEL, 128), 1)
    block = product[:, tile * 128:(tile + 1) * 128]
    if off:
        block = pltpu.roll(block, 128 - off, 1)
        if off + PANEL > 128:
            after = pltpu.roll(product[:, (tile + 1) * 128:(tile + 2) * 128], 128 - off, 1)
            block = jnp.where(lanes < 128 - off, block, after)
    top = jnp.where(lanes[:16] < 64, block[:16], pltpu.roll(block[16:32], 64, 1))
    return jnp.concatenate([top, block[32:48]], axis=0).astype(BF16)


class Ring:
    later = (1, 2)

    def __init__(self, lower, weight, sems, p, y, x, core, place, source):
        self.lower, self.weight = lower, weight
        self.sends, self.receives, self.over = sems
        self.p, self.y, self.x, self.core = p, y, x, core
        self.place, self.source = place, source
        self.sign = 1 - 2 * core

    def block(self, slot, kind, pair):
        if kind == 1:
            return self.weight.at[HALF_CHIPS * self.core + slot, :, :STEP * (pair + 1)]
        return self.lower.at[slot, :, slice(0, LEFT) if kind == 0 else slice(LEFT, B)]

    def copy(self, slot, kind, pair, way, y, x):
        block = self.block(slot, kind, pair)
        return pltpu.make_async_remote_copy(
            src_ref=block, dst_ref=block, send_sem=self.sends.at[self.sender(slot, kind, way)],
            recv_sem=self.receives.at[slot, kind],
            device_id=(self.p, (y * 4 + x) * 2 + self.core), device_id_type=MESH)

    def sender(self, slot, kind, way):
        if kind:
            return 35 + 20 * (kind - 1) + 5 * (slot // 4) + way
        return 2 * slot + way if way < 2 else 30 + way

    def along_x(self, slot, kind, pair, way):
        return self.copy(slot, kind, pair, 1 + way, self.y, (self.x + way) % 4)

    def along_y(self, slot, kind, pair, back):
        step = self.turn(slot, kind) * (-1 if back else 1)
        return self.copy(slot, kind, pair, back, (self.y + step + 8) % 8, self.x)

    def turn(self, slot, kind):
        return self.sign * (1 - 2 * (slot % 2)) if kind == 0 else self.sign

    def across(self, block):
        chip = self.y * 4 + self.x
        return pltpu.make_async_remote_copy(
            src_ref=block, dst_ref=block, send_sem=self.over.at[0], recv_sem=self.over.at[1],
            device_id=(self.p, chip * 2 + 1 - self.core), device_id_type=MESH)

    def cross(self, slot, kind, pair):
        if kind == 1:
            self.across(self.block(slot, kind, pair)).start()

    def arrived(self, slot, kind, pair):
        self.along_x(slot, kind, pair, 1).wait_recv()

    def of_row(self, origin, act):
        for pair in range(4):
            @pl.when(jnp.logical_and(origin // 2 == pair, self.core == pair // 2))
            def _():
                act(pair)

    def spread(self, act, slot, kind, pair, first):
        for way in (1, 3, 2):
            act(self.along_x(slot, kind, pair, way))
        if first:
            self.cross(slot, kind, pair)

    def round_y(self, act, slot, kind, pair):
        act(self.along_y(slot, kind, pair, 0))
        act(self.along_y(slot, kind, pair, 1))

    def own_sends(self, act, first):
        def begin(pair):
            for kind in self.later:
                self.round_y(act, self.place, kind, pair)

        def go_on(pair):
            for kind in self.later:
                self.spread(act, self.place, kind, pair, first)

        self.spread(act, self.place, 0, None, False)
        self.of_row(self.y, begin)
        self.round_y(act, self.place, 0, None)
        self.of_row(self.y, go_on)

    def row_sends(self, act, wait):
        for around in (1, 3, 2):
            slot = (self.y % 4) * 4 + (self.x + around) % 4
            if wait:
                self.arrived(slot, 0, None)
            self.round_y(act, slot, 0, None)

    def lower_hop(self, act, wait, distance, odd):
        columns = [(self.x + odd) % 4, (self.x + odd + 2) % 4]
        for back in range(2 if distance < 4 else 1):
            step = self.turn(columns[0], 0) * distance * (1 if back else -1)
            origin = (self.y + step + 8) % 8

            @pl.when(origin // 4 == self.core)
            def _():
                for column in columns:
                    slot = (origin % 4) * 4 + column
                    if wait:
                        self.arrived(slot, 0, None)
                    if distance < (3 if back else 4):
                        act(self.along_y(slot, 0, None, back))

    def weight_hop(self, act, wait, distance):
        for back in range(2 if distance < 4 else 1):
            origin = (self.y + self.sign * distance * (1 if back else -1) + 8) % 8
            slot = (origin % 4) * 4 + self.x

            def pass_on(pair):
                for kind in self.later:
                    if wait:
                        self.arrived(slot, kind, pair)
                    if distance < (3 if back else 4):
                        act(self.along_y(slot, kind, pair, back))
                    self.spread(act, slot, kind, pair, wait)

            self.of_row(origin, pass_on)

    def last_along_x(self):
        for s in range(4):
            def end(pair):
                for way in (1, 3, 2):
                    slot = s * 4 + (self.x + way) % 4
                    for kind in self.later:
                        self.arrived(slot, kind, pair)
                        self.cross(slot, kind, pair)

            self.of_row(4 * self.core + s, end)

    def both_ways(self, act):
        lower_rows = self.weight.at[:6]
        upper_rows = self.weight.at[:14]

        @pl.when(self.core == 0)
        def _():
            act(self.across(lower_rows), self.across(upper_rows))

        @pl.when(self.core == 1)
        def _():
            act(self.across(upper_rows), self.across(lower_rows))

    def walk(self, act, wait):
        @pl.when(self.source)
        def _():
            self.own_sends(act, wait)
            self.row_sends(act, wait)

        self.weight_hop(act, wait, 1)
        self.weight_hop(act, wait, 2)
        self.lower_hop(act, wait, 1, 0)
        self.lower_hop(act, wait, 1, 1)
        self.weight_hop(act, wait, 3)
        self.lower_hop(act, wait, 2, 0)
        self.lower_hop(act, wait, 2, 1)
        self.weight_hop(act, wait, 4)
        self.lower_hop(act, wait, 3, 0)
        self.lower_hop(act, wait, 3, 1)

    def run(self, arrived):
        self.walk(lambda copy: copy.start(), True)
        self.last_along_x()
        arrived()
        self.lower_hop(None, True, 4, 0)
        self.lower_hop(None, True, 4, 1)

    def finish(self):
        self.walk(lambda copy: copy.wait_send(), False)


class PlainRing(Ring):
    later = (1,)

    def __init__(self, held, sems, p, y, x, core, place, source):
        super().__init__(held, held, sems + (None,), p, y, x, core, place, source)

    def block(self, slot, kind, pair):
        return self.lower.at[slot, :, HALF * kind:HALF * (kind + 1)]

    def cross(self, slot, kind, pair):
        pass

    def of_row(self, origin, act):
        @pl.when(origin // 4 == self.core)
        def _():
            act(None)


def chain(
    flag_ref, weight_hbm, lower_hbm, end_hbm, sigma_ref, cross_ref,
    weight_rows, lower_rows, end_ref, weight_ref, lower_ref, coupled_ref,
    through_ref, through_in, through_out, first_sigma, cross_part, cross_in,
    rows_there, rows_here, gram_buf, end_buf, next_buf, next_out,
    part_out, part_in, part2_out, part2_in, pack, recv, rows_out,
    load_sem, here_sem, ring_send, ring_recv, across_sem,
    through_recv, through_sem, through_hop, ahead_sem,
    end_sem, next_sem, part_sem, part2_sem, rows_sem, pack_sem,
):
    parts = 8
    p = lax.axis_index("tm")
    r = lax.axis_index("rows")
    chip, core = r // 2, r % 2
    half = chip // HALF_CHIPS
    place = chip % HALF_CHIPS
    y, x = chip // 4, chip % 4
    source_core = core == half
    sibling = (p, chip * 2 + 1 - core)

    def peer(j):
        return (p, (core * HALF_CHIPS + j) * 2 + half)

    loads = [
        pltpu.make_async_copy(src, dst, load_sem.at[k])
        for k, (src, dst) in enumerate(
            ((lower_hbm, lower_rows), (weight_hbm, weight_rows), (end_hbm, end_ref)))
    ]
    for load in loads:
        load.start()
    barrier = pltpu.get_barrier_semaphore()
    pl.semaphore_signal(barrier, 1, device_id=sibling, device_id_type=MESH)

    @pl.when(p > 0)
    def _():
        pl.semaphore_signal(barrier, 1, device_id=(p - 1, r), device_id_type=MESH)

    @pl.when(p < parts - 1)
    def _():
        pl.semaphore_signal(barrier, 1, device_id=(p + 1, r), device_id_type=MESH)

    def is_self(j):
        return jnp.logical_and(core == half, place == j)

    for around in (1, 7):
        there = ((y + around) % 8) * 4 + x
        pl.semaphore_signal(
            barrier, 1, device_id=(p, there * 2 + core), device_id_type=MESH)
    for around in (1, 2, 3):
        there = y * 4 + (x + around) % 4
        pl.semaphore_signal(
            barrier, 1, device_id=(p, there * 2 + core), device_id_type=MESH)

    @pl.when(p < SPLIT - 1)
    def _():
        pl.semaphore_signal(barrier, 1, device_id=(SPLIT, r), device_id_type=MESH)

    expected = (
        6 + jnp.where(p > 0, 1, 0) + jnp.where(p < parts - 1, 1, 0)
        + jnp.where(p == SPLIT, SPLIT - 1, 0))
    for pair in range(3):
        weight_ref[8 * pair:8 * pair + 8, :, STEP * (pair + 1):] = jnp.zeros(
            (8, PANEL, B - STEP * (pair + 1)), BF16)
    for load in loads:
        load.wait()
    rows_here[0] = lower_rows[...].astype(F32)
    rows_here[1] = weight_rows[...].astype(F32)
    pl.semaphore_wait(barrier, expected)

    mine = pl.ds(pl.multiple_of(core * HALF, 128), HALF)
    theirs = pl.ds(pl.multiple_of((1 - core) * HALF, 128), HALF)
    my_rows = pl.ds(pl.multiple_of(core * OWN, 8), OWN)
    their_rows = pl.ds(pl.multiple_of((1 - core) * OWN, 8), OWN)

    def to_sibling(src, dst, sems):
        return pltpu.make_async_remote_copy(
            src_ref=src, dst_ref=dst, send_sem=sems.at[0], recv_sem=sems.at[1],
            device_id=sibling, device_id_type=MESH)

    here_copy = to_sibling(rows_here, rows_there, here_sem)

    @pl.when(jnp.logical_not(source_core))
    def _():
        here_copy.start()

    end_copy = to_sibling(end_ref.at[:, theirs], end_buf.at[my_rows], end_sem)
    end_copy.start()
    end_buf[my_rows] = end_ref[:, mine]
    ring = Ring(
        lower_ref, weight_ref, (ring_send, ring_recv, across_sem),
        p, y, x, core, place, source_core)

    @pl.when(source_core)
    def _():
        here_copy.wait_recv()
        for which, there in ((0, rows_there[0]), (1, rows_there[1])):
            ours = rows_here[which]
            low = jnp.where(core == 0, ours, there)
            high = jnp.where(core == 0, there, ours)
            both = jnp.concatenate([low, high], axis=0).astype(BF16)
            if which == 0:
                lower_ref[place] = both
            else:
                weight_ref[chip] = both

    def couple(s):
        rows = pl.ds(4 * s, 4)
        left = lower_ref[rows, :, :HALF].reshape(4 * PANEL, HALF)
        right = lower_ref[rows, :, HALF:].reshape(4 * PANEL, HALF)
        for k in range(B // WINDOW):
            columns = slice(WINDOW * k, WINDOW * (k + 1))
            total = dot(right, weight_ref[HALF_CHIPS:, :, columns].reshape(HALF, WINDOW))
            if k < HALF // WINDOW:
                total = total + dot(
                    left, weight_ref[:HALF_CHIPS, :, columns].reshape(HALF, WINDOW))
            coupled_ref[rows, :, columns] = total.astype(BF16).reshape(4, PANEL, WINDOW)

    def couple_near():
        ring.both_ways(lambda ours, others: others.wait_recv())

        @pl.loop(1, 4)
        def _(i):
            couple((y + i) % 4)

    ring.run(couple_near)
    couple(y % 4)

    def ring_sent():
        ring.both_ways(lambda ours, others: ours.wait_send())
        ring.finish()

    end_copy.wait_recv()
    end_b = end_buf[...].astype(BF16)
    broken = flag_ref[p] == 1
    early = p < SPLIT

    def down(src, dst, send, receive, target):
        return pltpu.make_async_remote_copy(
            src_ref=src, dst_ref=dst, send_sem=send, recv_sem=receive,
            device_id=(target, r), device_id_type=MESH)

    below = jnp.maximum(p - 1, 0)
    hops = [
        down(next_out.at[0], next_buf.at[0], next_sem.at[0, 0], next_sem.at[0, 1], below),
        None,
        down(next_out.at[1], next_buf.at[2], next_sem.at[2, 0], next_sem.at[2, 1], below),
    ]
    jumps = [
        down(next_out.at[0], next_buf.at[1], ahead_sem.at[q], next_sem.at[1, 1], q)
        for q in range(SPLIT)
    ]
    through_copy = down(
        through_out, through_in, through_hop.at[0], through_hop.at[1], below)

    def sum_halves(k, source, right_ref):
        copy = to_sibling(part_out.at[k], part_in.at[k], part_sem.at[k])
        part_out[k] = dot(source, right_ref[:, :, theirs].reshape(HALF, HALF))
        copy.start()
        own = dot(source, right_ref[:, :, mine].reshape(HALF, HALF))
        copy.wait_recv()
        return own + part_in[k]

    def pack_copy(k, j):
        return pltpu.make_async_remote_copy(
            src_ref=pack.at[k, j], dst_ref=recv.at[k, place], send_sem=pack_sem.at[k, 0],
            recv_sem=pack_sem.at[k, 1], device_id=peer(j), device_id_type=MESH)

    def messages(k, act):
        def count(n):
            return pltpu.make_async_remote_copy(
                src_ref=pack.at[k, :n], dst_ref=recv.at[k, :n], send_sem=pack_sem.at[k, 0],
                recv_sem=pack_sem.at[k, 1], device_id=sibling, device_id_type=MESH)

        @pl.when(source_core)
        def _():
            act(count(HALF_CHIPS - 1))

        @pl.when(jnp.logical_not(source_core))
        def _():
            act(count(HALF_CHIPS))

    def emit(which, value, out_ref, act):
        copy = to_sibling(
            rows_out.at[which, their_rows], out_ref.at[:, mine], rows_sem.at[which])
        if act == "start":
            rows_out[which] = value
            copy.start()
            out_ref[:, mine] = rows_out[which, my_rows]
        else:
            copy.wait()

    def step(k, source, right_ref, meanwhile):
        product = sum_halves(k, source, right_ref)
        for j in range(HALF_CHIPS):
            pack[k, j] = message(product, j)

        for j in range(HALF_CHIPS):
            @pl.when(jnp.logical_not(is_self(j)))
            def _():
                pack_copy(k, j).start()

        @pl.when(source_core)
        def _():
            recv[k, place] = pack[k, place]

        base = meanwhile(product)
        messages(k, lambda copy: copy.wait_recv())
        first = recv[k, :, :16].reshape(HALF_CHIPS * 16, 128).T
        second = recv[k, :, 16:].reshape(HALF_CHIPS * 16, 128).T

        def update(columns):
            def rows(i):
                return right_ref[:, 16 * i:16 * i + 16, columns].reshape(HALF_CHIPS * 16, HALF)
            total = dot(first[:48], rows(0)) + dot(first[64:112], rows(1))
            total = total + dot(second[:48], rows(2))
            return total if base is None else total + base(columns)

        copy = to_sibling(part2_out.at[k], part2_in.at[k], part2_sem.at[k])
        part2_out[k] = update(theirs)
        copy.start()
        sigma = update(mine)
        copy.wait_recv()
        return sigma + part2_in[k]

    through_ring = PlainRing(
        through_ref, (ring_send, through_recv), p, y, x, core, place, source_core)
    through_half = to_sibling(through_out, through_out, through_sem.at[0])
    through_here = to_sibling(through_out, through_ref.at[place, :, mine], through_sem.at[1])
    zero = jnp.zeros((PANEL, HALF), BF16)

    @pl.when(p == SPLIT - 1)
    def _():
        @pl.when(source_core)
        def _():
            next_out[1] = jnp.where(broken, zero, coupled_ref[place, :, theirs])
            half_copy = to_sibling(next_out.at[1], through_out, through_sem.at[0])
            half_copy.start()
            through_out[...] = jnp.where(broken, zero, coupled_ref[place, :, mine])
            half_copy.wait_send()

        @pl.when(jnp.logical_not(source_core))
        def _():
            through_half.wait_recv()

        through_copy.start()

        @pl.loop(0, HALF_CHIPS)
        def _(j):
            rows = coupled_ref[j]
            through_ref[j] = jnp.where(broken, jnp.zeros_like(rows), rows)

    @pl.when(p < SPLIT - 1)
    def _():
        through_copy.wait_recv()
        rows = sum_halves(2, through_in[...], coupled_ref).astype(BF16)
        through_out[...] = jnp.where(broken, zero, rows)

        @pl.when(p > 0)
        def _():
            through_copy.start()

        @pl.when(source_core)
        def _():
            through_ref[place, :, mine] = through_out[...]

        @pl.when(jnp.logical_not(source_core))
        def _():
            through_here.start()

    def gather_through():
        ring_sent()

        @pl.when(source_core)
        def _():
            to_sibling(through_out, through_ref.at[place, :, theirs], through_sem.at[1]).wait_recv()

        through_ring.run(lambda: None)

    @pl.when(p < SPLIT - 2)
    def _():
        gather_through()

    has_above = jnp.logical_and(p != parts - 1, p != SPLIT - 1)

    @pl.when(has_above)
    def _():
        hops[0].wait_recv()

    @pl.when(jnp.logical_not(has_above))
    def _():
        next_buf[0] = zero

    use_end = jnp.logical_or(broken, p == parts - 1)

    def settle(product):
        @pl.when(p < SPLIT - 1)
        def _():
            through_ring.finish()

        @pl.when(p == SPLIT - 1)
        def _():
            ring_sent()

    def gram(product):
        window = jnp.minimum(chip * PANEL // 128, (B - WINDOW) // 128) * 128
        chips = pl.ds(core * HALF_CHIPS, HALF_CHIPS)
        own = weight_ref[chips, :, pl.ds(pl.multiple_of(window, 128), WINDOW)]
        own = own.reshape(HALF, WINDOW).T
        for k in range(B // WINDOW):
            columns = slice(WINDOW * k, WINDOW * (k + 1))
            gram_buf[:, columns] = dot(own, weight_ref[chips, :, columns].reshape(HALF, WINDOW))
        gram_rows = pl.ds(pl.multiple_of(chip * PANEL - window, 16), PANEL)

        @pl.when(jnp.logical_not(early))
        def _():
            emit(0, -product, cross_ref, "start")

        return lambda columns: gram_buf[gram_rows, columns]

    sigma = step(0, jnp.where(use_end, end_b, next_buf[0]), coupled_ref, gram)
    next_out[0] = sigma.astype(BF16)
    sends_down = jnp.logical_and(p > 0, p != SPLIT)

    @pl.when(sends_down)
    def _():
        hops[0].start()

    @pl.when(p == SPLIT)
    def _():
        for q in (1, 0, 2, 3):
            jumps[q].start()

    @pl.when(jnp.logical_not(early))
    def _():
        emit(1, sigma, sigma_ref, "start")

    @pl.when(early)
    def _():
        first_sigma[...] = sigma

        @pl.when(p == SPLIT - 2)
        def _():
            gather_through()

        jumps[0].wait_recv()
        whole = first_sigma[...] + step(1, next_buf[1], through_ref, settle)
        next_out[1] = whole.astype(BF16)

        @pl.when(p > 0)
        def _():
            hops[2].start()

        emit(1, whole, sigma_ref, "start")

        @pl.when(p < SPLIT - 1)
        def _():
            hops[2].wait_recv()

        @pl.when(p == SPLIT - 1)
        def _():
            next_buf[2] = next_buf[1]

        source = jnp.where(broken, end_b, next_buf[2])
        for k in range(2):
            columns = slice(HALF * k, HALF * (k + 1))
            cross_part[:, columns] = -dot(
                source, coupled_ref[:, :, columns].reshape(HALF, HALF))
        cross_copy = to_sibling(cross_part.at[their_rows], cross_in, rows_sem.at[0])
        cross_copy.start()
        cross_copy.wait_recv()
        cross_ref[...] = cross_part[my_rows] + cross_in[...]

    end_copy.wait_send()

    @pl.when(jnp.logical_not(source_core))
    def _():
        here_copy.wait_send()

    def sent(k):
        to_sibling(part_out.at[k], part_in.at[k], part_sem.at[k]).wait_send()

    def step_sent(k):
        sent(k)
        to_sibling(part2_out.at[k], part2_in.at[k], part2_sem.at[k]).wait_send()
        messages(k, lambda copy: copy.wait_send())

    step_sent(0)

    @pl.when(sends_down)
    def _():
        hops[0].wait_send()

    @pl.when(p == SPLIT)
    def _():
        for jump in jumps:
            jump.wait_send()

    @pl.when(early)
    def _():
        step_sent(1)
        to_sibling(cross_part.at[their_rows], cross_in, rows_sem.at[0]).wait_send()

        @pl.when(p > 0)
        def _():
            through_copy.wait_send()
            hops[2].wait_send()

    @pl.when(p < SPLIT - 1)
    def _():
        sent(2)

        @pl.when(jnp.logical_not(source_core))
        def _():
            through_here.wait_send()

    @pl.when(jnp.logical_not(early))
    def _():
        ring_sent()
        emit(0, None, cross_ref, "wait")

    emit(1, None, sigma_ref, "wait")


def run_chain(flag, weight, lower, end):
    vmem = pl.BlockSpec(memory_space=pltpu.VMEM)
    dma = pltpu.SemaphoreType.DMA
    return pl.pallas_call(
        chain,
        out_shape=[jax.ShapeDtypeStruct((OWN, B), F32)] * 2,
        in_specs=[pl.BlockSpec(memory_space=pltpu.SMEM)] + [pl.BlockSpec(memory_space=pl.ANY)] * 3,
        out_specs=[vmem, vmem],
        scratch_shapes=[
            pltpu.VMEM((OWN, B), BF16),
            pltpu.VMEM((OWN, B), BF16),
            pltpu.VMEM((OWN, B), F32),
            pltpu.VMEM((CHIPS, PANEL, B), BF16),
            pltpu.VMEM((HALF_CHIPS, PANEL, B), BF16),
            pltpu.VMEM((HALF_CHIPS, PANEL, B), BF16),
            pltpu.VMEM((HALF_CHIPS, PANEL, B), BF16),
            pltpu.VMEM((PANEL, HALF), BF16),
            pltpu.VMEM((PANEL, HALF), BF16),
            pltpu.VMEM((PANEL, HALF), F32),
            pltpu.VMEM((PANEL, B), F32),
            pltpu.VMEM((OWN, B), F32),
            pltpu.VMEM((2, OWN, B), F32),
            pltpu.VMEM((2, OWN, B), F32),
            pltpu.VMEM((WINDOW, B), F32),
            pltpu.VMEM((PANEL, HALF), F32),
            pltpu.VMEM((3, PANEL, HALF), BF16),
            pltpu.VMEM((2, PANEL, HALF), BF16),
            pltpu.VMEM((3, PANEL, HALF), F32),
            pltpu.VMEM((3, PANEL, HALF), F32),
            pltpu.VMEM((2, PANEL, HALF), F32),
            pltpu.VMEM((2, PANEL, HALF), F32),
            pltpu.VMEM((2, HALF_CHIPS, 32, 128), BF16),
            pltpu.VMEM((2, HALF_CHIPS, 32, 128), BF16),
            pltpu.VMEM((2, PANEL, HALF), F32),
            dma((3,)), dma((2,)), dma((75,)), dma((HALF_CHIPS, 3)), dma((2,)),
            dma((HALF_CHIPS, 2)), dma((2, 2)), dma((2,)), dma((SPLIT,)),
            dma((2,)), dma((3, 2)), dma((3, 2)), dma((2, 2)), dma((2, 2)), dma((2, 2)),
        ],
        compiler_params=pltpu.CompilerParams(
            collective_id=0, has_side_effects=True, vmem_limit_bytes=40 * 1024 * 1024),
    )(flag, weight, lower, end)


def shards(w_inv, lower_block, sigma_end, chain_break):
    sigma, cross = run_chain(chain_break, w_inv[0], lower_block[0], sigma_end)
    return (sigma[None], cross[None])


def solution(mesh):
    in_specs = (P("tm", "rows", None), P("tm", "rows", None), P("rows", None), P())
    out_specs = (P("tm", "rows", None), P("tm", "rows", None))
    return jax.shard_map(shards, mesh=mesh, in_specs=in_specs, out_specs=out_specs, check_vma=False)
```
